32 devices in a mesh: batch: 8 (over z, x), mod: 4 (over y, core).
Axes of the slice: x: 2, y: 2, z: 4, core: 2. Of those that a mesh axis runs over, the one named last changes fastest.
Arguments:
- text: bfloat16 [32, 256, 2048], P(('batch', 'mod')), may hold values from -6 to 6
- patches: bfloat16 [32, 256, 1664], P(('batch', 'mod')), may hold values from -6 to 6
- text_lengths: int32 [32], P('batch'), may hold values from 1 to 256, as said below
- patch_mask: int32 [32, 256], P('batch'), may hold values from 0 to 1, as said below
- cotangent: bfloat16 [32, 256, 2048], P(('batch', 'mod')), may hold values from -6 to 6
- gains: bfloat16 [3, 2048], P(None, ('batch', 'mod')), may hold values from 0.5 to 1.5
- w_qkv: bfloat16 [3, 2048, 2048], P(None, 'batch', 'mod'), may hold values from -0.125 to 0.125
- w_so: bfloat16 [2048, 2048], P('mod', 'batch'), may hold values from -1 to 1
- w_cq: bfloat16 [2048, 2048], P('batch', 'mod'), may hold values from -0.125 to 0.125
- w_ckv: bfloat16 [2, 2048, 2048], P(None, 'batch', 'mod'), may hold values from -0.125 to 0.125
- w_co: bfloat16 [2048, 2048], P('mod', 'batch'), may hold values from -1 to 1
- w_patch: bfloat16 [1664, 2048], P(('batch', 'mod')), may hold values from -0.15625 to 0.15625
- w_gu: bfloat16 [2, 2048, 5120], P(None, 'batch', 'mod'), may hold values from -0.125 to 0.125
- w_down: bfloat16 [5120, 2048], P('mod', 'batch'), may hold values from -0.078125 to 0.078125
Outputs:
- result: float32 [32, 256, 2048], P(('batch', 'mod'))
- d_text: float32 [32, 256, 2048], P(('batch', 'mod'))
- d_gains: float32 [3, 2048], P(None, ('batch', 'mod'))
- d_qkv: float32 [3, 2048, 2048], P(None, 'batch', 'mod')
- d_so: float32 [2048, 2048], P('mod', 'batch')
- d_cq: float32 [2048, 2048], P('batch', 'mod')
- d_ckv: float32 [2, 2048, 2048], P(None, 'batch', 'mod')
- d_co: float32 [2048, 2048], P('mod', 'batch')
- d_patch: float32 [1664, 2048], P(('batch', 'mod'))
- d_gu: float32 [2, 2048, 5120], P(None, 'batch', 'mod')
- d_down: float32 [5120, 2048], P('mod', 'batch')
The draws below stay inside these ranges and needn't reach their ends.
Inputs may be any that keep to these rules, and one draw needn't show every extreme that they name: text_lengths[b] counts the valid text slots of item b, which come first; in every draw some item has all 256. `patch_mask`: 1 marks a patch that text may attend to; patch 0 of every item is 1.
All inputs are finite; a program needn't handle non-finite values.
Results may differ from the reference program's by a relative error of at most 0.024.
Values may be sent and summed in bfloat16 or wider, within the bound.
A program may use at most 320 MiB of HBM per device.

```python
import jax
import jax.numpy as jnp
from jax import lax

D = 2048
HD = 128
FF = 5120
PW = 1664
TEXT = 256
PATCH = 256
ITEMS = 32


def draw_text_lengths(key, part):
    key = jax.random.fold_in(key, 11)
    first_key, second_key, pick_key = jax.random.split(key, 3)
    first_draw = jax.random.randint(first_key, (ITEMS,), 1, TEXT + 1)
    second_draw = jax.random.randint(second_key, (ITEMS,), 1, TEXT + 1)
    lengths = jnp.minimum(first_draw, second_draw)
    chosen = jax.random.randint(pick_key, (), 0, ITEMS)
    return jnp.where(jnp.arange(ITEMS) == chosen, TEXT, lengths).astype(jnp.int32)


def draw_patch_mask(key, part):
    key = jax.random.fold_in(key, 23)
    levels = jax.random.randint(key, (ITEMS, PATCH), 0, 8)
    kept_mask = (levels < 7).astype(jnp.int32)
    return kept_mask.at[:, 0].set(1)


def spiked(values, rng, source, target, blocks, factor):
    def block_of(axis_at):
        return (jnp.arange(values.shape[axis_at]) // (values.shape[axis_at] // blocks)).reshape((-1,) + (1,) * (values.ndim - 1 - axis_at))

    first = jax.random.permutation(rng, blocks)[block_of(target)]
    other_side = (block_of(target) + blocks // 2) % blocks
    return jnp.where((block_of(source) == first) | (block_of(source) == other_side), factor * values, values)


def level_of(own_key, dims, cuts, least, largest):
    factor_of = 1.0
    for axis_at, shards_of in cuts:
        steps = jax.random.uniform(jax.random.fold_in(jax.random.fold_in(own_key, 6), axis_at), (shards_of,), jnp.float32, least / len(cuts), largest / len(cuts))
        factor_of = factor_of * jnp.repeat(jnp.exp(steps), dims[axis_at] // shards_of).reshape((-1,) + (1,) * (len(dims) - 1 - axis_at))
    return factor_of


def scatter_about(rng, dims, scale, reach, cuts=(), dtype=jnp.bfloat16):
    values = jax.random.normal(rng, dims, jnp.float32) * scale
    if len(cuts) > 0:
        values = level_of(rng, dims, cuts, -0.22, 0.18) * values
    return jnp.clip(values, min=-reach, max=reach).astype(dtype)


def heavy_noise(own_key, dims, deviation, reach, cuts, heavy, held_as=jnp.bfloat16):
    values = deviation * jax.random.normal(own_key, dims, jnp.float32)
    if cuts:
        values = values * level_of(own_key, dims, cuts, -0.22, 0.18)
    return jnp.clip(spiked(values, jax.random.fold_in(own_key, 3), *heavy), -reach, reach).astype(held_as)


def setup_inputs(seed: int = 0) -> dict:
    key_of = jax.random.split(jax.random.key(seed), 15)
    return {
        "text": scatter_about(key_of[0], (ITEMS, TEXT, D), 1.0, 6.0, ((0, 32),)),
        "patches": scatter_about(key_of[1], (ITEMS, PATCH, PW), 1.0, 6.0, ((0, 32),)),
        "text_lengths": draw_text_lengths(jax.random.fold_in(key_of[14], 71), 0),
        "patch_mask": draw_patch_mask(jax.random.fold_in(key_of[14], 71), 0),
        "cotangent": heavy_noise(key_of[4], (ITEMS, TEXT, D), 1.0, 6.0, ((0, 32),), (0, 2, 32, 2.75)),
        "gains": jnp.clip(1.0 + 0.1 * jax.random.normal(key_of[5], (3, D), jnp.float32), 0.5, 1.5).astype(jnp.bfloat16),
        "w_qkv": scatter_about(key_of[6], (3, D, D), D ** -0.5, 0.125, ((1, 8), (2, 4))),
        "w_so": scatter_about(key_of[7], (D, D), (D // 64) ** -0.5, 1.0, ((0, 4), (1, 8))),
        "w_cq": scatter_about(key_of[8], (D, D), D ** -0.5, 0.125, ((0, 8), (1, 4))),
        "w_ckv": scatter_about(key_of[9], (2, D, D), D ** -0.5, 0.125, ((1, 8), (2, 4))),
        "w_co": scatter_about(key_of[10], (D, D), (D // 64) ** -0.5, 1.0, ((0, 4), (1, 8))),
        "w_patch": scatter_about(key_of[11], (PW, D), PW ** -0.5, 0.15625, ((0, 32),)),
        "w_gu": scatter_about(key_of[12], (2, D, FF), D ** -0.5, 0.125, ((1, 8), (2, 4))),
        "w_down": scatter_about(key_of[13], (FF, D), FF ** -0.5, 0.078125, ((0, 4), (1, 8))),
    }


@jax.custom_vjp
def low(v):
    return lax.optimization_barrier(v.astype(jnp.bfloat16)).astype(jnp.float32)

@jax.custom_vjp
def low_back(v):
    return v

def low_keep(v):
    return (low(v), None)

def low_pass(kept, grad):
    return (grad,)

def back_keep(v):
    return (v, None)

def back_low(kept, grad):
    return (low(grad),)
low.defvjp(low_keep, low_pass)
low_back.defvjp(back_keep, back_low)
highest = lax.Precision.HIGHEST

def matmul(left, right):
    return jnp.tensordot(left, right, axes=1, precision=highest)

def rms_norm(values, gain):
    factor = lax.rsqrt(lax.optimization_barrier(jnp.mean(values * values, axis=-1, keepdims=True)) + 1e-06)
    return values * factor * gain

def attend(query, keys, values, allowed):
    item_count, query_rows, columns = query.shape
    head_count = columns // HD
    query_heads = query.reshape(item_count, query_rows, head_count, HD)
    key_heads = keys.reshape(item_count, keys.shape[1], head_count, HD)
    value_heads = values.reshape(item_count, keys.shape[1], head_count, HD)
    scores = jnp.einsum('bqhe,bkhe->bhqk', query_heads, key_heads, precision=highest) * HD ** (-0.5)
    scores = low_back(jnp.where(allowed[:, None], scores, -1e+30))
    probs = low(jax.nn.softmax(scores, axis=-1))
    context = jnp.einsum('bhqk,bkhe->bqhe', probs, value_heads, precision=highest)
    return context.reshape(item_count, query_rows, columns)

def forward(params, text_x, patch_x, lengths, mask_rows):
    gains, w_qkv, w_so, w_cq, w_ckv, w_co, w_patch, w_gu, w_down = params
    positions = jnp.arange(text_x.shape[1])
    causal = (positions[None, None, :] <= positions[None, :, None]) & (positions[None, None, :] < lengths[:, None, None])
    cross_ok = (mask_rows > 0)[:, None, :]
    act_one = low(rms_norm(text_x, gains[0]))
    query = low(low_back(matmul(act_one, w_qkv[0])))
    keys = low(low_back(matmul(act_one, w_qkv[1])))
    values = low(low_back(matmul(act_one, w_qkv[2])))
    context = low(low_back(attend(query, keys, values, causal)))
    x_one = text_x + low_back(matmul(context, w_so))
    act_two = low(rms_norm(x_one, gains[1]))
    cross_query = low(low_back(matmul(act_two, w_cq)))
    projected = low(low_back(matmul(patch_x, w_patch)))
    cross_keys = low(low_back(matmul(projected, w_ckv[0])))
    cross_values = low(low_back(matmul(projected, w_ckv[1])))
    cross_context = low(low_back(attend(cross_query, cross_keys, cross_values, cross_ok)))
    x_two = x_one + low_back(matmul(cross_context, w_co))
    act_three = low(rms_norm(x_two, gains[2]))
    gate = low_back(matmul(act_three, w_gu[0]))
    upward = low_back(matmul(act_three, w_gu[1]))
    hidden = low(jax.nn.gelu(gate, approximate=True) * upward)
    return x_two + low_back(matmul(hidden, w_down))

def reference(text, patches, text_lengths, patch_mask, cotangent, gains, w_qkv, w_so, w_cq, w_ckv, w_co, w_patch, w_gu, w_down):
    params = tuple((weight.astype(jnp.float32) for weight in (gains, w_qkv, w_so, w_cq, w_ckv, w_co, w_patch, w_gu, w_down)))
    group_size = 8
    group_count = text.shape[0] // group_size

    def by_group(array):
        return array.reshape((group_count, group_size) + array.shape[1:])

    def one_group(grad_total, pieces):
        text_g, patch_g, length_g, mask_g, cot_g = pieces
        text_f = text_g.astype(jnp.float32)
        patch_f = patch_g.astype(jnp.float32)

        def layer(weights_in, text_in):
            return forward(weights_in, text_in, patch_f, length_g, mask_g)
        output, pullback = jax.vjp(layer, params, text_f)
        positions = jnp.arange(text_g.shape[1])
        valid = (positions[None, :] < length_g[:, None]).astype(jnp.float32)
        grad_params, grad_text = pullback(cot_g.astype(jnp.float32) * valid[..., None])
        grad_total = jax.tree.map(jnp.add, grad_total, grad_params)
        return (grad_total, (output, grad_text))
    zeroes = tuple((jnp.zeros(weight.shape, jnp.float32) for weight in params))
    grad_total, (outputs, grad_texts) = lax.scan(one_group, zeroes, (by_group(text), by_group(patches), by_group(text_lengths), by_group(patch_mask), by_group(cotangent)))
    result = outputs.reshape((-1,) + outputs.shape[2:])
    d_text = grad_texts.reshape((-1,) + grad_texts.shape[2:])
    return (result, d_text, grad_total[0], grad_total[1], grad_total[2], grad_total[3], grad_total[4], grad_total[5], grad_total[6], grad_total[7], grad_total[8])
```

```python
import jax
import jax.numpy as jnp
from jax import lax
from jax.sharding import PartitionSpec as P

HD = 128
F32 = jnp.float32
BF = jnp.bfloat16


def rms_norm(values, gain):
    factor = lax.rsqrt(jnp.mean(values * values, axis=-1, keepdims=True) + 1e-06)
    return values * factor * gain


def norm_back(values, gain, grad_in):
    _, pullback = jax.vjp(rms_norm, values, gain)
    return pullback(grad_in)


def gelu_mix(gate, upward):
    return jax.nn.gelu(gate, approximate=True) * upward


def tie(value, deps):
    if not deps:
        return value
    return lax.optimization_barrier((value, tuple(deps)))[0]


def dot(spec, a, b):
    return jnp.einsum(spec, a, b, preferred_element_type=F32)


class Batch:
    def __init__(self, size):
        self.size = size
        self.n_out = size // 2
        here = lax.axis_index("batch")
        self.outer, self.inner = here // 2, here % 2
        self.last_z = []
        self.last_x = []

    def source(self, position):
        s, j = position // 2, position % 2
        return (self.outer - s + self.n_out) % self.n_out * 2 + (self.inner + j) % 2

    def shifts(self):
        n = self.n_out
        order = []
        for d in range(1, n // 2 + 1):
            order.append(d)
            if n - d != d:
                order.append(n - d)
        return order

    def along_z(self, value, s):
        n = self.n_out
        pairs = [(o * 2 + i, (o + s) % n * 2 + i) for o in range(n) for i in range(2)]
        return lax.ppermute(value, "batch", pairs)

    def along_x(self, value):
        return lax.ppermute(value, "batch", [(b, b ^ 1) for b in range(self.size)])

    def reorder(self, value, axis):
        width = value.shape[axis] // self.size
        return jnp.concatenate(
            [
                lax.dynamic_slice_in_dim(value, self.source(p) * width, width, axis)
                for p in range(self.size)
            ],
            axis=axis,
        )

    def fetch(self, shard, deps=()):
        shard = tie(shard, deps)
        z = {0: shard}
        for s in self.shifts():
            z[s] = self.along_z(shard, s)
        out = []
        for s in range(self.n_out):
            out += [z[s], self.along_x(z[s])]
        return out

    def reduce(self, blocks_x, blocks_own, deps=()):
        got = self.along_x(tie(blocks_x.astype(BF), deps))
        total = blocks_own.astype(F32) + got.astype(F32)
        send = total.astype(BF)
        result = total[0]
        for s in self.shifts():
            result = result + self.along_z(send[s], self.n_out - s).astype(F32)
        return result


def scores_of(query, keys, allowed):
    item_count, query_rows, columns = query.shape
    head_count = columns // HD
    query_heads = query.reshape(item_count, query_rows, head_count, HD)
    key_heads = keys.reshape(item_count, keys.shape[1], head_count, HD)
    raw_scores = dot("bqhe,bkhe->bhqk", query_heads, key_heads) * HD ** (-0.5)
    return jnp.where(allowed[:, None], raw_scores, -1e30)


def attend_forward(query, keys, values, allowed):
    item_count, query_rows, columns = query.shape
    head_count = columns // HD
    scores = scores_of(query, keys, allowed)
    row_max = jnp.max(scores, axis=-1, keepdims=True)
    weights = jnp.exp(scores - row_max)
    row_total = jnp.sum(weights, axis=-1, keepdims=True)
    probs = (weights / row_total).astype(BF)
    value_heads = values.reshape(item_count, values.shape[1], head_count, HD)
    context = dot("bhqk,bkhe->bqhe", probs, value_heads)
    return (
        context.reshape(item_count, query_rows, columns).astype(BF),
        row_max + jnp.log(row_total),
    )


def attend_backward(query, keys, values, allowed, log_total, grad_context):
    item_count, query_rows, columns = query.shape
    key_rows = keys.shape[1]
    head_count = columns // HD
    scale = HD ** (-0.5)
    probs = jnp.exp(scores_of(query, keys, allowed) - log_total)
    grad_heads = grad_context.reshape(item_count, query_rows, head_count, HD)
    query_heads = query.reshape(item_count, query_rows, head_count, HD)
    key_heads = keys.reshape(item_count, key_rows, head_count, HD)
    value_heads = values.reshape(item_count, key_rows, head_count, HD)
    grad_values = dot("bhqk,bqhe->bkhe", probs.astype(BF), grad_heads)
    grad_probs = dot("bqhe,bkhe->bhqk", grad_heads, value_heads)
    grad_scores = probs * (grad_probs - jnp.sum(probs * grad_probs, axis=-1, keepdims=True))
    grad_scores = grad_scores.astype(BF)
    grad_query = dot("bhqk,bkhe->bqhe", grad_scores, key_heads) * scale
    grad_keys = dot("bhqk,bqhe->bkhe", grad_scores, query_heads) * scale
    return (
        grad_query.reshape(item_count, query_rows, columns).astype(BF),
        grad_keys.reshape(item_count, key_rows, columns).astype(BF),
        grad_values.reshape(item_count, key_rows, columns).astype(BF),
    )


def mod_gather(value, axis=0):
    return lax.all_gather(value, "mod", axis=axis, tiled=True)


def mod_sum(partial):
    return lax.psum_scatter(partial.astype(BF), "mod", scatter_dimension=0, tiled=True).astype(F32)


def local(n_batch, n_mod, text, patches, text_lengths, patch_mask, cotangent, gains,
          w_qkv, w_so, w_cq, w_ckv, w_co, w_patch, w_gu, w_down):
    own_items, text_rows, width = text.shape
    heads_w = w_qkv.shape[2]
    mod = lax.axis_index("mod")
    ex = Batch(n_batch)
    nb, no = n_batch, n_batch // 2
    own_lengths = lax.dynamic_slice_in_dim(text_lengths, mod * own_items, own_items)
    positions = jnp.arange(text_rows)
    causal = (positions[None, None, :] <= positions[None, :, None]) & (
        positions[None, None, :] < text_lengths[:, None, None]
    )
    cross_allowed = (patch_mask > 0)[:, None, :]

    text_all = mod_gather(ex.reorder(text, 2))
    gain_parts = ex.fetch(gains)
    qkv_parts = ex.fetch(w_qkv)
    gain_cols = mod_gather(jnp.stack(gain_parts)[None], 0)
    gain_all = jnp.transpose(gain_cols, (2, 1, 0, 3)).reshape(3, width).astype(F32)
    x_zero = ex.reorder(text, 2).astype(F32)
    patch_all = mod_gather(patches)
    col_w = width // n_mod
    patch_rows = mod_gather(w_patch)
    patch_own = lax.dynamic_slice_in_dim(patch_rows, mod * col_w, col_w, 1)

    so_parts = ex.fetch(w_so.T, [qkv_parts[-1]])
    patch_parts = ex.fetch(patch_own, [qkv_parts[-1]])
    act_one = rms_norm(text_all.astype(F32), gain_all[0]).astype(BF)
    self_qkv = jnp.concatenate(qkv_parts, axis=1)
    qkv = dot("gtd,jdc->jgtc", act_one, self_qkv).astype(BF)
    self_ctx, self_log = attend_forward(qkv[0], qkv[1], qkv[2], causal)
    self_out = jnp.concatenate(so_parts, axis=0)
    x_one = x_zero + mod_sum(dot("gtc,dc->gtd", self_ctx, self_out))

    pr = w_patch.shape[0] * n_mod
    proj_w = jnp.zeros((pr * nb, col_w), BF)
    for p in range(nb):
        proj_w = lax.dynamic_update_slice_in_dim(proj_w, patch_parts[p], ex.source(p) * pr, 0)
    proj_cols = dot("gpe,ec->gpc", patch_all, proj_w).astype(BF)
    proj_all = ex.reorder(mod_gather(proj_cols, 2), 2)
    ckv_parts = ex.fetch(w_ckv, [so_parts[-1], patch_parts[-1]])
    cq_parts = ex.fetch(w_cq, [so_parts[-1], patch_parts[-1]])
    co_parts = ex.fetch(w_co.T, [ckv_parts[-1], cq_parts[-1]])
    gate_parts = ex.fetch(w_gu[0], [ckv_parts[-1], cq_parts[-1]])
    up_parts = ex.fetch(w_gu[1], [gate_parts[-1]])
    down_parts = ex.fetch(w_down.T, [up_parts[-1]])

    cross_query_w = jnp.concatenate(cq_parts, axis=0)
    cross_kv_w = jnp.concatenate(ckv_parts, axis=1)
    cross_out_w = jnp.concatenate(co_parts, axis=0)
    cross_kv = dot("gpd,jdc->jgpc", proj_all, cross_kv_w).astype(BF)
    act_two = mod_gather(rms_norm(x_one, gain_all[1]).astype(BF))
    cross_query = dot("gtd,dc->gtc", act_two, cross_query_w).astype(BF)
    cross_ctx, cross_log = attend_forward(cross_query, cross_kv[0], cross_kv[1], cross_allowed)
    x_two = x_one + mod_sum(dot("gtc,dc->gtd", cross_ctx, cross_out_w))

    act_three = mod_gather(rms_norm(x_two, gain_all[2]).astype(BF))
    gate_w = jnp.concatenate(gate_parts, axis=0)
    up_w = jnp.concatenate(up_parts, axis=0)
    gate = dot("gtd,df->gtf", act_three, gate_w)
    upward = dot("gtd,df->gtf", act_three, up_w)
    hidden = gelu_mix(gate, upward).astype(BF)

    valid = (positions[None, :] < own_lengths[:, None]).astype(F32)
    grad_result = ex.reorder(cotangent, 2).astype(F32) * valid[..., None]
    grad_branch = mod_gather(grad_result.astype(BF))

    def own_and_x(acts, grads, spec):
        a = acts.reshape(acts.shape[:2] + (no, 2, width // nb))
        return dot(spec, a[:, :, :, 1], grads).astype(BF), dot(spec, a[:, :, :, 0], grads)

    def reduced(acts, grads, spec="gtsd,gtc->sdc", deps=()):
        theirs, mine = own_and_x(acts, grads, spec)
        return ex.reduce(theirs, mine, deps)

    grad_down = reduced(grad_branch, hidden)
    down_w = jnp.concatenate(down_parts, axis=0)
    result = x_two + mod_sum(dot("gtf,df->gtd", hidden, down_w))
    grad_hidden = dot("gtd,df->gtf", grad_branch, down_w)
    _, mix_pull = jax.vjp(gelu_mix, gate, upward)
    grad_gate, grad_upward = mix_pull(grad_hidden)
    grad_gate = grad_gate.astype(BF)
    grad_upward = grad_upward.astype(BF)
    grad_act = mod_sum(dot("gtf,df->gtd", grad_gate, gate_w) + dot("gtf,df->gtd", grad_upward, up_w))
    grad_gate_w = reduced(act_three, grad_gate)
    grad_up_w = reduced(act_three, grad_upward)
    grad_inner, gain_grad_three = norm_back(x_two, gain_all[2], grad_act)
    grad_two = grad_result + grad_inner

    grad_branch = mod_gather(grad_two.astype(BF))
    grad_co_w = reduced(grad_branch, cross_ctx)
    grad_ctx = dot("gtd,dc->gtc", grad_branch, cross_out_w).astype(BF)
    grad_cq_act, grad_ck_act, grad_cv_act = attend_backward(
        cross_query, cross_kv[0], cross_kv[1], cross_allowed, cross_log, grad_ctx
    )
    grad_act = mod_sum(dot("gtc,dc->gtd", grad_cq_act, cross_query_w))
    grad_kv_act = jnp.stack([grad_ck_act, grad_cv_act])
    grad_proj_part = dot("jgpc,jdc->gpd", grad_kv_act, cross_kv_w).astype(BF)
    grad_proj_part = ex.reorder(grad_proj_part, 2)
    grad_proj = lax.psum_scatter(
        jnp.stack(jnp.split(grad_proj_part, n_mod, axis=2)), "mod", scatter_dimension=0, tiled=True
    )[0]
    grad_cq_w = reduced(act_two, grad_cq_act)
    grad_ckv_w = jnp.stack([reduced(proj_all, grad_ck_act), reduced(proj_all, grad_cv_act)])
    grad_inner, gain_grad_two = norm_back(x_one, gain_all[1], grad_act)
    grad_one = grad_two + grad_inner

    grad_branch = mod_gather(grad_one.astype(BF))
    grad_so_w = reduced(grad_branch, self_ctx)
    grad_ctx = dot("gtd,dc->gtc", grad_branch, self_out).astype(BF)
    grad_patch_all = dot("gpe,gpc->ec", patch_all, grad_proj).astype(BF)
    by_source = [lax.dynamic_slice_in_dim(grad_patch_all, ex.source(p) * pr, pr, 0) for p in range(nb)]
    grad_patch_cols = ex.reduce(jnp.stack(by_source[1::2]), jnp.stack(by_source[0::2]))
    grad_patch_w = lax.all_to_all(
        grad_patch_cols.reshape(n_mod, pr // n_mod, col_w), "mod", 0, 0, tiled=True
    )
    grad_patch_w = jnp.transpose(grad_patch_w, (1, 0, 2)).reshape(pr // n_mod, width)

    grad_q_act, grad_k_act, grad_v_act = attend_backward(
        qkv[0], qkv[1], qkv[2], causal, self_log, grad_ctx
    )
    grad_qkv_act = jnp.stack([grad_q_act, grad_k_act, grad_v_act])
    grad_act = mod_sum(dot("jgtc,jdc->gtd", grad_qkv_act, self_qkv))
    grad_qkv_w = jnp.stack([reduced(act_one, g) for g in (grad_q_act, grad_k_act, grad_v_act)])
    grad_inner, gain_grad_one = norm_back(x_zero, gain_all[0], grad_act)
    grad_zero = grad_one + grad_inner

    gain_grads = jnp.stack([gain_grad_one, gain_grad_two, gain_grad_three])
    gg = gain_grads.reshape(3, no, 2, width // nb)
    got = ex.along_x(gg[:, :, 1])
    gg = gg[:, :, 0] + got
    gsum = gg[:, 0]
    for s in ex.shifts():
        gsum = gsum + ex.along_z(gg[:, s], no - s)
    gsum = jnp.sum(mod_gather(gsum[None], 0), axis=0)
    gw = width // (nb * n_mod)
    gain_out = lax.dynamic_slice_in_dim(gsum, mod * gw, gw, 1)
    return (
        ex.reorder(result, 2),
        ex.reorder(grad_zero, 2),
        gain_out,
        grad_qkv_w,
        grad_so_w.T,
        grad_cq_w,
        grad_ckv_w,
        grad_co_w.T,
        grad_patch_w,
        jnp.stack([grad_gate_w, grad_up_w]),
        grad_down.T,
    )


def solution(mesh):
    placed = (
        P(("batch", "mod"), None, None),
        P(("batch", "mod"), None, None),
        P("batch"),
        P("batch", None),
        P(("batch", "mod"), None, None),
        P(None, ("batch", "mod")),
        P(None, "batch", "mod"),
        P("mod", "batch"),
        P("batch", "mod"),
        P(None, "batch", "mod"),
        P("mod", "batch"),
        P(("batch", "mod"), None),
        P(None, "batch", "mod"),
        P("mod", "batch"),
    )

    def run(*args):
        return local(mesh.shape["batch"], mesh.shape["mod"], *args)

    return jax.shard_map(
        run,
        mesh=mesh,
        in_specs=placed,
        out_specs=(
            P(("batch", "mod"), None, None),
            P(("batch", "mod"), None, None),
            P(None, ("batch", "mod")),
            P(None, "batch", "mod"),
            P("mod", "batch"),
            P("batch", "mod"),
            P(None, "batch", "mod"),
            P("mod", "batch"),
            P(("batch", "mod"), None),
            P(None, "batch", "mod"),
            P("mod", "batch"),
        ),
        check_vma=False,
    )
```

```python
import functools

import jax
import jax.numpy as jnp
from jax import lax
from jax.experimental import pallas as pl
from jax.experimental.pallas import tpu as pltpu
from jax.sharding import PartitionSpec as P

HD = 128
F32 = jnp.float32
BF = jnp.bfloat16


def rms_norm(values, gain):
    factor = lax.rsqrt(jnp.mean(values * values, axis=-1, keepdims=True) + 1e-06)
    return values * factor * gain


def norm_back(values, gain, grad_in):
    _, pullback = jax.vjp(rms_norm, values, gain)
    return pullback(grad_in)


def gelu_mix(gate, upward):
    return jax.nn.gelu(gate, approximate=True) * upward


def tie(value, deps):
    if not deps:
        return value
    return lax.optimization_barrier((value, tuple(deps)))[0]


def dot(spec, a, b):
    return jnp.einsum(spec, a, b, preferred_element_type=F32)


class Batch:
    def __init__(self, size):
        self.size = size
        self.n_out = size // 2
        here = lax.axis_index("batch")
        self.outer, self.inner = here // 2, here % 2
        self.last_z = []
        self.last_x = []

    def source(self, position):
        s, j = position // 2, position % 2
        return (self.outer - s + self.n_out) % self.n_out * 2 + (self.inner + j) % 2

    def shifts(self):
        n = self.n_out
        order = []
        for d in range(1, n // 2 + 1):
            order.append(d)
            if n - d != d:
                order.append(n - d)
        return order

    def along_z(self, value, s):
        n = self.n_out
        pairs = [(o * 2 + i, (o + s) % n * 2 + i) for o in range(n) for i in range(2)]
        return lax.ppermute(value, "batch", pairs)

    def along_x(self, value):
        return lax.ppermute(value, "batch", [(b, b ^ 1) for b in range(self.size)])

    def reorder(self, value, axis):
        width = value.shape[axis] // self.size
        return jnp.concatenate(
            [
                lax.dynamic_slice_in_dim(value, self.source(p) * width, width, axis)
                for p in range(self.size)
            ],
            axis=axis,
        )

    def fetch(self, shard, deps=()):
        shard = tie(shard, deps)
        z = {0: shard}
        for s in self.shifts():
            z[s] = self.along_z(shard, s)
        out = []
        for s in range(self.n_out):
            out += [z[s], self.along_x(z[s])]
        return out

    def reduce(self, blocks_x, blocks_own, deps=()):
        got = self.along_x(tie(blocks_x.astype(BF), deps))
        total = blocks_own.astype(F32) + got.astype(F32)
        send = total.astype(BF)
        result = total[0]
        for s in self.shifts():
            result = result + self.along_z(send[s], self.n_out - s).astype(F32)
        return result


MESH = pl.DeviceIdType.MESH


class Place:
    def __init__(self, n_batch):
        self.n_batch = n_batch
        self.n_out = n_batch // 2
        self.b = lax.axis_index("batch")
        self.m = lax.axis_index("mod")
        self.outer = self.b // 2
        self.inner = self.b % 2
        self.core = self.m + 1 - 2 * (self.m % 2)
        self.far = (self.m + 2) % 4
        self.farcore = (self.core + 2) % 4
        self.x_peer = self.b + 1 - 2 * self.inner
        self.shifts = []
        for d in range(1, self.n_out // 2 + 1):
            self.shifts += [d] if 2 * d == self.n_out else [d, self.n_out - d]

    def z_peer(self, s):
        return (self.outer + s) % self.n_out * 2 + self.inner

    def z_from(self, s):
        return (self.outer - s + self.n_out) % self.n_out * 2 + self.inner

    def greet(self):
        barrier = pltpu.get_barrier_semaphore()
        ids = [{"batch": self.z_peer(s), "mod": self.m} for s in self.shifts]
        ids.append({"batch": self.x_peer, "mod": self.m})
        for j in (self.core, self.far, self.farcore):
            ids.append({"batch": self.b, "mod": j})
        for device in ids:
            pl.semaphore_signal(barrier, inc=1, device_id=device, device_id_type=MESH)
        pl.semaphore_wait(barrier, len(ids))


def remote(src, dst, send, recv, **device):
    return pltpu.make_async_remote_copy(
        src_ref=src, dst_ref=dst, send_sem=send, recv_sem=recv, device_id=device, device_id_type=MESH
    )


class BatchGather:
    def __init__(self, place, tensors, sems):
        self.p = place
        self.tensors = tensors
        self.z_send, self.z_recv, self.x_send, self.x_recv, self.own = sems
        self.started = 0
        self.events = [(t, s) for t in range(len(tensors)) for s in [0] + place.shifts]
        self.at = 0

    @staticmethod
    def semaphores(n_out, count):
        dma = pltpu.SemaphoreType.DMA
        return [dma((count, n_out)) for _ in range(4)] + [dma((count,))]

    def z_copy(self, t, s):
        src, block = self.tensors[t]
        return remote(src, block(self.p.b), self.z_send.at[t, s], self.z_recv.at[t, s],
                      batch=self.p.z_peer(s), mod=self.p.m)

    def own_copy(self, t):
        src, block = self.tensors[t]
        return pltpu.make_async_copy(src, block(self.p.b), self.own.at[t])

    def x_copy(self, t, s):
        src, block = self.tensors[t]
        where = block(self.p.z_from(s))
        return remote(src if s == 0 else where, where, self.x_send.at[t, s], self.x_recv.at[t, s],
                      batch=self.p.x_peer, mod=self.p.m)

    def start(self, count=1):
        for t in range(self.started, min(self.started + count, len(self.tensors))):
            for s in self.p.shifts:
                self.z_copy(t, s).start()
            self.own_copy(t).start()
            self.started = t + 1

    def pump(self, upto):
        while self.at < len(self.events) and self.events[self.at][0] <= upto:
            t, s = self.events[self.at]
            if s:
                self.z_copy(t, s).wait_recv()
                if s == self.p.shifts[-1]:
                    self.start()
            self.x_copy(t, s).start()
            self.at += 1

    def arrived(self, t, ahead=1):
        self.pump(t + ahead)
        self.own_copy(t).wait()
        for s in [0] + self.p.shifts:
            self.x_copy(t, s).wait_recv()

    def sent(self):
        for t in range(len(self.tensors)):
            for s in self.p.shifts:
                self.z_copy(t, s).wait_send()
            for s in [0] + self.p.shifts:
                self.x_copy(t, s).wait_send()


class ModGather:
    def __init__(self, place, block, send, recv):
        self.p = place
        self.block = block
        mine = block(place.m)
        far = block(place.far)
        self.near = remote(mine, mine, send.at[0], recv.at[0], batch=place.b, mod=place.core)
        self.across = remote(mine, mine, send.at[1], recv.at[1], batch=place.b, mod=place.far)
        self.on = remote(far, far, send.at[2], recv.at[2], batch=place.b, mod=place.core)

    def start(self):
        self.across.start()
        self.near.start()

    def forward(self):
        self.across.wait_recv()
        self.on.start()

    def finish(self):
        self.near.wait_recv()
        self.on.wait_recv()
        self.near.wait_send()
        self.across.wait_send()
        self.on.wait_send()


def first_kernel(n_batch, text, patches, gain_tile, patch_tile, w_qkv, w_so, w_co, w_down,
                 text_all, patch_all, gain_all, patch_rows, qkv_all, so_t, co_t, down_t,
                 gain_mod, gain_sum, z_send, z_recv, x_send, x_recv, own, mod_send, mod_recv, misc):
    p = Place(n_batch)
    rows = w_qkv.shape[1]
    tensors = [
        (w_qkv.at[0], lambda q: qkv_all.at[0, pl.ds(q * rows, rows)]),
        (w_qkv.at[1], lambda q: qkv_all.at[1, pl.ds(q * rows, rows)]),
        (gain_sum, lambda q: gain_all.at[q]),
        (w_qkv.at[2], lambda q: qkv_all.at[2, pl.ds(q * rows, rows)]),
    ]
    g = BatchGather(p, tensors, (z_send, z_recv, x_send, x_recv, own))
    copies = [
        pltpu.make_async_copy(text, text_all.at[p.m], misc.at[0]),
        pltpu.make_async_copy(patches, patch_all.at[p.m], misc.at[1]),
        pltpu.make_async_copy(gain_tile, gain_mod.at[p.m], misc.at[2]),
        pltpu.make_async_copy(patch_tile.at[p.m], patch_rows.at[p.m], misc.at[3]),
    ]
    for c in copies:
        c.start()
    p.greet()
    gains = [
        remote(gain_tile, gain_mod.at[p.m], mod_send.at[2, k], mod_recv.at[2, k], batch=p.b, mod=j)
        for k, j in enumerate((p.core, p.far, p.farcore))
    ]
    for c in gains:
        c.start()
    g.start()
    for c in copies:
        c.wait()
    text_g = ModGather(p, lambda j: text_all.at[j], mod_send.at[0], mod_recv.at[0])
    patch_g = ModGather(p, lambda j: patch_all.at[j], mod_send.at[1], mod_recv.at[1])
    text_g.start()
    rows_c = [
        remote(patch_tile.at[j], patch_rows.at[p.m], mod_send.at[3, k], mod_recv.at[3, k], batch=p.b, mod=j)
        for k, j in enumerate((p.core, p.far, p.farcore))
    ]
    for c in rows_c:
        c.start()
    patch_g.start()
    for c in gains:
        c.wait_recv()
    gain_sum[...] = gain_mod[0] + gain_mod[1] + gain_mod[2] + gain_mod[3]
    so_t[...] = w_so[...].T
    co_t[...] = w_co[...].T
    down_t[...] = w_down[...].T
    g.pump(0)
    text_g.forward()
    g.pump(1)
    patch_g.forward()
    for t in range(4):
        g.arrived(t)
    text_g.finish()
    patch_g.finish()
    for c in gains:
        c.wait_send()
    for c in rows_c:
        c.wait_recv()
        c.wait_send()
    g.sent()


def first_call(n_batch, text, patches, gain_tile, patch_tile, w_qkv, w_so, w_co, w_down):
    n_out = n_batch // 2
    dma = pltpu.SemaphoreType.DMA
    j, rows, columns = w_qkv.shape
    return pl.pallas_call(
        functools.partial(first_kernel, n_batch),
        out_shape=[
            jax.ShapeDtypeStruct((4,) + text.shape, BF),
            jax.ShapeDtypeStruct((4,) + patches.shape, BF),
            jax.ShapeDtypeStruct((n_batch,) + gain_tile.shape, BF),
            jax.ShapeDtypeStruct(patch_tile.shape, BF),
            jax.ShapeDtypeStruct((j, rows * n_batch, columns), BF),
        ]
        + [jax.ShapeDtypeStruct(w.shape[::-1], BF) for w in (w_so, w_co, w_down)],
        in_specs=[pl.BlockSpec(memory_space=pltpu.VMEM)] * 8,
        out_specs=[pl.BlockSpec(memory_space=pl.ANY)] * 5 + [pl.BlockSpec(memory_space=pltpu.VMEM)] * 3,
        scratch_shapes=[
            pltpu.VMEM((4,) + gain_tile.shape, BF),
            pltpu.VMEM(gain_tile.shape, BF),
        ]
        + BatchGather.semaphores(n_out, 4)
        + [dma((4, 3)), dma((4, 3)), dma((4,))],
        compiler_params=pltpu.CompilerParams(collective_id=0, has_side_effects=True),
        cost_estimate=pl.CostEstimate(flops=10**6, bytes_accessed=300 * 10**6, transcendentals=0),
    )(text, patches, gain_tile, patch_tile, w_qkv, w_so, w_co, w_down)


def mm(a, b):
    return lax.dot_general(a, b, (((1,), (0,)), ((), ())), preferred_element_type=F32)


def mm_nt(a, b):
    return lax.dot_general(a, b, (((1,), (1,)), ((), ())), preferred_element_type=F32)


def mm_tn(a, b):
    return lax.dot_general(a, b, (((0,), (0,)), ((), ())), preferred_element_type=F32)


class Local:
    def __init__(self, sems):
        self.sems = sems
        self.used = 0

    def go(self, src, dst):
        copy = pltpu.make_async_copy(src, dst, self.sems.at[self.used])
        self.used += 1
        copy.start()
        return copy


STEP = 32


def each_rows(rows, body, step=STEP):
    def one(r, carry):
        body(pl.ds(pl.multiple_of(r * step, step), step))
        return carry

    lax.fori_loop(0, rows // step, one, 0)


def each(count, body, first=0):
    def one(k, carry):
        body(k)
        return carry

    lax.fori_loop(first, count, one, 0)


def cols(n, width):
    return pl.ds(pl.multiple_of(n * width, width), width)


def rms_of(values, gain):
    return values * lax.rsqrt(jnp.mean(values * values, axis=-1, keepdims=True) + 1e-06) * gain


def attend(q_ref, k_ref, v_ref, out_ref, lse_ref, j, allowed, heads):
    for h in range(heads):
        at = pl.ds(h * HD, HD)
        s = mm_nt(q_ref[j, :, at], k_ref[j, :, at]) * HD ** (-0.5)
        s = jnp.where(allowed, s, -1e30)
        top = jnp.max(s, axis=-1, keepdims=True)
        e = jnp.exp(s - top)
        total = jnp.sum(e, axis=-1, keepdims=True)
        probs = (e / total).astype(BF)
        out_ref[j, :, at] = mm(probs, v_ref[j, :, at]).astype(BF)
        lse_ref[j, :, pl.ds(h, 1)] = top + jnp.log(total)


def causal_ok(key_row, rows):
    shape = (rows, key_row.shape[1])
    return (lax.broadcasted_iota(jnp.int32, shape, 1) <= lax.broadcasted_iota(jnp.int32, shape, 0)) & (
        jnp.broadcast_to(key_row, shape) > 0.5
    )


class BranchSum:
    def __init__(self, place, bufs, send, recv):
        self.p = place
        self.fs, self.cf, self.ys, self.yr, self.ns, self.cn = bufs
        self.to_core = remote(self.fs, self.cf, send.at[0], recv.at[0], batch=place.b, mod=place.core)
        self.to_far = remote(self.ys, self.yr, send.at[1], recv.at[1], batch=place.b, mod=place.far)
        self.to_near = remote(self.ns, self.cn, send.at[2], recv.at[2], batch=place.b, mod=place.core)

    def send(self, part, width, step=512):
        p = self.p
        n = width // step

        def first(k):
            self.fs[:, cols(k, step)] = part(p.farcore, cols(k, step)).astype(BF)

        def second(k):
            self.ns[:, cols(k, step)] = part(p.core, cols(k, step)).astype(BF)

        def third(k):
            at = cols(k, step)
            self.ys[:, at] = (part(p.far, at) + self.cf[:, at].astype(F32)).astype(BF)

        each(n, first)
        self.to_core.start()
        each(n, second)
        self.to_near.start()
        self.to_core.wait_recv()
        each(n, third)
        self.to_far.start()

    def receive(self):
        self.to_near.wait_recv()
        self.to_far.wait_recv()

    def others(self, rows):
        return self.cn[rows, :].astype(F32) + self.yr[rows, :].astype(F32)

    def sent(self):
        self.to_core.wait_send()
        self.to_near.wait_send()
        self.to_far.wait_send()


def halves(shard, whole, rows):
    half = rows // 2

    def piece(k):
        return (shard.at[pl.ds(k * half, half)], lambda q: whole.at[pl.ds(q * rows + k * half, half)])

    return [piece(0), piece(1)]


def forward_kernel(n_batch, *refs):
    (text_all, patch_all, gains, patch_own, key_ok, cross_ok, qkv_w,
     w_so, w_ckv, w_cq, w_co, w_gu, w_down) = refs[:13]
    (so_all, patch_w, ckv_all, cq_all, co_all, gu_all, down_all, act1_o, act2_o, act3_o, qkv_o, cqkv_o,
     ctx_o, cctx_o, lse_o, clse_o, pp_o, x1_o, x2_o, gate_o, up_o, h_o) = refs[13:35]
    (act, x, wq, wo, wp, pat, pp, qkv, ctx, lse, fs, cf, ys, yr, ns, cn, wg, gate, up, hid,
     z_send, z_recv, x_send, x_recv, own, mod_send, mod_recv, sum_send, sum_recv, loc) = refs[35:]
    p = Place(n_batch)
    local = Local(loc)
    rows, width = x.shape
    heads = wq.shape[2] // HD
    cq_r, pr = w_cq.shape[0], patch_own.shape[0]
    g = BatchGather(
        p,
        [
            (w_so, lambda q: so_all.at[pl.ds(q * cq_r, cq_r)]),
            (patch_own, lambda q: patch_w.at[pl.ds(q * pr, pr)]),
            (w_ckv.at[0], lambda q: ckv_all.at[0, pl.ds(q * cq_r, cq_r)]),
            (w_ckv.at[1], lambda q: ckv_all.at[1, pl.ds(q * cq_r, cq_r)]),
            (w_cq, lambda q: cq_all.at[pl.ds(q * cq_r, cq_r)]),
            (w_co, lambda q: co_all.at[pl.ds(q * cq_r, cq_r)]),
        ]
        + halves(w_gu.at[0], gu_all.at[0], cq_r)
        + halves(w_gu.at[1], gu_all.at[1], cq_r)
        + halves(w_down, down_all, cq_r),
        (z_send, z_recv, x_send, x_recv, own),
    )
    SO, PATCH, CK, CV, CQ, CO, GATE, GATE2, UP, UP2, DOWN, DOWN2 = range(12)
    load_act = local.go(text_all, act)
    load_q = local.go(qkv_w, wq)
    load_pat = local.go(patch_all, pat)
    p.greet()
    g.start()
    bufs = (fs, cf, ys, yr, ns, cn)
    one = BranchSum(p, bufs, sum_send.at[0], sum_recv.at[0])
    two = BranchSum(p, bufs, sum_send.at[1], sum_recv.at[1])
    act_block = lambda j: act.at[j]
    col_w = wq.shape[2]
    pp_g = ModGather(p, lambda j: pp.at[:, :, pl.ds(pl.multiple_of(j * col_w, col_w), col_w)], mod_send.at[0], mod_recv.at[0])
    a2_g = ModGather(p, act_block, mod_send.at[1], mod_recv.at[1])
    a3_g = ModGather(p, act_block, mod_send.at[2], mod_recv.at[2])

    load_act.wait()
    x[...] = act[p.m].astype(F32)

    def norm_one(j):
        def body(r):
            act[j, r, :] = rms_of(act[j, r, :].astype(F32), gains[pl.ds(0, 1), :]).astype(BF)

        each_rows(rows, body)

    each(4, norm_one)
    save_act = local.go(act, act1_o)
    load_q.wait()

    def project(j):
        for w in range(3):
            qkv[w, j] = mm(act[j], wq[w]).astype(BF)

    each(4, project)
    save_qkv = local.go(qkv, qkv_o)
    g.pump(SO)
    attend_one = lambda j: attend(qkv.at[0], qkv.at[1], qkv.at[2], ctx, lse, j, causal_ok(key_ok[j, pl.ds(0, 1), :], rows), heads)
    each(4, attend_one)
    save_ctx = local.go(ctx, ctx_o)
    save_lse = local.go(lse, lse_o)
    g.arrived(SO)
    load_o = local.go(so_all, wo)
    save_act.wait()
    save_qkv.wait()
    load_o.wait()
    part = lambda j, at: mm_nt(ctx[j], wo[at, :])
    one.send(part, width)

    def add_own(k):
        at = cols(k, 512)
        x[:, at] += part(p.m, at)

    each(width // 512, add_own)
    g.arrived(PATCH)
    load_p = local.go(patch_w, wp)
    load_p.wait()
    load_pat.wait()
    own_cols = pl.ds(pl.multiple_of(p.m * col_w, col_w), col_w)

    def project_patch(j):
        pp[j, :, own_cols] = mm(pat[j], wp[...]).astype(BF)

    each(4, project_patch)
    pp_g.start()
    one.receive()

    def finish_one(r):
        x[r, :] += one.others(r)
        act[p.m, r, :] = rms_of(x[r, :], gains[pl.ds(1, 1), :]).astype(BF)

    each_rows(rows, finish_one)
    a2_g.start()
    save_x = local.go(x, x1_o)
    one.sent()
    g.pump(CV)
    pp_g.forward()
    g.pump(CQ)
    a2_g.forward()
    g.arrived(CK)
    load_ck = local.go(ckv_all.at[0], wq.at[1])
    pp_g.finish()
    save_pp = local.go(pp, pp_o)
    load_ck.wait()

    def project_pp(w):
        def body(j):
            qkv[w, j] = mm(pp[j], wq[w]).astype(BF)

        return body

    each(4, project_pp(1))
    g.arrived(CV)
    load_cv = local.go(ckv_all.at[1], wq.at[2])
    load_cv.wait()
    each(4, project_pp(2))
    g.arrived(CQ)
    load_cq = local.go(cq_all, wq.at[0])
    a2_g.finish()
    save_act = local.go(act, act2_o)
    load_cq.wait()

    def project_cq(j):
        qkv[0, j] = mm(act[j], wq[0]).astype(BF)

    each(4, project_cq)
    save_ctx.wait()
    save_lse.wait()
    save_qkv = local.go(qkv, cqkv_o)

    def attend_two(j):
        ok = jnp.broadcast_to(cross_ok[j, pl.ds(0, 1), :], (rows, cross_ok.shape[2])) > 0.5
        attend(qkv.at[0], qkv.at[1], qkv.at[2], ctx, lse, j, ok, heads)

    each(4, attend_two)
    save_ctx = local.go(ctx, cctx_o)
    save_lse = local.go(lse, clse_o)
    g.arrived(CO)
    load_o = local.go(co_all, wo)
    save_act.wait()
    save_x.wait()
    load_o.wait()
    two.send(part, width)
    each(width // 512, add_own)
    g.pump(GATE2)
    two.receive()

    def finish_two(r):
        x[r, :] += two.others(r)
        act[p.m, r, :] = rms_of(x[r, :], gains[pl.ds(2, 1), :]).astype(BF)

    each_rows(rows, finish_two)
    a3_g.start()
    save_x = local.go(x, x2_o)
    two.sent()
    g.pump(UP)
    a3_g.forward()
    a3_g.finish()
    save_act = local.go(act, act3_o)

    g.arrived(GATE)
    g.arrived(GATE2)
    load_g = local.go(gu_all.at[0], wg)
    load_g.wait()

    def gate_one(j):
        gate[j] = mm(act[j], wg[...])

    each(4, gate_one)
    save_gate = local.go(gate, gate_o)
    g.arrived(UP)
    g.arrived(UP2)
    load_g = local.go(gu_all.at[1], wg)
    load_g.wait()

    def up_one(j):
        u = mm(act[j], wg[...])
        up[j] = u.astype(BF)
        hid[j] = (jax.nn.gelu(gate[j], approximate=True) * u).astype(BF)

    each(4, up_one)
    save_up = local.go(up, up_o)
    save_h = local.go(hid, h_o)
    g.arrived(DOWN)
    g.arrived(DOWN2)
    g.sent()
    for c in (save_act, save_x, save_gate, save_up, save_h, save_ctx, save_lse, save_qkv, save_pp):
        c.wait()


def forward_call(n_batch, text_all, patch_all, gains, patch_own, key_ok, cross_ok, qkv_w,
                 w_so, w_ckv, w_cq, w_co, w_gu, w_down):
    n_out = n_batch // 2
    dma = pltpu.SemaphoreType.DMA
    items, rows, width = text_all.shape
    c, f = qkv_w.shape[2], w_gu.shape[2]
    patch_width = patch_all.shape[2]
    keys = patch_all.shape[1]
    sds = jax.ShapeDtypeStruct
    any_ = pl.BlockSpec(memory_space=pl.ANY)
    vmem = pl.BlockSpec(memory_space=pltpu.VMEM)
    big = (items, rows, width)
    return pl.pallas_call(
        functools.partial(forward_kernel, n_batch),
        out_shape=[
            sds((width, c), BF), sds((patch_width, c), BF), sds((2, width, c), BF), sds((width, c), BF),
            sds((width, c), BF), sds((2, width, f), BF), sds((width, f), BF),
            sds(big, BF), sds(big, BF), sds(big, BF),
            sds((3, items, rows, c), BF), sds((3, items, rows, c), BF),
            sds((items, rows, c), BF), sds((items, rows, c), BF),
            sds((items, rows, 128), F32), sds((items, rows, 128), F32),
            sds((items, keys, width), BF), sds((rows, width), F32), sds((rows, width), F32),
            sds((items, rows, f), F32), sds((items, rows, f), BF), sds((items, rows, f), BF),
        ],
        in_specs=[any_, any_, vmem, vmem, vmem, vmem, any_] + [vmem] * 6,
        out_specs=[any_] * 22,
        scratch_shapes=[
            pltpu.VMEM(big, BF), pltpu.VMEM((rows, width), F32), pltpu.VMEM((3, width, c), BF),
            pltpu.VMEM((width, c), BF), pltpu.VMEM((patch_width, c), BF), pltpu.VMEM((items, keys, patch_width), BF),
            pltpu.VMEM((items, keys, width), BF), pltpu.VMEM((3, items, rows, c), BF), pltpu.VMEM((items, rows, c), BF),
            pltpu.VMEM((items, rows, 128), F32),
        ]
        + [pltpu.VMEM((rows, width), BF)] * 6
        + [pltpu.VMEM((width, f), BF), pltpu.VMEM((items, rows, f), F32), pltpu.VMEM((items, rows, f), BF), pltpu.VMEM((items, rows, f), BF)]
        + BatchGather.semaphores(n_out, 12)
        + [dma((3, 3)), dma((3, 3)), dma((2, 3)), dma((2, 3)), dma((32,))],
        compiler_params=pltpu.CompilerParams(collective_id=1, has_side_effects=True, vmem_limit_bytes=60 * 2**20),
        cost_estimate=pl.CostEstimate(flops=35 * 10**9, bytes_accessed=600 * 10**6, transcendentals=0),
    )(text_all, patch_all, gains, patch_own, key_ok, cross_ok, qkv_w, w_so, w_ckv, w_cq, w_co, w_gu, w_down)


def scores_of(query, keys, allowed):
    item_count, query_rows, columns = query.shape
    head_count = columns // HD
    query_heads = query.reshape(item_count, query_rows, head_count, HD)
    key_heads = keys.reshape(item_count, keys.shape[1], head_count, HD)
    raw_scores = dot("bqhe,bkhe->bhqk", query_heads, key_heads) * HD ** (-0.5)
    return jnp.where(allowed[:, None], raw_scores, -1e30)


def attend_forward(query, keys, values, allowed):
    item_count, query_rows, columns = query.shape
    head_count = columns // HD
    scores = scores_of(query, keys, allowed)
    row_max = jnp.max(scores, axis=-1, keepdims=True)
    weights = jnp.exp(scores - row_max)
    row_total = jnp.sum(weights, axis=-1, keepdims=True)
    probs = (weights / row_total).astype(BF)
    value_heads = values.reshape(item_count, values.shape[1], head_count, HD)
    context = dot("bhqk,bkhe->bqhe", probs, value_heads)
    return (
        context.reshape(item_count, query_rows, columns).astype(BF),
        row_max + jnp.log(row_total),
    )


def attend_backward(query, keys, values, allowed, log_total, grad_context):
    item_count, query_rows, columns = query.shape
    key_rows = keys.shape[1]
    head_count = columns // HD
    scale = HD ** (-0.5)
    probs = jnp.exp(scores_of(query, keys, allowed) - log_total)
    grad_heads = grad_context.reshape(item_count, query_rows, head_count, HD)
    query_heads = query.reshape(item_count, query_rows, head_count, HD)
    key_heads = keys.reshape(item_count, key_rows, head_count, HD)
    value_heads = values.reshape(item_count, key_rows, head_count, HD)
    grad_values = dot("bhqk,bqhe->bkhe", probs.astype(BF), grad_heads)
    grad_probs = dot("bqhe,bkhe->bhqk", grad_heads, value_heads)
    grad_scores = probs * (grad_probs - jnp.sum(probs * grad_probs, axis=-1, keepdims=True))
    grad_scores = grad_scores.astype(BF)
    grad_query = dot("bhqk,bkhe->bqhe", grad_scores, key_heads) * scale
    grad_keys = dot("bhqk,bqhe->bkhe", grad_scores, query_heads) * scale
    return (
        grad_query.reshape(item_count, query_rows, columns).astype(BF),
        grad_keys.reshape(item_count, key_rows, columns).astype(BF),
        grad_values.reshape(item_count, key_rows, columns).astype(BF),
    )


def mod_gather(value, axis=0):
    return lax.all_gather(value, "mod", axis=axis, tiled=True)


def mod_sum(partial):
    return lax.psum_scatter(partial.astype(BF), "mod", scatter_dimension=0, tiled=True).astype(F32)


def local(n_batch, n_mod, text, patches, text_lengths, patch_mask, cotangent, gains,
          w_qkv, w_so, w_cq, w_ckv, w_co, w_patch, w_gu, w_down):
    own_items, text_rows, width = text.shape
    heads_w = w_qkv.shape[2]
    mod = lax.axis_index("mod")
    ex = Batch(n_batch)
    nb, no = n_batch, n_batch // 2
    own_lengths = lax.dynamic_slice_in_dim(text_lengths, mod * own_items, own_items)
    positions = jnp.arange(text_rows)
    causal = (positions[None, None, :] <= positions[None, :, None]) & (
        positions[None, None, :] < text_lengths[:, None, None]
    )
    cross_allowed = (patch_mask > 0)[:, None, :]

    gw = width // (nb * n_mod)
    gain_tile = lax.dynamic_update_slice(jnp.zeros((16, gw * n_mod), BF), gains, (0, mod * gw))
    col_w = width // n_mod
    pr = w_patch.shape[0]
    pr_pad = -(-pr // 16) * 16
    patch_tile = jnp.pad(w_patch, ((0, pr_pad - pr), (0, 0))).reshape(pr_pad, n_mod, col_w)
    patch_tile = jnp.transpose(patch_tile, (1, 0, 2))
    text_all, patch_all, gain_raw, patch_rows, self_qkv, so_t, co_t, down_t = first_call(
        n_batch, text[0], patches[0], gain_tile, patch_tile, w_qkv, w_so, w_co, w_down
    )
    gain_all = jnp.transpose(gain_raw[:, :3], (1, 0, 2)).reshape(3, width).astype(F32)
    patch_own = patch_rows[:, :pr].reshape(n_mod * pr, col_w)
    block, block_pad = n_mod * pr, -(-n_mod * pr // 16) * 16
    patch_in = patch_all
    if block_pad != block:
        patch_own = jnp.pad(patch_own, ((0, block_pad - block), (0, 0)))
        patch_in = jnp.pad(
            patch_all.reshape(patch_all.shape[:2] + (nb, block)), ((0, 0), (0, 0), (0, 0), (0, block_pad - block))
        ).reshape(patch_all.shape[:2] + (nb * block_pad,))
    row_ok = (positions[None, :] < text_lengths[:, None]).astype(F32)
    key_ok = jnp.broadcast_to(row_ok[:, None, :], (n_mod, 8, text_rows))
    cross_ok = jnp.broadcast_to((patch_mask > 0).astype(F32)[:, None, :], (n_mod, 8, patch_mask.shape[1]))
    gain_pad = jnp.pad(gain_all, ((0, 5), (0, 0)))
    (self_out, _, cross_kv_w, cross_query_w, cross_out_w, gu_w, down_w, act_one, act_two, act_three, qkv, cqkv,
     self_ctx, cross_ctx, self_lse, cross_lse, proj_all, x_one, x_two, gate, upward, hidden) = forward_call(
        n_batch, text_all, patch_in, gain_pad, patch_own, key_ok, cross_ok, self_qkv,
        so_t, w_ckv, w_cq, co_t, w_gu, down_t)
    gain_all = ex.reorder(gain_all, 1)
    x_zero = ex.reorder(text, 2).astype(F32)
    self_qkv = ex.reorder(self_qkv, 1)
    self_out = ex.reorder(self_out, 0)
    cross_kv_w = ex.reorder(cross_kv_w, 1)
    cross_query_w = ex.reorder(cross_query_w, 0)
    cross_out_w = ex.reorder(cross_out_w, 0)
    gate_w, up_w = ex.reorder(gu_w[0], 0), ex.reorder(gu_w[1], 0)
    down_w = ex.reorder(down_w, 0)
    act_one, act_two, act_three, proj_all = [ex.reorder(v, 2) for v in (act_one, act_two, act_three, proj_all)]
    x_one, x_two = ex.reorder(x_one[None], 2), ex.reorder(x_two[None], 2)
    upward = upward.astype(F32)
    cross_query, cross_kv = cqkv[0], cqkv[1:]
    self_log = jnp.transpose(self_lse[:, :, :heads_w // HD], (0, 2, 1))[..., None]
    cross_log = jnp.transpose(cross_lse[:, :, :heads_w // HD], (0, 2, 1))[..., None]

    pr = w_patch.shape[0] * n_mod
    valid = (positions[None, :] < own_lengths[:, None]).astype(F32)
    grad_result = ex.reorder(cotangent, 2).astype(F32) * valid[..., None]
    grad_branch = mod_gather(grad_result.astype(BF))

    def own_and_x(acts, grads, spec):
        a = acts.reshape(acts.shape[:2] + (no, 2, width // nb))
        return dot(spec, a[:, :, :, 1], grads).astype(BF), dot(spec, a[:, :, :, 0], grads)

    def reduced(acts, grads, spec="gtsd,gtc->sdc", deps=()):
        theirs, mine = own_and_x(acts, grads, spec)
        return ex.reduce(theirs, mine, deps)

    grad_down = reduced(grad_branch, hidden)
    result = x_two + mod_sum(dot("gtf,df->gtd", hidden, down_w))
    grad_hidden = dot("gtd,df->gtf", grad_branch, down_w)
    _, mix_pull = jax.vjp(gelu_mix, gate, upward)
    grad_gate, grad_upward = mix_pull(grad_hidden)
    grad_gate = grad_gate.astype(BF)
    grad_upward = grad_upward.astype(BF)
    grad_act = mod_sum(dot("gtf,df->gtd", grad_gate, gate_w) + dot("gtf,df->gtd", grad_upward, up_w))
    grad_gate_w = reduced(act_three, grad_gate)
    grad_up_w = reduced(act_three, grad_upward)
    grad_inner, gain_grad_three = norm_back(x_two, gain_all[2], grad_act)
    grad_two = grad_result + grad_inner

    grad_branch = mod_gather(grad_two.astype(BF))
    grad_co_w = reduced(grad_branch, cross_ctx)
    grad_ctx = dot("gtd,dc->gtc", grad_branch, cross_out_w).astype(BF)
    grad_cq_act, grad_ck_act, grad_cv_act = attend_backward(
        cross_query, cross_kv[0], cross_kv[1], cross_allowed, cross_log, grad_ctx
    )
    grad_act = mod_sum(dot("gtc,dc->gtd", grad_cq_act, cross_query_w))
    grad_kv_act = jnp.stack([grad_ck_act, grad_cv_act])
    grad_proj_part = dot("jgpc,jdc->gpd", grad_kv_act, cross_kv_w).astype(BF)
    grad_proj_part = ex.reorder(grad_proj_part, 2)
    grad_proj = lax.psum_scatter(
        jnp.stack(jnp.split(grad_proj_part, n_mod, axis=2)), "mod", scatter_dimension=0, tiled=True
    )[0]
    grad_cq_w = reduced(act_two, grad_cq_act)
    grad_ckv_w = jnp.stack([reduced(proj_all, grad_ck_act), reduced(proj_all, grad_cv_act)])
    grad_inner, gain_grad_two = norm_back(x_one, gain_all[1], grad_act)
    grad_one = grad_two + grad_inner

    grad_branch = mod_gather(grad_one.astype(BF))
    grad_so_w = reduced(grad_branch, self_ctx)
    grad_ctx = dot("gtd,dc->gtc", grad_branch, self_out).astype(BF)
    grad_patch_all = dot("gpe,gpc->ec", patch_all, grad_proj).astype(BF)
    by_source = [lax.dynamic_slice_in_dim(grad_patch_all, ex.source(p) * pr, pr, 0) for p in range(nb)]
    grad_patch_cols = ex.reduce(jnp.stack(by_source[1::2]), jnp.stack(by_source[0::2]))
    grad_patch_w = lax.all_to_all(
        grad_patch_cols.reshape(n_mod, pr // n_mod, col_w), "mod", 0, 0, tiled=True
    )
    grad_patch_w = jnp.transpose(grad_patch_w, (1, 0, 2)).reshape(pr // n_mod, width)

    grad_q_act, grad_k_act, grad_v_act = attend_backward(
        qkv[0], qkv[1], qkv[2], causal, self_log, grad_ctx
    )
    grad_qkv_act = jnp.stack([grad_q_act, grad_k_act, grad_v_act])
    grad_act = mod_sum(dot("jgtc,jdc->gtd", grad_qkv_act, self_qkv))
    grad_qkv_w = jnp.stack([reduced(act_one, g) for g in (grad_q_act, grad_k_act, grad_v_act)])
    grad_inner, gain_grad_one = norm_back(x_zero, gain_all[0], grad_act)
    grad_zero = grad_one + grad_inner

    gain_grads = jnp.stack([gain_grad_one, gain_grad_two, gain_grad_three])
    gg = gain_grads.reshape(3, no, 2, width // nb)
    got = ex.along_x(gg[:, :, 1])
    gg = gg[:, :, 0] + got
    gsum = gg[:, 0]
    for s in ex.shifts():
        gsum = gsum + ex.along_z(gg[:, s], no - s)
    gsum = jnp.sum(mod_gather(gsum[None], 0), axis=0)
    gain_out = lax.dynamic_slice_in_dim(gsum, mod * gw, gw, 1)
    return (
        ex.reorder(result, 2),
        ex.reorder(grad_zero, 2),
        gain_out,
        grad_qkv_w,
        grad_so_w.T,
        grad_cq_w,
        grad_ckv_w,
        grad_co_w.T,
        grad_patch_w,
        jnp.stack([grad_gate_w, grad_up_w]),
        grad_down.T,
    )


def solution(mesh):
    placed = (
        P(("batch", "mod"), None, None),
        P(("batch", "mod"), None, None),
        P("batch"),
        P("batch", None),
        P(("batch", "mod"), None, None),
        P(None, ("batch", "mod")),
        P(None, "batch", "mod"),
        P("mod", "batch"),
        P("batch", "mod"),
        P(None, "batch", "mod"),
        P("mod", "batch"),
        P(("batch", "mod"), None),
        P(None, "batch", "mod"),
        P("mod", "batch"),
    )

    def run(*args):
        return local(mesh.shape["batch"], mesh.shape["mod"], *args)

    return jax.shard_map(
        run,
        mesh=mesh,
        in_specs=placed,
        out_specs=(
            P(("batch", "mod"), None, None),
            P(("batch", "mod"), None, None),
            P(None, ("batch", "mod")),
            P(None, "batch", "mod"),
            P("mod", "batch"),
            P("batch", "mod"),
            P(None, "batch", "mod"),
            P("mod", "batch"),
            P(("batch", "mod"), None),
            P(None, "batch", "mod"),
            P("mod", "batch"),
        ),
        check_vma=False,
    )
```

```python
import functools

import jax
import jax.numpy as jnp
from jax import lax
from jax.experimental import pallas as pl
from jax.experimental.pallas import tpu as pltpu
from jax.sharding import PartitionSpec as P

HD = 128
F32 = jnp.float32
BF = jnp.bfloat16


VMEM_LIMIT = 62 * 2**20
MESH = pl.DeviceIdType.MESH


class Place:
    def __init__(self, n_batch):
        self.n_batch = n_batch
        self.n_out = n_batch // 2
        self.b = lax.axis_index("batch")
        self.m = lax.axis_index("mod")
        self.outer = self.b // 2
        self.inner = self.b % 2
        self.core = self.m + 1 - 2 * (self.m % 2)
        self.far = (self.m + 2) % 4
        self.farcore = (self.core + 2) % 4
        self.x_peer = self.b + 1 - 2 * self.inner
        self.shifts = []
        for d in range(1, self.n_out // 2 + 1):
            self.shifts += [d] if 2 * d == self.n_out else [d, self.n_out - d]

    def z_peer(self, s):
        return (self.outer + s) % self.n_out * 2 + self.inner

    def z_from(self, s):
        return (self.outer - s + self.n_out) % self.n_out * 2 + self.inner

    def greet(self):
        barrier = pltpu.get_barrier_semaphore()
        ids = [{"batch": self.z_peer(s), "mod": self.m} for s in self.shifts]
        ids.append({"batch": self.x_peer, "mod": self.m})
        for j in (self.core, self.far, self.farcore):
            ids.append({"batch": self.b, "mod": j})
        for device in ids:
            pl.semaphore_signal(barrier, inc=1, device_id=device, device_id_type=MESH)
        pl.semaphore_wait(barrier, len(ids))


def remote(src, dst, send, recv, **device):
    return pltpu.make_async_remote_copy(
        src_ref=src, dst_ref=dst, send_sem=send, recv_sem=recv, device_id=device, device_id_type=MESH
    )


class BatchGather:
    def __init__(self, place, tensors, sems):
        self.p = place
        self.tensors = tensors
        self.z_send, self.z_recv, self.x_send, self.x_recv, self.own = sems
        self.started = 0
        self.events = [(t, s) for t in range(len(tensors)) for s in [0] + place.shifts]
        self.at = 0

    @staticmethod
    def semaphores(n_out, count):
        dma = pltpu.SemaphoreType.DMA
        return [dma((count, n_out)) for _ in range(4)] + [dma((count,))]

    def z_copy(self, t, s):
        src, block = self.tensors[t]
        return remote(src, block(self.p.b), self.z_send.at[t, s], self.z_recv.at[t, s],
                      batch=self.p.z_peer(s), mod=self.p.m)

    def own_copy(self, t):
        src, block = self.tensors[t]
        return pltpu.make_async_copy(src, block(self.p.b), self.own.at[t])

    def x_copy(self, t, s):
        src, block = self.tensors[t]
        where = block(self.p.z_from(s))
        return remote(src if s == 0 else where, where, self.x_send.at[t, s], self.x_recv.at[t, s],
                      batch=self.p.x_peer, mod=self.p.m)

    def start(self, count=1):
        for t in range(self.started, min(self.started + count, len(self.tensors))):
            for s in self.p.shifts:
                self.z_copy(t, s).start()
            self.own_copy(t).start()
            self.started = t + 1

    def pump(self, upto):
        while self.at < len(self.events) and self.events[self.at][0] <= upto:
            t, s = self.events[self.at]
            if s:
                self.z_copy(t, s).wait_recv()
                if s == self.p.shifts[-1]:
                    self.start()
            self.x_copy(t, s).start()
            self.at += 1

    def arrived(self, t, ahead=1):
        self.pump(t + ahead)
        self.own_copy(t).wait()
        for s in [0] + self.p.shifts:
            self.x_copy(t, s).wait_recv()

    def sent(self):
        for t in range(len(self.tensors)):
            for s in self.p.shifts:
                self.z_copy(t, s).wait_send()
            for s in [0] + self.p.shifts:
                self.x_copy(t, s).wait_send()


class ModGather:
    def __init__(self, place, block, send, recv):
        self.p = place
        self.block = block
        mine = block(place.m)
        far = block(place.far)
        self.near = remote(mine, mine, send.at[0], recv.at[0], batch=place.b, mod=place.core)
        self.across = remote(mine, mine, send.at[1], recv.at[1], batch=place.b, mod=place.far)
        self.on = remote(far, far, send.at[2], recv.at[2], batch=place.b, mod=place.core)

    def start(self):
        self.across.start()
        self.near.start()

    def forward(self):
        self.across.wait_recv()
        self.on.start()

    def finish(self):
        self.near.wait_recv()
        self.on.wait_recv()
        self.near.wait_send()
        self.across.wait_send()
        self.on.wait_send()


def first_kernel(n_batch, text, patches, gain_tile, patch_tile, w_qkv, w_so, w_co, w_down, cot, valid,
                 text_all, patch_all, gain_all, patch_rows, qkv_all, dy_all, so_t, co_t, down_t,
                 dy, gain_mod, gain_sum, z_send, z_recv, x_send, x_recv, own, mod_send, mod_recv, misc):
    p = Place(n_batch)
    rows = w_qkv.shape[1]
    tensors = [
        (w_qkv.at[0], lambda q: qkv_all.at[0, pl.ds(q * rows, rows)]),
        (w_qkv.at[1], lambda q: qkv_all.at[1, pl.ds(q * rows, rows)]),
        (gain_sum, lambda q: gain_all.at[q]),
        (w_qkv.at[2], lambda q: qkv_all.at[2, pl.ds(q * rows, rows)]),
    ]
    g = BatchGather(p, tensors, (z_send, z_recv, x_send, x_recv, own))
    copies = [
        pltpu.make_async_copy(text, text_all.at[p.m], misc.at[0]),
        pltpu.make_async_copy(patches, patch_all.at[p.m], misc.at[1]),
        pltpu.make_async_copy(gain_tile, gain_mod.at[p.m], misc.at[2]),
        pltpu.make_async_copy(patch_tile.at[p.m], patch_rows.at[p.m], misc.at[3]),
        pltpu.make_async_copy(dy, dy_all.at[p.m], misc.at[4]),
    ]

    def mask_rows(r):
        dy[r, :] = (cot[r, :].astype(F32) * valid[r, pl.ds(0, 1)]).astype(BF)

    each_rows(dy.shape[0], mask_rows)
    for c in copies:
        c.start()
    p.greet()
    gains = [
        remote(gain_tile, gain_mod.at[p.m], mod_send.at[2, k], mod_recv.at[2, k], batch=p.b, mod=j)
        for k, j in enumerate((p.core, p.far, p.farcore))
    ]
    for c in gains:
        c.start()
    g.start()
    for c in copies:
        c.wait()
    text_g = ModGather(p, lambda j: text_all.at[j], mod_send.at[0], mod_recv.at[0])
    patch_g = ModGather(p, lambda j: patch_all.at[j], mod_send.at[1], mod_recv.at[1])
    dy_g = ModGather(p, lambda j: dy_all.at[j], mod_send.at[4], mod_recv.at[4])
    text_g.start()
    rows_c = [
        remote(patch_tile.at[j], patch_rows.at[p.m], mod_send.at[3, k], mod_recv.at[3, k], batch=p.b, mod=j)
        for k, j in enumerate((p.core, p.far, p.farcore))
    ]
    for c in rows_c:
        c.start()
    patch_g.start()
    for c in gains:
        c.wait_recv()
    gain_sum[...] = gain_mod[0] + gain_mod[1] + gain_mod[2] + gain_mod[3]
    so_t[...] = w_so[...].T
    co_t[...] = w_co[...].T
    down_t[...] = w_down[...].T
    g.pump(0)
    text_g.forward()
    dy_g.start()
    g.pump(1)
    patch_g.forward()
    g.pump(3)
    dy_g.forward()
    for t in range(4):
        g.arrived(t)
    text_g.finish()
    patch_g.finish()
    dy_g.finish()
    for c in gains:
        c.wait_send()
    for c in rows_c:
        c.wait_recv()
        c.wait_send()
    g.sent()


def first_call(n_batch, text, patches, gain_tile, patch_tile, w_qkv, w_so, w_co, w_down, cot, valid):
    n_out = n_batch // 2
    dma = pltpu.SemaphoreType.DMA
    j, rows, columns = w_qkv.shape
    return pl.pallas_call(
        functools.partial(first_kernel, n_batch),
        out_shape=[
            jax.ShapeDtypeStruct((4,) + text.shape, BF),
            jax.ShapeDtypeStruct((4,) + patches.shape, BF),
            jax.ShapeDtypeStruct((n_batch,) + gain_tile.shape, BF),
            jax.ShapeDtypeStruct(patch_tile.shape, BF),
            jax.ShapeDtypeStruct((j, rows * n_batch, columns), BF),
            jax.ShapeDtypeStruct((4,) + cot.shape, BF),
        ]
        + [jax.ShapeDtypeStruct(w.shape[::-1], BF) for w in (w_so, w_co, w_down)],
        in_specs=[pl.BlockSpec(memory_space=pltpu.VMEM)] * 10,
        out_specs=[pl.BlockSpec(memory_space=pl.ANY)] * 6 + [pl.BlockSpec(memory_space=pltpu.VMEM)] * 3,
        scratch_shapes=[
            pltpu.VMEM(cot.shape, BF),
            pltpu.VMEM((4,) + gain_tile.shape, BF),
            pltpu.VMEM(gain_tile.shape, BF),
        ]
        + BatchGather.semaphores(n_out, 4)
        + [dma((5, 3)), dma((5, 3)), dma((5,))],
        compiler_params=pltpu.CompilerParams(collective_id=0, has_side_effects=True),
        cost_estimate=pl.CostEstimate(flops=10**6, bytes_accessed=300 * 10**6, transcendentals=0),
    )(text, patches, gain_tile, patch_tile, w_qkv, w_so, w_co, w_down, cot, valid)


def mm(a, b):
    return lax.dot_general(a, b, (((1,), (0,)), ((), ())), preferred_element_type=F32)


def mm_nt(a, b):
    return lax.dot_general(a, b, (((1,), (1,)), ((), ())), preferred_element_type=F32)


def mm_tn(a, b):
    return lax.dot_general(a, b, (((0,), (0,)), ((), ())), preferred_element_type=F32)


class Local:
    def __init__(self, sems):
        self.sems = sems
        self.used = 0

    def go(self, src, dst):
        copy = pltpu.make_async_copy(src, dst, self.sems.at[self.used])
        self.used += 1
        copy.start()
        return copy


STEP = 32


def each_rows(rows, body, step=STEP):
    def one(r, carry):
        body(pl.ds(pl.multiple_of(r * step, step), step))
        return carry

    lax.fori_loop(0, rows // step, one, 0)


def each(count, body, first=0):
    def one(k, carry):
        body(k)
        return carry

    lax.fori_loop(first, count, one, 0)


def cols(n, width):
    return pl.ds(pl.multiple_of(n * width, width), width)


def rms_of(values, gain):
    return values * lax.rsqrt(jnp.mean(values * values, axis=-1, keepdims=True) + 1e-06) * gain


def attend(q_ref, k_ref, v_ref, out_ref, lse_ref, j, allowed, heads):
    for h in range(heads):
        at = pl.ds(h * HD, HD)
        s = mm_nt(q_ref[j, :, at], k_ref[j, :, at]) * HD ** (-0.5)
        s = jnp.where(allowed, s, -1e30)
        top = jnp.max(s, axis=-1, keepdims=True)
        e = jnp.exp(s - top)
        total = jnp.sum(e, axis=-1, keepdims=True)
        probs = (e / total).astype(BF)
        out_ref[j, :, at] = mm(probs, v_ref[j, :, at]).astype(BF)
        lse_ref[j, :, pl.ds(h, 1)] = top + jnp.log(total)


def causal_ok(key_row, rows):
    shape = (rows, key_row.shape[1])
    return (lax.broadcasted_iota(jnp.int32, shape, 1) <= lax.broadcasted_iota(jnp.int32, shape, 0)) & (
        jnp.broadcast_to(key_row, shape) > 0.5
    )


class BranchSum:
    def __init__(self, place, bufs, send, recv, step=512):
        self.p = place
        self.step = step
        self.fs, self.ns, self.cf, self.yr, self.cn = bufs
        self.to_core = remote(self.fs, self.cf, send.at[0], recv.at[0], batch=place.b, mod=place.core)
        self.to_far = remote(self.fs, self.yr, send.at[1], recv.at[1], batch=place.b, mod=place.far)
        self.to_near = remote(self.ns, self.cn, send.at[2], recv.at[2], batch=place.b, mod=place.core)

    def send(self, part):
        p, step = self.p, self.step
        n = self.fs.shape[1] // step

        def first(k):
            self.fs[:, cols(k, step)] = part(p.farcore, k).astype(BF)

        def second(k):
            self.ns[:, cols(k, step)] = part(p.core, k).astype(BF)

        def third(k):
            at = cols(k, step)
            self.fs[:, at] = (part(p.far, k) + self.cf[:, at].astype(F32)).astype(BF)

        each(n, first)
        self.to_core.start()
        each(n, second)
        self.to_near.start()
        self.to_core.wait()
        each(n, third)
        self.to_far.start()

    def receive(self):
        self.to_near.wait_recv()
        self.to_far.wait_recv()

    def others(self, rows, at=slice(None)):
        return self.cn[rows, at].astype(F32) + self.yr[rows, at].astype(F32)

    def sent(self):
        self.to_near.wait_send()
        self.to_far.wait_send()


def halves(shard, whole, rows):
    half = rows // 2

    def piece(k):
        return (shard.at[pl.ds(k * half, half)], lambda q: whole.at[pl.ds(q * rows + k * half, half)])

    return [piece(0), piece(1)]


def forward_kernel(n_batch, *refs):
    (text_all, patch_all, gains, patch_own, key_ok, cross_ok, qkv_w,
     w_so, w_ckv, w_cq, w_co, w_gu, w_down) = refs[:13]
    (so_all, patch_w, ckv_all, cq_all, co_all, gu_all, down_all, act1_o, act2_o, act3_o, qkv_o, cqkv_o,
     ctx_o, cctx_o, lse_o, clse_o, pp_o, x1_o, x2_o, gate_o, up_o, h_o) = refs[13:35]
    (act, x, wq, wo, wp, pat, pp, qkv, ctx, lse, fs, ns, cf, yr, cn, wg, gate, gate_b, up, hid,
     z_send, z_recv, x_send, x_recv, own, mod_send, mod_recv, sum_send, sum_recv, loc) = refs[35:]
    p = Place(n_batch)
    local = Local(loc)
    rows, width = x.shape
    heads = wq.shape[2] // HD
    cq_r, pr = w_cq.shape[0], patch_own.shape[0]
    g = BatchGather(
        p,
        [
            (w_so, lambda q: so_all.at[pl.ds(q * cq_r, cq_r)]),
            (patch_own, lambda q: patch_w.at[pl.ds(q * pr, pr)]),
            (w_ckv.at[0], lambda q: ckv_all.at[0, pl.ds(q * cq_r, cq_r)]),
            (w_ckv.at[1], lambda q: ckv_all.at[1, pl.ds(q * cq_r, cq_r)]),
            (w_cq, lambda q: cq_all.at[pl.ds(q * cq_r, cq_r)]),
            (w_co, lambda q: co_all.at[pl.ds(q * cq_r, cq_r)]),
        ]
        + halves(w_gu.at[0], gu_all.at[0], cq_r)
        + halves(w_gu.at[1], gu_all.at[1], cq_r)
        + halves(w_down, down_all, cq_r),
        (z_send, z_recv, x_send, x_recv, own),
    )
    SO, PATCH, CK, CV, CQ, CO, GATE, GATE2, UP, UP2, DOWN, DOWN2 = range(12)
    load_act = local.go(text_all, act)
    load_q = local.go(qkv_w, wq)
    load_pat = local.go(patch_all, pat)
    p.greet()
    g.start()
    bufs = (fs, ns, cf, yr, cn)
    one = BranchSum(p, bufs, sum_send.at[0], sum_recv.at[0])
    two = BranchSum(p, bufs, sum_send.at[1], sum_recv.at[1])
    act_block = lambda j: act.at[j]
    col_w = wq.shape[2]
    pp_g = ModGather(p, lambda j: pp.at[:, :, pl.ds(pl.multiple_of(j * col_w, col_w), col_w)], mod_send.at[0], mod_recv.at[0])
    a2_g = ModGather(p, act_block, mod_send.at[1], mod_recv.at[1])
    a3_g = ModGather(p, act_block, mod_send.at[2], mod_recv.at[2])

    load_act.wait()
    x[...] = act[p.m].astype(F32)

    def norm_one(j):
        def body(r):
            act[j, r, :] = rms_of(act[j, r, :].astype(F32), gains[pl.ds(0, 1), :]).astype(BF)

        each_rows(rows, body)

    each(4, norm_one)
    save_act = local.go(act, act1_o)
    load_q.wait()

    def project(j):
        for w in range(3):
            qkv[w, j] = mm(act[j], wq[w]).astype(BF)

    each(4, project)
    save_qkv = local.go(qkv, qkv_o)
    g.pump(SO)
    attend_one = lambda j: attend(qkv.at[0], qkv.at[1], qkv.at[2], ctx, lse, j, causal_ok(key_ok[j, pl.ds(0, 1), :], rows), heads)
    each(4, attend_one)
    save_ctx = local.go(ctx, ctx_o)
    save_lse = local.go(lse, lse_o)
    g.arrived(SO)
    load_o = local.go(so_all, wo)
    save_act.wait()
    save_qkv.wait()
    load_o.wait()
    part = lambda j, k: mm_nt(ctx[j], wo[cols(k, 512), :])
    one.send(part)

    def add_own(k):
        at = cols(k, 512)
        x[:, at] += part(p.m, k)

    each(width // 512, add_own)
    g.arrived(PATCH)
    if pr != cq_r:
        wp[...] = jnp.zeros(wp.shape, BF)
    for c in [local.go(patch_w.at[pl.ds(q * pr, pr)], wp.at[pl.ds(q * cq_r, pr)]) for q in range(n_batch)]:
        c.wait()
    load_pat.wait()
    own_cols = pl.ds(pl.multiple_of(p.m * col_w, col_w), col_w)

    def project_patch(j):
        pp[j, :, own_cols] = mm(pat[j], wp[...]).astype(BF)

    each(4, project_patch)
    pp_g.start()
    one.receive()

    def finish_one(r):
        x[r, :] += one.others(r)
        act[p.m, r, :] = rms_of(x[r, :], gains[pl.ds(1, 1), :]).astype(BF)

    each_rows(rows, finish_one)
    a2_g.start()
    save_x = local.go(x, x1_o)
    one.sent()
    g.pump(CV)
    pp_g.forward()
    g.pump(CQ)
    a2_g.forward()
    g.arrived(CK)
    load_ck = local.go(ckv_all.at[0], wq.at[1])
    pp_g.finish()
    save_pp = local.go(pp, pp_o)
    load_ck.wait()

    def project_pp(w):
        def body(j):
            qkv[w, j] = mm(pp[j], wq[w]).astype(BF)

        return body

    each(4, project_pp(1))
    g.arrived(CV)
    load_cv = local.go(ckv_all.at[1], wq.at[2])
    load_cv.wait()
    each(4, project_pp(2))
    g.arrived(CQ)
    load_cq = local.go(cq_all, wq.at[0])
    a2_g.finish()
    save_act = local.go(act, act2_o)
    load_cq.wait()

    def project_cq(j):
        qkv[0, j] = mm(act[j], wq[0]).astype(BF)

    each(4, project_cq)
    save_ctx.wait()
    save_lse.wait()
    save_qkv = local.go(qkv, cqkv_o)

    def attend_two(j):
        ok = jnp.broadcast_to(cross_ok[j, pl.ds(0, 1), :], (rows, cross_ok.shape[2])) > 0.5
        attend(qkv.at[0], qkv.at[1], qkv.at[2], ctx, lse, j, ok, heads)

    each(4, attend_two)
    save_ctx = local.go(ctx, cctx_o)
    save_lse = local.go(lse, clse_o)
    g.arrived(CO)
    load_o = local.go(co_all, wo)
    save_act.wait()
    save_x.wait()
    load_o.wait()
    two.send(part)
    each(width // 512, add_own)
    g.pump(GATE2)
    two.receive()

    def finish_two(r):
        x[r, :] += two.others(r)
        act[p.m, r, :] = rms_of(x[r, :], gains[pl.ds(2, 1), :]).astype(BF)

    each_rows(rows, finish_two)
    a3_g.start()
    save_x = local.go(x, x2_o)
    two.sent()
    g.pump(UP)
    a3_g.forward()
    a3_g.finish()
    save_act = local.go(act, act3_o)

    g.arrived(GATE)
    g.arrived(GATE2)
    load_g = local.go(gu_all.at[0], wg)
    load_g.wait()

    def gate_one(j):
        gate[j] = mm(act[j], wg[...])
        gate_b[j] = gate[j].astype(BF)

    each(4, gate_one)
    save_gate = local.go(gate_b, gate_o)
    g.arrived(UP)
    g.arrived(UP2)
    load_g = local.go(gu_all.at[1], wg)
    load_g.wait()

    def up_one(j):
        u = mm(act[j], wg[...])
        up[j] = u.astype(BF)
        hid[j] = (jax.nn.gelu(gate[j], approximate=True) * u).astype(BF)

    each(4, up_one)
    save_up = local.go(up, up_o)
    save_h = local.go(hid, h_o)
    g.arrived(DOWN)
    g.arrived(DOWN2)
    g.sent()
    for c in (save_act, save_x, save_gate, save_up, save_h, save_ctx, save_lse, save_qkv, save_pp):
        c.wait()


def forward_call(n_batch, text_all, patch_all, gains, patch_own, key_ok, cross_ok, qkv_w,
                 w_so, w_ckv, w_cq, w_co, w_gu, w_down):
    n_out = n_batch // 2
    dma = pltpu.SemaphoreType.DMA
    items, rows, width = text_all.shape
    c, f = qkv_w.shape[2], w_gu.shape[2]
    patch_width = patch_all.shape[2]
    keys = patch_all.shape[1]
    sds = jax.ShapeDtypeStruct
    any_ = pl.BlockSpec(memory_space=pl.ANY)
    vmem = pl.BlockSpec(memory_space=pltpu.VMEM)
    big = (items, rows, width)
    return pl.pallas_call(
        functools.partial(forward_kernel, n_batch),
        out_shape=[
            sds((width, c), BF), sds((n_batch * patch_own.shape[0], c), BF), sds((2, width, c), BF), sds((width, c), BF),
            sds((width, c), BF), sds((2, width, f), BF), sds((width, f), BF),
            sds(big, BF), sds(big, BF), sds(big, BF),
            sds((3, items, rows, c), BF), sds((3, items, rows, c), BF),
            sds((items, rows, c), BF), sds((items, rows, c), BF),
            sds((items, rows, 128), F32), sds((items, rows, 128), F32),
            sds((items, keys, width), BF), sds((rows, width), F32), sds((rows, width), F32),
            sds((items, rows, f), BF), sds((items, rows, f), BF), sds((items, rows, f), BF),
        ],
        in_specs=[any_, any_, vmem, vmem, vmem, vmem, any_] + [vmem] * 6,
        out_specs=[any_] * 22,
        scratch_shapes=[
            pltpu.VMEM(big, BF), pltpu.VMEM((rows, width), F32), pltpu.VMEM((3, width, c), BF),
            pltpu.VMEM((width, c), BF), pltpu.VMEM((patch_width, c), BF), pltpu.VMEM((items, keys, patch_width), BF),
            pltpu.VMEM((items, keys, width), BF), pltpu.VMEM((3, items, rows, c), BF), pltpu.VMEM((items, rows, c), BF),
            pltpu.VMEM((items, rows, 128), F32),
        ]
        + [pltpu.VMEM((rows, width), BF)] * 5
        + [pltpu.VMEM((width, f), BF), pltpu.VMEM((items, rows, f), F32), pltpu.VMEM((items, rows, f), BF), pltpu.VMEM((items, rows, f), BF), pltpu.VMEM((items, rows, f), BF)]
        + BatchGather.semaphores(n_out, 12)
        + [dma((3, 3)), dma((3, 3)), dma((2, 3)), dma((2, 3)), dma((32 + n_batch,))],
        compiler_params=pltpu.CompilerParams(collective_id=1, has_side_effects=True, vmem_limit_bytes=VMEM_LIMIT),
        cost_estimate=pl.CostEstimate(flops=35 * 10**9, bytes_accessed=600 * 10**6, transcendentals=0),
    )(text_all, patch_all, gains, patch_own, key_ok, cross_ok, qkv_w, w_so, w_ckv, w_cq, w_co, w_gu, w_down)


class GradSum:
    def __init__(self, place, pieces, mine, got, sems, loc):
        self.p = place
        self.pieces = pieces
        self.mine, self.got = mine, got
        self.x_send, self.x_recv, self.z_send, self.z_recv = sems
        self.loc = loc
        self.ready = self.started = self.done = 0
        self.window = 1

    @staticmethod
    def semaphores(n_out, count):
        dma = pltpu.SemaphoreType.DMA
        return [dma((count,)), dma((count,)), dma((count, n_out)), dma((count, n_out))]

    def x_copy(self, t):
        whole, from_x, _ = self.pieces[t]
        return remote(whole.at[:, 1 - self.p.inner], from_x, self.x_send.at[t], self.x_recv.at[t],
                      batch=self.p.x_peer, mod=self.p.m)

    def z_copy(self, t, s):
        _, from_x, from_z = self.pieces[t]
        return remote(from_x.at[(self.p.outer + s) % self.p.n_out], from_z.at[s], self.z_send.at[t, s],
                      self.z_recv.at[t, s], batch=self.p.z_peer(s), mod=self.p.m)

    def kick(self):
        while self.started < self.ready and self.started - self.done < self.window:
            self.x_copy(self.started).start()
            self.started += 1

    def add(self):
        self.ready += 1
        self.kick()

    def pump(self, count=1):
        for _ in range(min(count, self.ready - self.done)):
            t = self.done
            whole, from_x, from_z = self.pieces[t]
            n_out, rows, width = from_x.shape
            self.x_copy(t).wait_recv()
            self.done += 1
            self.kick()
            mine = self.mine.at[:, pl.ds(0, rows), pl.ds(0, width)]
            got = self.got.at[:, pl.ds(0, rows), pl.ds(0, width)]
            one = pltpu.make_async_copy(whole.at[:, self.p.inner], mine, self.loc.at[0])
            two = pltpu.make_async_copy(from_x, got, self.loc.at[1])
            one.start()
            two.start()
            one.wait()
            two.wait()
            step = 16

            def body(o):
                def add(r):
                    mine[o, r, :] = (mine[o, r, :].astype(F32) + got[o, r, :].astype(F32)).astype(BF)

                each_rows(rows, add, step)

            each(n_out, body)
            one = pltpu.make_async_copy(mine, from_x, self.loc.at[0])
            two = pltpu.make_async_copy(mine.at[self.p.outer], from_z.at[0], self.loc.at[1])
            one.start()
            two.start()
            one.wait()
            for s in self.p.shifts:
                self.z_copy(t, s).start()
            two.wait()

    def finish(self):
        self.pump(len(self.pieces))
        for t in range(len(self.pieces)):
            self.x_copy(t).wait_send()
            for s in self.p.shifts:
                self.z_copy(t, s).wait()


def attend_back(q_ref, k_ref, v_ref, do_ref, lse_ref, dq_ref, dk_ref, dv_ref, j, allowed, heads):
    scale = HD ** (-0.5)
    for h in range(heads):
        at = pl.ds(h * HD, HD)
        q, k, v, do = q_ref[j, :, at], k_ref[j, :, at], v_ref[j, :, at], do_ref[j, :, at]
        s = jnp.where(allowed, mm_nt(q, k) * scale, -1e30)
        probs = jnp.exp(s - lse_ref[j, :, pl.ds(h, 1)])
        dp = mm_nt(do, v)
        ds = (probs * (dp - jnp.sum(probs * dp, axis=-1, keepdims=True))).astype(BF)
        dv_ref[j, :, at] = mm_tn(probs.astype(BF), do).astype(BF)
        dq_ref[j, :, at] = (mm(ds, k) * scale).astype(BF)
        dk_ref[j, :, at] = (mm_tn(ds, q) * scale).astype(BF)


def gelu_parts(g):
    c = 0.7978845608028654
    t = jnp.tanh(c * (g + 0.044715 * g * g * g))
    half = 0.5 * (1.0 + t)
    return g * half, half + 0.5 * g * (1.0 - t * t) * c * (1.0 + 3 * 0.044715 * g * g)


def backward_kernel(n_batch, *refs):
    (dy_all, text, pat_all, gains, key_ok, cross_ok, qkv_w, so_all, ckv_all, cq_all, co_all, gu_all, down_all,
     act1, act2, act3, qkv_i, cqkv_i, ctx_i, cctx_i, lse_i, clse_i, pp_i, x1_i, x2_i, gate_i, up_i, h_i) = refs[:28]
    (result, d_text, gain_out, whole_f, from_x_f, from_z_f, whole_c, from_x_c, from_z_c,
     whole_p, from_x_p, from_z_p) = refs[28:40]
    (dy, act_a, act_b, gate, up, hid, w0, w1, qkv, dqkv, ctx, dctx, dpp, lse, g, da, v, fs, ns, cf, yr, cn,
     cf2, yr2, cn2, st, mine, got, dg, dgm, dgx, dgz,
     gx_send, gx_recv, gz_send, gz_recv, mod_send, mod_recv, sum_send, sum_recv, gain_send, gain_recv,
     gx, loc, loc2) = refs[40:]
    p = Place(n_batch)
    local = Local(loc)
    items, rows, width = dy.shape
    c, f = qkv_w.shape[2], gu_all.shape[2]
    half = f // 2
    n_out, blk = p.n_out, width // n_batch
    heads = c // HD
    pieces = [(whole_f.at[k], from_x_f.at[k], from_z_f.at[k]) for k in range(6)]
    pieces += [(whole_c.at[k], from_x_c.at[k], from_z_c.at[k]) for k in range(8)]
    pieces.append((whole_p, from_x_p, from_z_p))
    gs = GradSum(p, pieces, mine, got, (gx_send, gx_recv, gz_send, gz_recv), loc2)
    left = pl.ds(0, c)
    right = pl.ds(c, c)

    load_dy = local.go(dy_all, dy)
    load_h = local.go(h_i, hid)
    load_w0 = local.go(down_all, w0)
    load_v = local.go(x2_i, v)
    load_gate = local.go(gate_i, gate)
    load_up = local.go(up_i, up)
    load_w1 = local.go(gu_all.at[0], w1)
    load_a = local.go(act3, act_a)
    load_b = local.go(act2, act_b)
    p.greet()
    set_a = (fs, ns, cf, yr, cn)
    set_b = (fs, ns, cf2, yr2, cn2)
    sums = [
        BranchSum(p, bufs, sum_send.at[k], sum_recv.at[k])
        for k, bufs in enumerate((set_b, set_a, set_a, set_b, set_a))
    ]
    gathers = [ModGather(p, lambda j: dy.at[j], mod_send.at[k], mod_recv.at[k]) for k in range(2)]
    dg[...] = jnp.zeros(dg.shape, F32)

    def piece(acts, grads, first, count):
        t = gs.ready
        whole = pieces[t][0]
        used = whole.shape[2]
        chunk = max(256, 2 * blk)
        per = chunk // (2 * blk)

        def body(n):
            a = acts[:, :, cols(n, chunk)].reshape(items * rows, chunk)
            b = grads[:, :, pl.ds(first, count)].reshape(items * rows, count)
            st[pl.ds(n * per, per), :, :, pl.ds(0, count)] = mm_tn(a, b).astype(BF).reshape(per, 2, blk, count)

        each(width // chunk, body)
        copy = pltpu.make_async_copy(st.at[:, :, pl.ds(0, used), pl.ds(0, count)], whole, loc2.at[2])
        copy.start()
        copy.wait()
        gs.add()

    def norm_back(k, total, v_rows):
        def body(r):
            grad = da[r, :] + total.others(r)
            val = v_rows(r)
            factor = lax.rsqrt(jnp.mean(val * val, axis=-1, keepdims=True) + 1e-06)
            dg[pl.ds(k, 1), :] += jnp.sum(grad * val * factor, axis=0, keepdims=True)
            scaled = gains[pl.ds(k, 1), :] * grad
            back = factor * scaled - val * (factor * factor * factor * jnp.mean(scaled * val, axis=-1, keepdims=True))
            g[r, :] += back
            if k:
                dy[p.m, r, :] = g[r, :].astype(BF)

        each_rows(rows, body)

    load_dy.wait()
    load_h.wait()
    g[...] = dy[p.m].astype(F32)
    piece(dy, hid, 0, half)
    piece(dy, hid, half, half)
    load_w0.wait()
    load_v.wait()
    out_part = lambda j, k: mm_nt(hid[j], w0[cols(k, 512), :])
    sums[0].send(out_part)

    def result_own(k):
        at = cols(k, 512)
        da[:, at] = v[:, at] + out_part(p.m, k)

    each(width // 512, result_own)
    load_gate.wait()
    load_up.wait()

    def mix_back(j):
        dh = mm(dy[j], w0[...])
        value, slope = gelu_parts(gate[j].astype(F32))
        gate[j] = (dh * up[j].astype(F32) * slope).astype(BF)
        hid[j] = (dh * value).astype(BF)

    each(items, mix_back)
    load_w0 = local.go(gu_all.at[1], w0)
    gs.pump()
    sums[0].receive()

    def result_done(r):
        da[r, :] += sums[0].others(r)

    each_rows(rows, result_done)
    save_result = local.go(da, result)
    sums[0].sent()
    load_w1.wait()
    load_w0.wait()
    act_part = lambda j, k: mm_nt(gate[j], w1[cols(k, 512), :]) + mm_nt(hid[j], w0[cols(k, 512), :])
    sums[1].send(act_part)
    save_result.wait()

    def own_part(part):
        def body(k):
            da[:, cols(k, 512)] = part(p.m, k)

        each(width // 512, body)

    own_part(act_part)
    load_w0 = [local.go(co_all, w0.at[:, left]), local.go(cq_all, w0.at[:, right])]
    load_w1 = [local.go(ckv_all.at[0], w1.at[:, left]), local.go(ckv_all.at[1], w1.at[:, right])]
    load_s = [local.go(cqkv_i, qkv), local.go(cctx_i, ctx), local.go(clse_i, lse)]
    load_a.wait()
    piece(act_a, gate, 0, half)
    piece(act_a, gate, half, half)
    gs.pump()
    sums[1].receive()
    norm_back(2, sums[1], lambda r: v[r, :])
    gathers[0].start()
    sums[1].sent()
    load_v = local.go(x1_i, v)
    piece(act_a, hid, 0, half)
    piece(act_a, hid, half, half)
    load_a = local.go(pp_i, act_a)
    gs.pump()
    gathers[0].forward()
    gathers[0].finish()

    for copy in load_w0 + load_w1 + load_s:
        copy.wait()

    def ctx_back(j):
        dctx[j] = mm(dy[j], w0[:, left]).astype(BF)

    each(items, ctx_back)
    piece(dy, ctx, 0, c)

    def cross_back(j):
        ok = jnp.broadcast_to(cross_ok[j, pl.ds(0, 1), :], (rows, cross_ok.shape[2])) > 0.5
        attend_back(qkv.at[0], qkv.at[1], qkv.at[2], dctx, lse, dqkv.at[0], dqkv.at[1], dqkv.at[2], j, ok, heads)

    each(items, cross_back)
    query_part = lambda j, k: mm_nt(dqkv[0, j], w0[cols(k, 512), right])
    sums[2].send(query_part)
    gs.pump()
    own_part(query_part)
    load_w0 = [local.go(so_all, w0.at[:, left]), local.go(qkv_w.at[0], w0.at[:, right])]
    load_s = [local.go(qkv_i, qkv), local.go(ctx_i, ctx), local.go(lse_i, lse)]
    load_b.wait()
    piece(act_b, dqkv.at[0], 0, c)
    load_b = local.go(act1, act_b)
    load_a.wait()
    piece(act_a, dqkv.at[1], 0, c)
    load_v.wait()
    sums[2].receive()
    norm_back(1, sums[2], lambda r: v[r, :])
    gathers[1].start()
    sums[2].sent()
    piece(act_a, dqkv.at[2], 0, c)
    load_a = local.go(pat_all, act_a)
    gs.pump()
    gathers[1].forward()
    gathers[1].finish()

    proj_part = lambda j, k: mm_nt(dqkv[1, k], w1[cols(j, c), left]) + mm_nt(dqkv[2, k], w1[cols(j, c), right])
    sums[3].send(proj_part)

    def proj_own(k):
        dpp[k] = proj_part(p.m, k).astype(BF)

    each(items, proj_own)
    load_w1 = [local.go(qkv_w.at[1], w1.at[:, left]), local.go(qkv_w.at[2], w1.at[:, right])]

    for copy in load_w0 + load_s:
        copy.wait()
    each(items, ctx_back)
    piece(dy, ctx, 0, c)
    gs.pump()

    def self_back(j):
        ok = causal_ok(key_ok[j, pl.ds(0, 1), :], rows)
        attend_back(qkv.at[0], qkv.at[1], qkv.at[2], dctx, lse, dqkv.at[0], dqkv.at[1], dqkv.at[2], j, ok, heads)

    each(items, self_back)
    gs.pump()
    sums[3].receive()

    def proj_done(k):
        every = pl.ds(0, rows)
        dpp[k] = (dpp[k].astype(F32) + sums[3].others(every, cols(k, c))).astype(BF)

    each(items, proj_done)
    sums[3].sent()
    for copy in load_w1:
        copy.wait()
    self_part = lambda j, k: (
        mm_nt(dqkv[0, j], w0[cols(k, 512), right])
        + mm_nt(dqkv[1, j], w1[cols(k, 512), left])
        + mm_nt(dqkv[2, j], w1[cols(k, 512), right])
    )
    sums[4].send(self_part)
    own_part(self_part)
    gs.pump()
    load_b.wait()
    for k in range(3):
        piece(act_b, dqkv.at[k], 0, c)
    load_a.wait()
    piece(act_a, dpp, 0, c)
    gs.pump()
    sums[4].receive()
    norm_back(0, sums[4], lambda r: text[r, :].astype(F32))
    save_text = local.go(g, d_text)
    sums[4].sent()

    mod_g = [
        remote(dg, dgm.at[k], gain_send.at[k], gain_recv.at[k], batch=p.b, mod=j)
        for k, j in enumerate((p.core, p.far, p.farcore))
    ]
    for copy in mod_g:
        copy.start()
    gs.pump()
    for copy in mod_g:
        copy.wait()
    dg[...] += dgm[0] + dgm[1] + dgm[2]
    across = remote(dg, dgx, gx.at[0], gx.at[1], batch=p.x_peer, mod=p.m)
    across.start()
    gs.pump()
    across.wait()
    dg[...] += dgx[...]
    along = [
        remote(dg, dgz.at[s], gain_send.at[3 + s], gain_recv.at[3 + s], batch=p.z_peer(s), mod=p.m)
        for s in p.shifts
    ]
    for copy in along:
        copy.start()
    gs.pump()
    for copy in along:
        copy.wait()
    total = dg[...]
    for s in p.shifts:
        total = total + dgz[s]
    gain_out[...] = total
    gs.finish()
    save_text.wait()


def backward_call(n_batch, inputs, patch_rows):
    n_out = n_batch // 2
    dma = pltpu.SemaphoreType.DMA
    sds = jax.ShapeDtypeStruct
    items, rows, width = inputs[0].shape
    c, f = inputs[6].shape[2], inputs[11].shape[2]
    blk = width // n_batch
    any_ = pl.BlockSpec(memory_space=pl.ANY)
    vmem = pl.BlockSpec(memory_space=pltpu.VMEM)
    big = (items, rows, width)
    heads_shape = (items, rows, c)
    V = lambda shape, dtype=BF: pltpu.VMEM(shape, dtype)

    def bufs(count, r, w):
        lead = (count,) if count else ()
        return [sds(lead + (n_out, 2, r, w), BF), sds(lead + (n_out, r, w), BF), sds(lead + (n_out, r, w), BF)]

    return pl.pallas_call(
        functools.partial(backward_kernel, n_batch),
        out_shape=[sds((rows, width), F32), sds((rows, width), F32), sds((8, width), F32)]
        + bufs(6, blk, f // 2) + bufs(8, blk, c) + bufs(0, patch_rows, c),
        in_specs=[any_, vmem, any_, vmem, vmem, vmem] + [any_] * 22,
        out_specs=[any_, any_, vmem] + [any_] * 9,
        scratch_shapes=[V(big)] * 3
        + [V((items, rows, f))] * 3
        + [V((width, f))] * 2
        + [V((3,) + heads_shape)] * 2
        + [V(heads_shape)] * 3
        + [V((items, rows, 128), F32)]
        + [V((rows, width), F32)] * 3
        + [V((rows, width))] * 8
        + [V((n_out, 2, blk, f // 2)), V((n_out, blk, f // 2)), V((n_out, blk, f // 2))]
        + [V((8, width), F32), V((3, 8, width), F32), V((8, width), F32), V((n_out, 8, width), F32)]
        + GradSum.semaphores(n_out, 15)
        + [dma((2, 3)), dma((2, 3)), dma((5, 3)), dma((5, 3)), dma((3 + n_out,)), dma((3 + n_out,)), dma((2,)),
           dma((48,)), dma((3,))],
        compiler_params=pltpu.CompilerParams(collective_id=2, has_side_effects=True, vmem_limit_bytes=VMEM_LIMIT),
        cost_estimate=pl.CostEstimate(flops=75 * 10**9, bytes_accessed=800 * 10**6, transcendentals=0),
    )(*inputs)


def local(n_batch, n_mod, text, patches, text_lengths, patch_mask, cotangent, gains,
          w_qkv, w_so, w_cq, w_ckv, w_co, w_patch, w_gu, w_down):
    own_items, text_rows, width = text.shape
    mod = lax.axis_index("mod")
    nb = n_batch
    blk = width // nb
    positions = jnp.arange(text_rows)

    gw = blk // n_mod
    gain_tile = lax.dynamic_update_slice(jnp.zeros((16, blk), BF), gains, (0, mod * gw))
    col_w = width // n_mod
    pr = w_patch.shape[0]
    pr_pad = -(-pr // 16) * 16
    patch_tile = jnp.pad(w_patch, ((0, pr_pad - pr), (0, 0))).reshape(pr_pad, n_mod, col_w)
    patch_tile = jnp.transpose(patch_tile, (1, 0, 2))
    block, block_pad = n_mod * pr, -(-n_mod * pr // 16) * 16
    patch_in = jnp.pad(patches[0].reshape(-1, nb, block), ((0, 0), (0, 0), (0, blk - block))).reshape(-1, width)
    own_length = lax.dynamic_slice_in_dim(text_lengths, mod * own_items, own_items)
    valid = jnp.broadcast_to((positions[:, None] < own_length).astype(F32), (text_rows, 128))
    text_all, patch_all, gain_raw, patch_rows, self_qkv, dy_all, so_t, co_t, down_t = first_call(
        n_batch, text[0], patch_in, gain_tile, patch_tile, w_qkv, w_so, w_co, w_down, cotangent[0], valid
    )
    gain_all = jnp.transpose(gain_raw[:, :8], (1, 0, 2)).reshape(8, width).astype(F32)
    patch_own = patch_rows[:, :pr].reshape(block, col_w)
    patch_own = jnp.pad(patch_own, ((0, block_pad - block), (0, 0)))
    row_ok = (positions[None, :] < text_lengths[:, None]).astype(F32)
    key_ok = jnp.broadcast_to(row_ok[:, None, :], (n_mod, 8, text_rows))
    cross_ok = jnp.broadcast_to((patch_mask > 0).astype(F32)[:, None, :], (n_mod, 8, patch_mask.shape[1]))
    (so_all, _, ckv_all, cq_all, co_all, gu_all, down_all, act1, act2, act3, qkv, cqkv,
     ctx, cctx, lse, clse, pp, x1, x2, gate, up, hid) = forward_call(
        n_batch, text_all, patch_all, gain_all, patch_own, key_ok, cross_ok, self_qkv,
        so_t, w_ckv, w_cq, co_t, w_gu, down_t)
    outs = backward_call(
        n_batch,
        (dy_all, text[0], patch_all, gain_all, key_ok, cross_ok, self_qkv, so_all, ckv_all, cq_all, co_all, gu_all,
         down_all, act1, act2, act3, qkv, cqkv, ctx, cctx, lse, clse, pp, x1, x2, gate, up, hid),
        block_pad,
    )
    result, d_text, gain_sum = outs[:3]
    sum_f, sum_c, sum_p = outs[5], outs[8], outs[11]
    at = lax.axis_index("batch") * blk + mod * gw
    d_gains = lax.dynamic_slice(gain_sum, (0, at), (3, gw))

    def total(parts, axis=0):
        return jnp.sum(parts.astype(F32), axis=axis)

    def pair(k):
        return jnp.concatenate([total(sum_f[k]), total(sum_f[k + 1])], axis=1)

    grad_patch = total(sum_p)[:block].reshape(n_mod, pr, col_w)
    grad_patch = lax.all_to_all(grad_patch, "mod", 0, 0, tiled=True)
    grad_patch = jnp.transpose(grad_patch, (1, 0, 2)).reshape(pr, width)
    return (
        result[None],
        d_text[None],
        d_gains,
        total(sum_c[5:8], 1),
        total(sum_c[4]).T,
        total(sum_c[1]),
        total(sum_c[2:4], 1),
        total(sum_c[0]).T,
        grad_patch,
        jnp.stack([pair(2), pair(4)]),
        pair(0).T,
    )


def solution(mesh):
    placed = (
        P(("batch", "mod"), None, None),
        P(("batch", "mod"), None, None),
        P("batch"),
        P("batch", None),
        P(("batch", "mod"), None, None),
        P(None, ("batch", "mod")),
        P(None, "batch", "mod"),
        P("mod", "batch"),
        P("batch", "mod"),
        P(None, "batch", "mod"),
        P("mod", "batch"),
        P(("batch", "mod"), None),
        P(None, "batch", "mod"),
        P("mod", "batch"),
    )

    def run(*args):
        return local(mesh.shape["batch"], mesh.shape["mod"], *args)

    return jax.shard_map(
        run,
        mesh=mesh,
        in_specs=placed,
        out_specs=(
            P(("batch", "mod"), None, None),
            P(("batch", "mod"), None, None),
            P(None, ("batch", "mod")),
            P(None, "batch", "mod"),
            P("mod", "batch"),
            P("batch", "mod"),
            P(None, "batch", "mod"),
            P("mod", "batch"),
            P(("batch", "mod"), None),
            P(None, "batch", "mod"),
            P("mod", "batch"),
        ),
        check_vma=False,
    )
```

```python
import functools

import jax
import jax.numpy as jnp
from jax import lax
from jax.experimental import pallas as pl
from jax.experimental.pallas import tpu as pltpu
from jax.sharding import PartitionSpec as P

HD = 128
F32 = jnp.float32
BF = jnp.bfloat16


VMEM_LIMIT = 62 * 2**20
MESH = pl.DeviceIdType.MESH


class Place:
    def __init__(self, n_batch):
        self.n_batch = n_batch
        self.n_out = n_batch // 2
        self.b = lax.axis_index("batch")
        self.m = lax.axis_index("mod")
        self.outer = self.b // 2
        self.inner = self.b % 2
        self.core = self.m + 1 - 2 * (self.m % 2)
        self.far = (self.m + 2) % 4
        self.farcore = (self.core + 2) % 4
        self.x_peer = self.b + 1 - 2 * self.inner
        self.line = self.n_out == 4
        self.shifts = [2, 1, 3] if self.line else list(range(1, self.n_out))
        self.is_mid = (self.outer + 1) // 2 == 1
        self.is_end = (self.outer + 1) // 2 != 1
        self.inward = 1 + 2 * (self.outer // 2)
        self.outward = 3 - 2 * (self.outer // 2)
        self.end = 3 * (self.outer // 2)
        self.relay = 2 - self.outer // 3
        self.opposite = 3 - self.outer

    def z_peer(self, s):
        return (self.outer + s) % self.n_out * 2 + self.inner

    def z_from(self, s):
        return (self.outer - s + self.n_out) % self.n_out * 2 + self.inner

    def greet(self):
        barrier = pltpu.get_barrier_semaphore()
        ids = [{"batch": self.z_peer(s), "mod": self.m} for s in self.shifts]
        ids.append({"batch": self.x_peer, "mod": self.m})
        for j in (self.core, self.far, self.farcore):
            ids.append({"batch": self.b, "mod": j})
        for device in ids:
            pl.semaphore_signal(barrier, inc=1, device_id=device, device_id_type=MESH)
        pl.semaphore_wait(barrier, len(ids))


def remote(src, dst, send, recv, **device):
    return pltpu.make_async_remote_copy(
        src_ref=src, dst_ref=dst, send_sem=send, recv_sem=recv, device_id=device, device_id_type=MESH
    )


class BatchGather:
    def __init__(self, place, tensors, sems, wides=(), wide_sems=None):
        self.p = place
        self.tensors = tensors
        self.z_send, self.z_recv, self.x_send, self.x_recv, self.own = sems
        self.started = 0
        self.events = [(t, s) for t in range(len(tensors)) for s in [0] + place.shifts]
        self.at = 0
        self.wides = wides
        self.wide_sems = wide_sems
        self.steps = [step for c in range(len(wides)) for step in ((self.wide_z, c), (self.wide_relay, c))]

    @staticmethod
    def semaphores(n_out, count):
        dma = pltpu.SemaphoreType.DMA
        return [dma((count, n_out)) for _ in range(4)] + [dma((count,))]

    def z_copy(self, t, s):
        src, block = self.tensors[t]
        return remote(src, block(self.p.b), self.z_send.at[t, s], self.z_recv.at[t, s],
                      batch=self.p.z_peer(s), mod=self.p.m)

    def z_relay(self, t):
        where = self.tensors[t][1]((self.p.outer + 2) % 4 * 2 + self.p.inner)
        return remote(where, where, self.z_send.at[t, 0], self.z_recv.at[t, self.p.inward],
                      batch=self.p.end * 2 + self.p.inner, mod=self.p.m)

    def own_copy(self, t):
        src, block = self.tensors[t]
        return pltpu.make_async_copy(src, block(self.p.b), self.own.at[t])

    def x_copy(self, t, s):
        src, block = self.tensors[t]
        where = block(self.p.z_from(s))
        return remote(src if s == 0 else where, where, self.x_send.at[t, s], self.x_recv.at[t, s],
                      batch=self.p.x_peer, mod=self.p.m)

    def straight(self, copy, act):
        p = self.p
        if not p.line:
            for s in p.shifts:
                act(copy(s))
            return
        act(copy(2))
        act(copy(p.inward))

        @pl.when(p.is_mid)
        def _():
            act(copy(p.outward))

    def start(self, count=1):
        for t in range(self.started, min(self.started + count, len(self.tensors))):
            self.straight(lambda s: self.z_copy(t, s), lambda c: c.start())
            self.own_copy(t).start()
            self.started = t + 1

    def pump(self, upto):
        p = self.p
        while self.at < len(self.events) and self.events[self.at][0] <= upto:
            t, s = self.events[self.at]
            if s:
                self.z_copy(t, s).wait_recv()
                if p.line and s == 2:

                    @pl.when(p.is_mid)
                    def _():
                        self.z_relay(t).start()

                if s == p.shifts[-1]:
                    self.start()
            self.x_copy(t, s).start()
            self.at += 1
            if s == p.shifts[-1] and self.steps:
                step, c = self.steps.pop(0)
                step(c)

    def arrived(self, t, ahead=1):
        self.pump(t + ahead)
        self.own_copy(t).wait()
        for s in [0] + self.p.shifts:
            self.x_copy(t, s).wait_recv()

    def wide_own(self, c):
        shard, block, _ = self.wides[c]
        return pltpu.make_async_copy(shard, block(self.p.b), self.wide_sems[2].at[c])

    def wide_x(self, c):
        shard, block, _ = self.wides[c]
        return remote(shard, block(self.p.b), self.wide_sems[0].at[c, 0], self.wide_sems[1].at[c, 0],
                      batch=self.p.x_peer, mod=self.p.m)

    def wide_copy(self, c, s):
        pair = self.wides[c][2](self.p.outer)
        return remote(pair, pair, self.wide_sems[0].at[c, s], self.wide_sems[1].at[c, s],
                      batch=self.p.z_peer(s), mod=self.p.m)

    def wide_on(self, c):
        pair = self.wides[c][2]((self.p.outer + 2) % 4)
        return remote(pair, pair, self.wide_sems[0].at[c, self.p.n_out], self.wide_sems[1].at[c, self.p.inward],
                      batch=self.p.end * 2 + self.p.inner, mod=self.p.m)

    def wide_start(self):
        for c in range(len(self.wides)):
            self.wide_own(c).start()
            self.wide_x(c).start()

    def wide_z(self, c):
        self.wide_own(c).wait()
        self.wide_x(c).wait_recv()
        self.straight(lambda s: self.wide_copy(c, s), lambda d: d.start())

    def wide_relay(self, c):
        if self.p.line:
            self.wide_copy(c, 2).wait_recv()

            @pl.when(self.p.is_mid)
            def _():
                self.wide_on(c).start()

    def sent(self):
        p = self.p
        for step, c in self.steps:
            step(c)
        for t in range(len(self.tensors)):
            self.straight(lambda s: self.z_copy(t, s), lambda c: c.wait_send())
            for s in [0] + p.shifts:
                self.x_copy(t, s).wait_send()
        for c in range(len(self.wides)):
            self.wide_x(c).wait_send()
            self.straight(lambda s: self.wide_copy(c, s), lambda d: d.wait_send())
            for s in p.shifts[1:] if p.line else p.shifts:
                self.wide_copy(c, s).wait_recv()
        if p.line:

            @pl.when(p.is_mid)
            def _():
                for t in range(len(self.tensors)):
                    self.z_relay(t).wait_send()
                for c in range(len(self.wides)):
                    self.wide_on(c).wait_send()


class ModGather:
    def __init__(self, place, block, send, recv):
        self.p = place
        self.block = block
        mine = block(place.m)
        far = block(place.far)
        self.near = remote(mine, mine, send.at[0], recv.at[0], batch=place.b, mod=place.core)
        self.across = remote(mine, mine, send.at[1], recv.at[1], batch=place.b, mod=place.far)
        self.on = remote(far, far, send.at[2], recv.at[2], batch=place.b, mod=place.core)

    def start(self):
        self.across.start()
        self.near.start()

    def forward(self):
        self.across.wait_recv()
        self.on.start()

    def finish(self):
        self.near.wait_recv()
        self.on.wait_recv()
        self.near.wait_send()
        self.across.wait_send()
        self.on.wait_send()


def first_kernel(n_batch, text, patches, gain_tile, patch_tile, w_qkv, w_so, w_co, w_down, cot, valid,
                 text_all, patch_all, gain_all, patch_rows, qkv_all, dy_all, so_t, co_t, down_t,
                 dy, gain_mod, gain_sum, z_send, z_recv, x_send, x_recv, own, mod_send, mod_recv, misc):
    p = Place(n_batch)
    rows = w_qkv.shape[1]
    tensors = [
        (w_qkv.at[0], lambda q: qkv_all.at[0, pl.ds(q * rows, rows)]),
        (w_qkv.at[1], lambda q: qkv_all.at[1, pl.ds(q * rows, rows)]),
        (gain_sum, lambda q: gain_all.at[q]),
        (w_qkv.at[2], lambda q: qkv_all.at[2, pl.ds(q * rows, rows)]),
    ]
    g = BatchGather(p, tensors, (z_send, z_recv, x_send, x_recv, own))
    copies = [
        pltpu.make_async_copy(text, text_all.at[p.m], misc.at[0]),
        pltpu.make_async_copy(patches, patch_all.at[p.m], misc.at[1]),
        pltpu.make_async_copy(gain_tile, gain_mod.at[p.m], misc.at[2]),
        pltpu.make_async_copy(patch_tile.at[p.m], patch_rows.at[p.m], misc.at[3]),
        pltpu.make_async_copy(dy, dy_all.at[p.m], misc.at[4]),
    ]

    def mask_rows(r):
        dy[r, :] = (cot[r, :].astype(F32) * valid[r, pl.ds(0, 1)]).astype(BF)

    each_rows(dy.shape[0], mask_rows)
    for c in copies:
        c.start()
    p.greet()
    gains = [
        remote(gain_tile, gain_mod.at[p.m], mod_send.at[2, k], mod_recv.at[2, k], batch=p.b, mod=j)
        for k, j in enumerate((p.core, p.far, p.farcore))
    ]
    for c in gains:
        c.start()
    g.start()
    for c in copies:
        c.wait()
    text_g = ModGather(p, lambda j: text_all.at[j], mod_send.at[0], mod_recv.at[0])
    patch_g = ModGather(p, lambda j: patch_all.at[j], mod_send.at[1], mod_recv.at[1])
    dy_g = ModGather(p, lambda j: dy_all.at[j], mod_send.at[4], mod_recv.at[4])
    text_g.start()
    rows_c = [
        remote(patch_tile.at[j], patch_rows.at[p.m], mod_send.at[3, k], mod_recv.at[3, k], batch=p.b, mod=j)
        for k, j in enumerate((p.core, p.far, p.farcore))
    ]
    for c in rows_c:
        c.start()
    patch_g.start()
    for c in gains:
        c.wait_recv()
    gain_sum[...] = gain_mod[0] + gain_mod[1] + gain_mod[2] + gain_mod[3]
    so_t[...] = w_so[...].T
    co_t[...] = w_co[...].T
    down_t[...] = w_down[...].T
    g.pump(0)
    text_g.forward()
    dy_g.start()
    g.pump(1)
    patch_g.forward()
    g.pump(3)
    dy_g.forward()
    for t in range(4):
        g.arrived(t)
    text_g.finish()
    patch_g.finish()
    dy_g.finish()
    for c in gains:
        c.wait_send()
    for c in rows_c:
        c.wait_recv()
        c.wait_send()
    g.sent()


def first_call(n_batch, text, patches, gain_tile, patch_tile, w_qkv, w_so, w_co, w_down, cot, valid):
    n_out = n_batch // 2
    dma = pltpu.SemaphoreType.DMA
    j, rows, columns = w_qkv.shape
    return pl.pallas_call(
        functools.partial(first_kernel, n_batch),
        out_shape=[
            jax.ShapeDtypeStruct((4,) + text.shape, BF),
            jax.ShapeDtypeStruct((4,) + patches.shape, BF),
            jax.ShapeDtypeStruct((n_batch,) + gain_tile.shape, BF),
            jax.ShapeDtypeStruct(patch_tile.shape, BF),
            jax.ShapeDtypeStruct((j, rows * n_batch, columns), BF),
            jax.ShapeDtypeStruct((4,) + cot.shape, BF),
        ]
        + [jax.ShapeDtypeStruct(w.shape[::-1], BF) for w in (w_so, w_co, w_down)],
        in_specs=[pl.BlockSpec(memory_space=pltpu.VMEM)] * 10,
        out_specs=[pl.BlockSpec(memory_space=pl.ANY)] * 6 + [pl.BlockSpec(memory_space=pltpu.VMEM)] * 3,
        scratch_shapes=[
            pltpu.VMEM(cot.shape, BF),
            pltpu.VMEM((4,) + gain_tile.shape, BF),
            pltpu.VMEM(gain_tile.shape, BF),
        ]
        + BatchGather.semaphores(n_out, 4)
        + [dma((5, 3)), dma((5, 3)), dma((5,))],
        compiler_params=pltpu.CompilerParams(collective_id=0, has_side_effects=True),
        cost_estimate=pl.CostEstimate(flops=10**6, bytes_accessed=300 * 10**6, transcendentals=0),
    )(text, patches, gain_tile, patch_tile, w_qkv, w_so, w_co, w_down, cot, valid)


def mm(a, b):
    return lax.dot_general(a, b, (((1,), (0,)), ((), ())), preferred_element_type=F32)


def mm_nt(a, b):
    return lax.dot_general(a, b, (((1,), (1,)), ((), ())), preferred_element_type=F32)


def mm_tn(a, b):
    return lax.dot_general(a, b, (((0,), (0,)), ((), ())), preferred_element_type=F32)


class Local:
    def __init__(self, sems):
        self.sems = sems
        self.used = 0

    def go(self, src, dst):
        copy = pltpu.make_async_copy(src, dst, self.sems.at[self.used])
        self.used += 1
        copy.start()
        return copy


STEP = 32


def each_rows(rows, body, step=STEP):
    def one(r, carry):
        body(pl.ds(pl.multiple_of(r * step, step), step))
        return carry

    lax.fori_loop(0, rows // step, one, 0)


def each(count, body, first=0):
    def one(k, carry):
        body(k)
        return carry

    lax.fori_loop(first, count, one, 0)


def cols(n, width):
    return pl.ds(pl.multiple_of(n * width, width), width)


def rms_of(values, gain):
    return values * lax.rsqrt(jnp.mean(values * values, axis=-1, keepdims=True) + 1e-06) * gain


def attend(q_ref, k_ref, v_ref, out_ref, lse_ref, j, allowed, heads):
    for h in range(heads):
        at = pl.ds(h * HD, HD)
        s = mm_nt(q_ref[j, :, at], k_ref[j, :, at]) * HD ** (-0.5)
        s = jnp.where(allowed, s, -1e30)
        top = jnp.max(s, axis=-1, keepdims=True)
        e = jnp.exp(s - top)
        total = jnp.sum(e, axis=-1, keepdims=True)
        probs = (e / total).astype(BF)
        out_ref[j, :, at] = mm(probs, v_ref[j, :, at]).astype(BF)
        lse_ref[j, :, pl.ds(h, 1)] = top + jnp.log(total)


def causal_ok(key_row, rows):
    shape = (rows, key_row.shape[1])
    return (lax.broadcasted_iota(jnp.int32, shape, 1) <= lax.broadcasted_iota(jnp.int32, shape, 0)) & (
        jnp.broadcast_to(key_row, shape) > 0.5
    )


class BranchSum:
    def __init__(self, place, bufs, send, recv, step=512):
        self.p = place
        self.step = step
        self.fs, self.ns, self.cf, self.yr, self.cn = bufs
        self.to_core = remote(self.fs, self.cf, send.at[0], recv.at[0], batch=place.b, mod=place.core)
        self.to_far = remote(self.fs, self.yr, send.at[1], recv.at[1], batch=place.b, mod=place.far)
        self.to_near = remote(self.ns, self.cn, send.at[2], recv.at[2], batch=place.b, mod=place.core)

    def send(self, part):
        self.send_core(part)
        self.send_far(part)

    def send_core(self, part):
        p, step = self.p, self.step
        n = self.fs.shape[1] // step

        def first(k):
            self.fs[:, cols(k, step)] = part(p.farcore, k).astype(BF)

        def second(k):
            self.ns[:, cols(k, step)] = part(p.core, k).astype(BF)

        each(n, first)
        self.to_core.start()
        each(n, second)
        self.to_near.start()

    def send_far(self, part):
        p, step = self.p, self.step
        n = self.fs.shape[1] // step

        def third(k):
            at = cols(k, step)
            self.fs[:, at] = (part(p.far, k) + self.cf[:, at].astype(F32)).astype(BF)

        self.to_core.wait()
        each(n, third)
        self.to_far.start()

    def receive(self):
        self.to_near.wait_recv()
        self.to_far.wait_recv()

    def others(self, rows, at=slice(None)):
        return self.cn[rows, at].astype(F32) + self.yr[rows, at].astype(F32)

    def sent(self):
        self.to_near.wait_send()
        self.to_far.wait_send()


def halves(shard, whole, rows):
    half = rows // 2

    def piece(k):
        return (shard.at[pl.ds(k * half, half)], lambda q: whole.at[pl.ds(q * rows + k * half, half)])

    return [piece(0), piece(1)]


STRIP = 256


def strip(shard, whole, rows, k):
    at = pl.ds(k * STRIP, STRIP)
    return (
        shard.at[:, at],
        lambda q: whole.at[pl.ds(q * rows, rows), at],
        lambda o: whole.at[pl.ds(o * 2 * rows, 2 * rows), at],
    )


def forward_kernel(n_batch, *refs):
    (text_all, patch_all, gains, patch_own, key_ok, cross_ok, qkv_w,
     w_so, w_ckv, w_cq, w_co, w_gu, w_down) = refs[:13]
    (so_all, patch_w, ckv_all, cq_all, co_all, gu_all, down_all, act1_o, act2_o, act3_o, qkv_o, cqkv_o,
     ctx_o, cctx_o, lse_o, clse_o, pp_o, x1_o, x2_o, gate_o, up_o, h_o) = refs[13:35]
    (act, x, wq, wo, wp, pat, pp, qkv, ctx, lse, fs, ns, cf, yr, cn, wg, gate, gate_b, up, hid,
     z_send, z_recv, x_send, x_recv, own, mod_send, mod_recv, sum_send, sum_recv, loc, wide_send, wide_recv, wide_own) = refs[35:]
    p = Place(n_batch)
    local = Local(loc)
    rows, width = x.shape
    heads = wq.shape[2] // HD
    cq_r, pr = w_cq.shape[0], patch_own.shape[0]
    g = BatchGather(
        p,
        [
            (w_so, lambda q: so_all.at[pl.ds(q * cq_r, cq_r)]),
            (patch_own, lambda q: patch_w.at[pl.ds(q * pr, pr)]),
            (w_ckv.at[0], lambda q: ckv_all.at[0, pl.ds(q * cq_r, cq_r)]),
            (w_ckv.at[1], lambda q: ckv_all.at[1, pl.ds(q * cq_r, cq_r)]),
            (w_cq, lambda q: cq_all.at[pl.ds(q * cq_r, cq_r)]),
            (w_co, lambda q: co_all.at[pl.ds(q * cq_r, cq_r)]),
        ]
        + halves(w_gu.at[0], gu_all.at[0], cq_r)
        + halves(w_gu.at[1], gu_all.at[1], cq_r),
        (z_send, z_recv, x_send, x_recv, own),
        [strip(w_down, down_all, cq_r, k) for k in range(w_down.shape[1] // STRIP)],
        (wide_send, wide_recv, wide_own),
    )
    SO, PATCH, CK, CV, CQ, CO, GATE, GATE2, UP, UP2 = range(10)
    load_act = local.go(text_all, act)
    load_q = local.go(qkv_w, wq)
    load_pat = local.go(patch_all, pat)
    p.greet()
    g.start()
    g.wide_start()
    bufs = (fs, ns, cf, yr, cn)
    one = BranchSum(p, bufs, sum_send.at[0], sum_recv.at[0])
    two = BranchSum(p, bufs, sum_send.at[1], sum_recv.at[1])
    act_block = lambda j: act.at[j]
    col_w = wq.shape[2]
    pp_g = ModGather(p, lambda j: pp.at[:, :, pl.ds(pl.multiple_of(j * col_w, col_w), col_w)], mod_send.at[0], mod_recv.at[0])
    a2_g = ModGather(p, act_block, mod_send.at[1], mod_recv.at[1])
    a3_g = ModGather(p, act_block, mod_send.at[2], mod_recv.at[2])

    load_act.wait()
    x[...] = act[p.m].astype(F32)

    def norm_one(j):
        def body(r):
            act[j, r, :] = rms_of(act[j, r, :].astype(F32), gains[pl.ds(0, 1), :]).astype(BF)

        each_rows(rows, body)

    each(4, norm_one)
    save_act = local.go(act, act1_o)
    load_q.wait()

    def project(j):
        for w in range(3):
            qkv[w, j] = mm(act[j], wq[w]).astype(BF)

    each(4, project)
    save_qkv = local.go(qkv, qkv_o)
    g.pump(SO)
    attend_one = lambda j: attend(qkv.at[0], qkv.at[1], qkv.at[2], ctx, lse, j, causal_ok(key_ok[j, pl.ds(0, 1), :], rows), heads)
    each(4, attend_one)
    save_ctx = local.go(ctx, ctx_o)
    save_lse = local.go(lse, lse_o)
    g.arrived(SO)
    load_o = local.go(so_all, wo)
    save_act.wait()
    save_qkv.wait()
    load_o.wait()
    part = lambda j, k: mm_nt(ctx[j], wo[cols(k, 512), :])
    one.send(part)

    def add_own(k):
        at = cols(k, 512)
        x[:, at] += part(p.m, k)

    each(width // 512, add_own)
    g.arrived(PATCH)
    if pr != cq_r:
        wp[...] = jnp.zeros(wp.shape, BF)
    for c in [local.go(patch_w.at[pl.ds(q * pr, pr)], wp.at[pl.ds(q * cq_r, pr)]) for q in range(n_batch)]:
        c.wait()
    load_pat.wait()
    own_cols = pl.ds(pl.multiple_of(p.m * col_w, col_w), col_w)

    def project_patch(j):
        pp[j, :, own_cols] = mm(pat[j], wp[...]).astype(BF)

    each(4, project_patch)
    pp_g.start()
    one.receive()

    def finish_one(r):
        x[r, :] += one.others(r)
        act[p.m, r, :] = rms_of(x[r, :], gains[pl.ds(1, 1), :]).astype(BF)

    each_rows(rows, finish_one)
    a2_g.start()
    save_x = local.go(x, x1_o)
    one.sent()
    g.pump(CV)
    pp_g.forward()
    g.pump(CQ)
    a2_g.forward()
    g.arrived(CK)
    load_ck = local.go(ckv_all.at[0], wq.at[1])
    pp_g.finish()
    save_pp = local.go(pp, pp_o)
    load_ck.wait()

    def project_pp(w):
        def body(j):
            qkv[w, j] = mm(pp[j], wq[w]).astype(BF)

        return body

    each(4, project_pp(1))
    g.arrived(CV)
    load_cv = local.go(ckv_all.at[1], wq.at[2])
    load_cv.wait()
    each(4, project_pp(2))
    g.arrived(CQ)
    load_cq = local.go(cq_all, wq.at[0])
    a2_g.finish()
    save_act = local.go(act, act2_o)
    load_cq.wait()

    def project_cq(j):
        qkv[0, j] = mm(act[j], wq[0]).astype(BF)

    each(4, project_cq)
    save_ctx.wait()
    save_lse.wait()
    save_qkv = local.go(qkv, cqkv_o)

    def attend_two(j):
        ok = jnp.broadcast_to(cross_ok[j, pl.ds(0, 1), :], (rows, cross_ok.shape[2])) > 0.5
        attend(qkv.at[0], qkv.at[1], qkv.at[2], ctx, lse, j, ok, heads)

    each(4, attend_two)
    save_ctx = local.go(ctx, cctx_o)
    save_lse = local.go(lse, clse_o)
    g.arrived(CO)
    load_o = local.go(co_all, wo)
    save_act.wait()
    save_x.wait()
    load_o.wait()
    two.send(part)
    each(width // 512, add_own)
    g.pump(GATE2)
    two.receive()

    def finish_two(r):
        x[r, :] += two.others(r)
        act[p.m, r, :] = rms_of(x[r, :], gains[pl.ds(2, 1), :]).astype(BF)

    each_rows(rows, finish_two)
    a3_g.start()
    save_x = local.go(x, x2_o)
    two.sent()
    g.pump(UP)
    a3_g.forward()
    a3_g.finish()
    save_act = local.go(act, act3_o)

    g.arrived(GATE)
    g.arrived(GATE2)
    load_g = local.go(gu_all.at[0], wg)
    load_g.wait()

    def gate_one(j):
        gate[j] = mm(act[j], wg[...])
        gate_b[j] = gate[j].astype(BF)

    each(4, gate_one)
    save_gate = local.go(gate_b, gate_o)
    g.arrived(UP)
    g.arrived(UP2)
    load_g = local.go(gu_all.at[1], wg)
    load_g.wait()

    def up_one(j):
        u = mm(act[j], wg[...])
        up[j] = u.astype(BF)
        hid[j] = (jax.nn.gelu(gate[j], approximate=True) * u).astype(BF)

    each(4, up_one)
    save_up = local.go(up, up_o)
    save_h = local.go(hid, h_o)
    g.sent()
    for c in (save_act, save_x, save_gate, save_up, save_h, save_ctx, save_lse, save_qkv, save_pp):
        c.wait()


def forward_call(n_batch, text_all, patch_all, gains, patch_own, key_ok, cross_ok, qkv_w,
                 w_so, w_ckv, w_cq, w_co, w_gu, w_down):
    n_out = n_batch // 2
    dma = pltpu.SemaphoreType.DMA
    items, rows, width = text_all.shape
    c, f = qkv_w.shape[2], w_gu.shape[2]
    patch_width = patch_all.shape[2]
    keys = patch_all.shape[1]
    sds = jax.ShapeDtypeStruct
    any_ = pl.BlockSpec(memory_space=pl.ANY)
    vmem = pl.BlockSpec(memory_space=pltpu.VMEM)
    big = (items, rows, width)
    return pl.pallas_call(
        functools.partial(forward_kernel, n_batch),
        out_shape=[
            sds((width, c), BF), sds((n_batch * patch_own.shape[0], c), BF), sds((2, width, c), BF), sds((width, c), BF),
            sds((width, c), BF), sds((2, width, f), BF), sds((width, f), BF),
            sds(big, BF), sds(big, BF), sds(big, BF),
            sds((3, items, rows, c), BF), sds((3, items, rows, c), BF),
            sds((items, rows, c), BF), sds((items, rows, c), BF),
            sds((items, rows, 128), F32), sds((items, rows, 128), F32),
            sds((items, keys, width), BF), sds((rows, width), F32), sds((rows, width), F32),
            sds((items, rows, f), BF), sds((items, rows, f), BF), sds((items, rows, f), BF),
        ],
        in_specs=[any_, any_, vmem, vmem, vmem, vmem, any_] + [vmem] * 6,
        out_specs=[any_] * 22,
        scratch_shapes=[
            pltpu.VMEM(big, BF), pltpu.VMEM((rows, width), F32), pltpu.VMEM((3, width, c), BF),
            pltpu.VMEM((width, c), BF), pltpu.VMEM((patch_width, c), BF), pltpu.VMEM((items, keys, patch_width), BF),
            pltpu.VMEM((items, keys, width), BF), pltpu.VMEM((3, items, rows, c), BF), pltpu.VMEM((items, rows, c), BF),
            pltpu.VMEM((items, rows, 128), F32),
        ]
        + [pltpu.VMEM((rows, width), BF)] * 5
        + [pltpu.VMEM((width, f), BF), pltpu.VMEM((items, rows, f), F32), pltpu.VMEM((items, rows, f), BF), pltpu.VMEM((items, rows, f), BF), pltpu.VMEM((items, rows, f), BF)]
        + BatchGather.semaphores(n_out, 10)
        + [dma((3, 3)), dma((3, 3)), dma((2, 3)), dma((2, 3)), dma((32 + n_batch,)),
           dma((f // STRIP, n_out + 1)), dma((f // STRIP, n_out)), dma((f // STRIP,))],
        compiler_params=pltpu.CompilerParams(collective_id=1, has_side_effects=True, vmem_limit_bytes=VMEM_LIMIT),
        cost_estimate=pl.CostEstimate(flops=35 * 10**9, bytes_accessed=600 * 10**6, transcendentals=0),
    )(text_all, patch_all, gains, patch_own, key_ok, cross_ok, qkv_w, w_so, w_ckv, w_cq, w_co, w_gu, w_down)


class Line:
    def z_copy(self, t, s):
        p = self.p
        return remote(self.block(t, (p.outer + s) % p.n_out), self.slot(t, s), self.z_send.at[t, s],
                      self.z_recv.at[t, s], batch=p.z_peer(s), mod=p.m)

    def to_relay(self, t):
        p = self.p
        return remote(self.block(t, p.opposite), self.slot(t, p.n_out), self.z_send.at[t, 0], self.z_recv.at[t, 0],
                      batch=p.relay * 2 + p.inner, mod=p.m)

    def to_end(self, t):
        p = self.p
        return remote(self.block(t, p.end), self.slot(t, p.outward), self.z_send.at[t, 0],
                      self.z_recv.at[t, p.outward], batch=p.end * 2 + p.inner, mod=p.m)

    def z_start(self, t):
        p = self.p
        if not self.line:
            for s in p.shifts:
                self.z_copy(t, s).start()
            return
        self.z_copy(t, 2).start()
        self.z_copy(t, p.inward).start()

        @pl.when(p.is_end)
        def _():
            self.to_relay(t).start()

    def z_relay(self, t):
        p = self.p
        if not self.line:
            return

        @pl.when(p.is_mid)
        def _():
            self.to_relay(t).wait_recv()
            a, b = self.views(t)
            self.fetch((self.block(t, p.end), a), (self.slot(t, p.n_out), b))
            self.add(a, b)
            self.fetch((a, self.block(t, p.end)))
            self.to_end(t).start()

    def fetch(self, *pairs):
        copies = [pltpu.make_async_copy(a, b, self.loc.at[k]) for k, (a, b) in enumerate(pairs)]
        for copy in copies:
            copy.start()
        for copy in copies:
            copy.wait()

    def add(self, a, *others):
        lead, rows, width = a.shape
        step = 16
        while rows % (2 * step) == 0 and step * width < 16384:
            step *= 2

        def body(o):
            def one(r):
                total = a[o, r, :].astype(F32)
                for b in others:
                    total = total + b[o, r, :].astype(F32)
                a[o, r, :] = total.astype(BF)

            each_rows(rows, one, step)

        each(lead, body)

    def z_arrived(self, t):
        p = self.p
        if not self.line:
            for s in p.shifts:
                self.z_copy(t, s).wait_recv()
            return
        self.z_copy(t, 2).wait_recv()
        self.z_copy(t, self.first_slot()).wait_recv()

        @pl.when(p.is_mid)
        def _():
            self.z_copy(t, 3).wait_recv()

    def first_slot(self):
        return 3 - 2 * ((self.p.outer + 2) // 3)

    def z_sent(self, t):
        p = self.p
        if not self.line:
            for s in p.shifts:
                self.z_copy(t, s).wait_send()
            return
        self.z_copy(t, 2).wait_send()
        self.z_copy(t, p.inward).wait_send()
        self.to_relay(t).wait_send()


class GradSum(Line):
    def __init__(self, place, pieces, mine, got, sems, loc):
        self.p = place
        self.pieces = pieces
        self.mine, self.got = mine, got
        self.x_send, self.x_recv, self.z_send, self.z_recv = sems
        self.loc = loc
        self.line = place.line
        self.ready = self.started = self.done = 0
        self.window = 2

    @staticmethod
    def semaphores(n_out, count):
        dma = pltpu.SemaphoreType.DMA
        return [dma((count,)), dma((count,)), dma((count, n_out)), dma((count, n_out))]

    def block(self, t, o):
        return self.pieces[t][1].at[pl.ds(o, 1)]

    def slot(self, t, s):
        return self.pieces[t][2].at[pl.ds(s, 1)]

    def views(self, t):
        _, rows, width = self.pieces[t][1].shape
        return [v.at[pl.ds(0, 1), pl.ds(0, rows), pl.ds(0, width)] for v in (self.mine, self.got)]

    def x_copy(self, t):
        whole, from_x, _ = self.pieces[t]
        return remote(whole.at[:, 1 - self.p.inner], from_x, self.x_send.at[t], self.x_recv.at[t],
                      batch=self.p.x_peer, mod=self.p.m)

    def kick(self):
        while self.started < self.ready and self.started - self.done < self.window:
            self.x_copy(self.started).start()
            self.started += 1

    def advance(self):
        self.ready += 1
        self.kick()

    def pump(self, count=1):
        for _ in range(min(count, self.ready - self.done)):
            t = self.done
            whole, from_x, from_z = self.pieces[t]
            n_out, rows, width = from_x.shape
            self.x_copy(t).wait_recv()
            self.done += 1
            self.kick()
            mine = self.mine.at[:, pl.ds(0, rows), pl.ds(0, width)]
            got = self.got.at[:, pl.ds(0, rows), pl.ds(0, width)]
            self.fetch((whole.at[:, self.p.inner], mine), (from_x, got))
            self.add(mine, got)
            self.fetch((mine, from_x), (mine.at[self.p.outer], from_z.at[0]))
            self.z_start(t)
            if t:
                self.z_relay(t - 1)

    def finish(self):
        last = len(self.pieces) - 1
        self.pump(len(self.pieces))
        self.z_relay(last)
        for t in range(len(self.pieces)):
            self.x_copy(t).wait_send()
            self.z_arrived(t)
            self.z_sent(t)


def attend_back(q_ref, k_ref, v_ref, do_ref, lse_ref, dq_ref, dk_ref, dv_ref, j, allowed, heads):
    scale = HD ** (-0.5)
    for h in range(heads):
        at = pl.ds(h * HD, HD)
        q, k, v, do = q_ref[j, :, at], k_ref[j, :, at], v_ref[j, :, at], do_ref[j, :, at]
        s = jnp.where(allowed, mm_nt(q, k) * scale, -1e30)
        probs = jnp.exp(s - lse_ref[j, :, pl.ds(h, 1)])
        dp = mm_nt(do, v)
        ds = (probs * (dp - jnp.sum(probs * dp, axis=-1, keepdims=True))).astype(BF)
        dv_ref[j, :, at] = mm_tn(probs.astype(BF), do).astype(BF)
        dq_ref[j, :, at] = (mm(ds, k) * scale).astype(BF)
        dk_ref[j, :, at] = (mm_tn(ds, q) * scale).astype(BF)


def gelu_parts(g):
    c = 0.7978845608028654
    t = jnp.tanh(c * (g + 0.044715 * g * g * g))
    half = 0.5 * (1.0 + t)
    return g * half, half + 0.5 * g * (1.0 - t * t) * c * (1.0 + 3 * 0.044715 * g * g)


def backward_kernel(n_batch, *refs):
    (dy_all, text, pat_all, gains, key_ok, cross_ok, qkv_w, so_all, ckv_all, cq_all, co_all, gu_all, down_all,
     act1, act2, act3, qkv_i, cqkv_i, ctx_i, cctx_i, lse_i, clse_i, pp_i, x1_i, x2_i, gate_i, up_i, h_i) = refs[:28]
    (result, d_text, gain_out, whole_f, from_x_f, from_z_f, whole_c, from_x_c, from_z_c,
     whole_p, from_x_p, from_z_p) = refs[28:40]
    (dy, act_a, act_b, gate, up, hid, w0, w1, qkv, dqkv, ctx, dctx, dpp, lse, g, da, v, fs, ns, cf, yr, cn,
     cf2, yr2, cn2, st, mine, got, dg, dgm, dgx, dgz,
     gx_send, gx_recv, gz_send, gz_recv, mod_send, mod_recv, sum_send, sum_recv, gain_send, gain_recv,
     gx, loc, loc2) = refs[40:]
    p = Place(n_batch)
    local = Local(loc)
    items, rows, width = dy.shape
    c, f = qkv_w.shape[2], gu_all.shape[2]
    half = f // 2
    n_out, blk = p.n_out, width // n_batch
    heads = c // HD
    pieces = [
        (whole_f.at[k], from_x_f.at[k], from_z_f.at[k // 2, :, :, pl.ds(k % 2 * half, half)]) for k in range(6)
    ]
    pieces += [(whole_c.at[k], from_x_c.at[k], from_z_c.at[k]) for k in range(8)]
    pieces.append((whole_p, from_x_p, from_z_p))
    gs = GradSum(p, pieces, mine, got, (gx_send, gx_recv, gz_send, gz_recv), loc2)
    left = pl.ds(0, c)
    right = pl.ds(c, c)

    load_dy = local.go(dy_all, dy)
    load_h = local.go(h_i, hid)
    load_w0 = local.go(down_all, w0)
    load_v = local.go(x2_i, v)
    load_gate = local.go(gate_i, gate)
    load_up = local.go(up_i, up)
    load_w1 = local.go(gu_all.at[0], w1)
    load_a = local.go(act3, act_a)
    load_b = local.go(act2, act_b)
    p.greet()
    set_a = (fs, ns, cf, yr, cn)
    set_b = (fs, ns, cf2, yr2, cn2)
    sums = [
        BranchSum(p, bufs, sum_send.at[k], sum_recv.at[k])
        for k, bufs in enumerate((set_b, set_a, set_a, set_b, set_a))
    ]
    gathers = [ModGather(p, lambda j: dy.at[j], mod_send.at[k], mod_recv.at[k]) for k in range(2)]
    dg[...] = jnp.zeros(dg.shape, F32)

    def piece(acts, grads, first, count):
        t = gs.ready
        whole = pieces[t][0]
        used = whole.shape[2]
        chunk = max(256, 2 * blk)
        per = chunk // (2 * blk)

        def body(n):
            a = acts[:, :, cols(n, chunk)].reshape(items * rows, chunk)
            b = grads[:, :, pl.ds(first, count)].reshape(items * rows, count)
            st[pl.ds(n * per, per), :, :, pl.ds(0, count)] = mm_tn(a, b).astype(BF).reshape(per, 2, blk, count)

        each(width // chunk, body)
        copy = pltpu.make_async_copy(st.at[:, :, pl.ds(0, used), pl.ds(0, count)], whole, loc2.at[2])
        copy.start()
        copy.wait()
        gs.advance()

    def norm_back(k, total, v_rows):
        def body(r):
            grad = da[r, :] + total.others(r)
            val = v_rows(r)
            factor = lax.rsqrt(jnp.mean(val * val, axis=-1, keepdims=True) + 1e-06)
            dg[pl.ds(k, 1), :] += jnp.sum(grad * val * factor, axis=0, keepdims=True)
            scaled = gains[pl.ds(k, 1), :] * grad
            back = factor * scaled - val * (factor * factor * factor * jnp.mean(scaled * val, axis=-1, keepdims=True))
            g[r, :] += back
            if k:
                dy[p.m, r, :] = g[r, :].astype(BF)

        each_rows(rows, body)

    load_dy.wait()
    load_h.wait()
    g[...] = dy[p.m].astype(F32)
    piece(dy, hid, 0, half)
    piece(dy, hid, half, half)
    load_w0.wait()
    load_gate.wait()
    load_up.wait()

    def mix_back(j):
        dh = mm(dy[j], w0[...])
        value, slope = gelu_parts(gate[j].astype(F32))
        gate[j] = (dh * up[j].astype(F32) * slope).astype(BF)
        up[j] = (dh * value).astype(BF)

    each(items, mix_back)
    load_w0 = local.go(gu_all.at[1], w0)
    load_w1.wait()
    load_w0.wait()
    act_part = lambda j, k: mm_nt(gate[j], w1[cols(k, 512), :]) + mm_nt(up[j], w0[cols(k, 512), :])
    sums[1].send(act_part)
    gs.pump()

    def own_part(part):
        def body(k):
            da[:, cols(k, 512)] = part(p.m, k)

        each(width // 512, body)

    own_part(act_part)
    load_w0 = [local.go(co_all, w0.at[:, left]), local.go(cq_all, w0.at[:, right])]
    load_w1 = [local.go(ckv_all.at[0], w1.at[:, left]), local.go(ckv_all.at[1], w1.at[:, right])]
    load_s = [local.go(cqkv_i, qkv), local.go(cctx_i, ctx), local.go(clse_i, lse)]
    load_a.wait()
    piece(act_a, gate, 0, half)
    piece(act_a, gate, half, half)
    piece(act_a, up, 0, half)
    gs.pump()
    load_v.wait()
    sums[1].receive()
    norm_back(2, sums[1], lambda r: v[r, :])
    gathers[0].start()
    sums[1].sent()
    load_v = local.go(x1_i, v)
    piece(act_a, up, half, half)
    load_a = local.go(pp_i, act_a)
    gs.pump()
    gathers[0].forward()
    gathers[0].finish()

    for copy in load_w0 + load_w1 + load_s:
        copy.wait()

    def ctx_back(j):
        dctx[j] = mm(dy[j], w0[:, left]).astype(BF)

    each(items, ctx_back)
    piece(dy, ctx, 0, c)

    def cross_back(j):
        ok = jnp.broadcast_to(cross_ok[j, pl.ds(0, 1), :], (rows, cross_ok.shape[2])) > 0.5
        attend_back(qkv.at[0], qkv.at[1], qkv.at[2], dctx, lse, dqkv.at[0], dqkv.at[1], dqkv.at[2], j, ok, heads)

    each(items, cross_back)
    query_part = lambda j, k: mm_nt(dqkv[0, j], w0[cols(k, 512), right])
    sums[2].send(query_part)
    gs.pump()
    own_part(query_part)
    load_w0 = [local.go(so_all, w0.at[:, left]), local.go(qkv_w.at[0], w0.at[:, right])]
    load_s = [local.go(qkv_i, qkv), local.go(ctx_i, ctx), local.go(lse_i, lse)]
    load_b.wait()
    piece(act_b, dqkv.at[0], 0, c)
    load_b = local.go(act1, act_b)
    load_a.wait()
    piece(act_a, dqkv.at[1], 0, c)
    piece(act_a, dqkv.at[2], 0, c)
    load_a = local.go(pat_all, act_a)
    load_v.wait()
    sums[2].receive()
    norm_back(1, sums[2], lambda r: v[r, :])
    gathers[1].start()
    sums[2].sent()
    load_v = local.go(x2_i, v)
    gs.pump()
    proj_part = lambda j, k: mm_nt(dqkv[1, k], w1[cols(j, c), left]) + mm_nt(dqkv[2, k], w1[cols(j, c), right])
    sums[3].send_core(proj_part)

    def proj_own(k):
        dpp[k] = proj_part(p.m, k).astype(BF)

    each(items, proj_own)
    gathers[1].forward()
    gathers[1].finish()
    sums[3].send_far(proj_part)
    load_w1 = [local.go(qkv_w.at[1], w1.at[:, left]), local.go(qkv_w.at[2], w1.at[:, right])]

    for copy in load_w0 + load_s:
        copy.wait()
    each(items, ctx_back)
    piece(dy, ctx, 0, c)
    gs.pump()

    def self_back(j):
        ok = causal_ok(key_ok[j, pl.ds(0, 1), :], rows)
        attend_back(qkv.at[0], qkv.at[1], qkv.at[2], dctx, lse, dqkv.at[0], dqkv.at[1], dqkv.at[2], j, ok, heads)

    each(items, self_back)
    load_b.wait()
    for k in range(3):
        piece(act_b, dqkv.at[k], 0, c)
    gs.pump()
    sums[3].receive()

    def proj_done(k):
        every = pl.ds(0, rows)
        dpp[k] = (dpp[k].astype(F32) + sums[3].others(every, cols(k, c))).astype(BF)

    each(items, proj_done)
    sums[3].sent()
    for copy in load_w1:
        copy.wait()
    self_part = lambda j, k: (
        mm_nt(dqkv[0, j], w0[cols(k, 512), right])
        + mm_nt(dqkv[1, j], w1[cols(k, 512), left])
        + mm_nt(dqkv[2, j], w1[cols(k, 512), right])
    )
    sums[4].send(self_part)
    own_part(self_part)
    load_w0 = local.go(down_all, w0)
    gs.pump()
    load_a.wait()
    piece(act_a, dpp, 0, c)
    gs.pump()
    sums[4].receive()
    norm_back(0, sums[4], lambda r: text[r, :].astype(F32))
    save_text = local.go(g, d_text)
    sums[4].sent()

    mod_g = [
        remote(dg, dgm.at[k], gain_send.at[k], gain_recv.at[k], batch=p.b, mod=j)
        for k, j in enumerate((p.core, p.far, p.farcore))
    ]
    for copy in mod_g:
        copy.start()
    load_w0.wait()
    out_part = lambda j, k: mm_nt(hid[j], w0[cols(k, 512), :])
    sums[0].send(out_part)
    gs.pump()
    load_v.wait()

    def result_own(k):
        at = cols(k, 512)
        da[:, at] = v[:, at] + out_part(p.m, k)

    each(width // 512, result_own)
    for copy in mod_g:
        copy.wait()
    dg[...] += dgm[0] + dgm[1] + dgm[2]
    across = remote(dg, dgx, gx.at[0], gx.at[1], batch=p.x_peer, mod=p.m)
    across.start()
    gs.pump()
    sums[0].receive()

    def result_done(r):
        da[r, :] += sums[0].others(r)

    each_rows(rows, result_done)
    save_result = local.go(da, result)
    sums[0].sent()
    across.wait()
    dg[...] += dgx[...]
    along = [
        remote(dg, dgz.at[s], gain_send.at[3 + s], gain_recv.at[3 + s], batch=p.z_peer(s), mod=p.m)
        for s in p.shifts
    ]
    for copy in along:
        copy.start()
    gs.pump()
    for copy in along:
        copy.wait()
    total = dg[...]
    for s in p.shifts:
        total = total + dgz[s]
    gain_out[...] = total
    gs.finish()
    save_result.wait()
    save_text.wait()


def backward_call(n_batch, inputs, patch_rows):
    n_out = n_batch // 2
    dma = pltpu.SemaphoreType.DMA
    sds = jax.ShapeDtypeStruct
    items, rows, width = inputs[0].shape
    c, f = inputs[6].shape[2], inputs[11].shape[2]
    blk = width // n_batch
    any_ = pl.BlockSpec(memory_space=pl.ANY)
    vmem = pl.BlockSpec(memory_space=pltpu.VMEM)
    big = (items, rows, width)
    heads_shape = (items, rows, c)
    V = lambda shape, dtype=BF: pltpu.VMEM(shape, dtype)

    def bufs(count, r, w):
        lead = (count,) if count else ()
        return [sds(lead + (n_out, 2, r, w), BF), sds(lead + (n_out, r, w), BF), sds(lead + (n_out + 1, r, w), BF)]

    return pl.pallas_call(
        functools.partial(backward_kernel, n_batch),
        out_shape=[sds((rows, width), F32), sds((rows, width), F32), sds((8, width), F32)]
        + bufs(6, blk, f // 2)[:2] + [sds((3, n_out + 1, blk, f), BF)] + bufs(8, blk, c) + bufs(0, patch_rows, c),
        in_specs=[any_, vmem, any_, vmem, vmem, vmem] + [any_] * 22,
        out_specs=[any_, any_, vmem] + [any_] * 9,
        scratch_shapes=[V(big)] * 3
        + [V((items, rows, f))] * 3
        + [V((width, f))] * 2
        + [V((3,) + heads_shape)] * 2
        + [V(heads_shape)] * 3
        + [V((items, rows, 128), F32)]
        + [V((rows, width), F32)] * 3
        + [V((rows, width))] * 8
        + [V((n_out, 2, blk, f // 2)), V((n_out, blk, f // 2)), V((n_out, blk, f // 2))]
        + [V((8, width), F32), V((3, 8, width), F32), V((8, width), F32), V((n_out, 8, width), F32)]
        + GradSum.semaphores(n_out, 15)
        + [dma((2, 3)), dma((2, 3)), dma((5, 3)), dma((5, 3)), dma((3 + n_out,)), dma((3 + n_out,)), dma((2,)),
           dma((48,)), dma((4,))],
        compiler_params=pltpu.CompilerParams(collective_id=2, has_side_effects=True, vmem_limit_bytes=VMEM_LIMIT),
        cost_estimate=pl.CostEstimate(flops=75 * 10**9, bytes_accessed=800 * 10**6, transcendentals=0),
    )(*inputs)


def local(n_batch, n_mod, text, patches, text_lengths, patch_mask, cotangent, gains,
          w_qkv, w_so, w_cq, w_ckv, w_co, w_patch, w_gu, w_down):
    own_items, text_rows, width = text.shape
    mod = lax.axis_index("mod")
    nb = n_batch
    blk = width // nb
    positions = jnp.arange(text_rows)

    gw = blk // n_mod
    gain_tile = lax.dynamic_update_slice(jnp.zeros((16, blk), BF), gains, (0, mod * gw))
    col_w = width // n_mod
    pr = w_patch.shape[0]
    pr_pad = -(-pr // 16) * 16
    patch_tile = jnp.pad(w_patch, ((0, pr_pad - pr), (0, 0))).reshape(pr_pad, n_mod, col_w)
    patch_tile = jnp.transpose(patch_tile, (1, 0, 2))
    block, block_pad = n_mod * pr, -(-n_mod * pr // 16) * 16
    patch_in = jnp.pad(patches[0].reshape(-1, nb, block), ((0, 0), (0, 0), (0, blk - block))).reshape(-1, width)
    own_length = lax.dynamic_slice_in_dim(text_lengths, mod * own_items, own_items)
    valid = jnp.broadcast_to((positions[:, None] < own_length).astype(F32), (text_rows, 128))
    text_all, patch_all, gain_raw, patch_rows, self_qkv, dy_all, so_t, co_t, down_t = first_call(
        n_batch, text[0], patch_in, gain_tile, patch_tile, w_qkv, w_so, w_co, w_down, cotangent[0], valid
    )
    gain_all = jnp.transpose(gain_raw[:, :8], (1, 0, 2)).reshape(8, width).astype(F32)
    patch_own = patch_rows[:, :pr].reshape(block, col_w)
    patch_own = jnp.pad(patch_own, ((0, block_pad - block), (0, 0)))
    row_ok = (positions[None, :] < text_lengths[:, None]).astype(F32)
    key_ok = jnp.broadcast_to(row_ok[:, None, :], (n_mod, 8, text_rows))
    cross_ok = jnp.broadcast_to((patch_mask > 0).astype(F32)[:, None, :], (n_mod, 8, patch_mask.shape[1]))
    (so_all, _, ckv_all, cq_all, co_all, gu_all, down_all, act1, act2, act3, qkv, cqkv,
     ctx, cctx, lse, clse, pp, x1, x2, gate, up, hid) = forward_call(
        n_batch, text_all, patch_all, gain_all, patch_own, key_ok, cross_ok, self_qkv,
        so_t, w_ckv, w_cq, co_t, w_gu, down_t)
    outs = backward_call(
        n_batch,
        (dy_all, text[0], patch_all, gain_all, key_ok, cross_ok, self_qkv, so_all, ckv_all, cq_all, co_all, gu_all,
         down_all, act1, act2, act3, qkv, cqkv, ctx, cctx, lse, clse, pp, x1, x2, gate, up, hid),
        block_pad,
    )
    result, d_text, gain_sum = outs[:3]
    sum_f, sum_c, sum_p = outs[5], outs[8], outs[11]
    at = lax.axis_index("batch") * blk + mod * gw
    d_gains = lax.dynamic_slice(gain_sum, (0, at), (3, gw))

    n_out = nb // 2
    outer = lax.axis_index("batch") // 2
    slots = jnp.arange(n_out)
    missing = (((outer == 0) & (slots == 1)) | ((outer == 3) & (slots == 3))) & (n_out == 4)

    def total(parts, axis=0):
        parts = lax.slice_in_dim(parts, 0, n_out, axis=axis)
        gone = missing.reshape((1,) * axis + (n_out,) + (1,) * (parts.ndim - axis - 1))
        return jnp.sum(jnp.where(gone, 0.0, parts.astype(F32)), axis=axis)

    grad_patch = total(sum_p)[:block].reshape(n_mod, pr, col_w)
    grad_patch = lax.all_to_all(grad_patch, "mod", 0, 0, tiled=True)
    grad_patch = jnp.transpose(grad_patch, (1, 0, 2)).reshape(pr, width)
    return (
        result[None],
        d_text[None],
        d_gains,
        total(sum_c[5:8], 1),
        total(sum_c[4]).T,
        total(sum_c[1]),
        total(sum_c[2:4], 1),
        total(sum_c[0]).T,
        grad_patch,
        total(sum_f[1:], 1),
        total(sum_f[0]).T,
    )


def solution(mesh):
    placed = (
        P(("batch", "mod"), None, None),
        P(("batch", "mod"), None, None),
        P("batch"),
        P("batch", None),
        P(("batch", "mod"), None, None),
        P(None, ("batch", "mod")),
        P(None, "batch", "mod"),
        P("mod", "batch"),
        P("batch", "mod"),
        P(None, "batch", "mod"),
        P("mod", "batch"),
        P(("batch", "mod"), None),
        P(None, "batch", "mod"),
        P("mod", "batch"),
    )

    def run(*args):
        return local(mesh.shape["batch"], mesh.shape["mod"], *args)

    return jax.shard_map(
        run,
        mesh=mesh,
        in_specs=placed,
        out_specs=(
            P(("batch", "mod"), None, None),
            P(("batch", "mod"), None, None),
            P(None, ("batch", "mod")),
            P(None, "batch", "mod"),
            P("mod", "batch"),
            P("batch", "mod"),
            P(None, "batch", "mod"),
            P("mod", "batch"),
            P(("batch", "mod"), None),
            P(None, "batch", "mod"),
            P("mod", "batch"),
        ),
        check_vma=False,
    )
```

```python
import functools

import jax
import jax.numpy as jnp
from jax import lax
from jax.experimental import pallas as pl
from jax.experimental.pallas import tpu as pltpu
from jax.sharding import PartitionSpec as P

HD = 128
F32 = jnp.float32
BF = jnp.bfloat16


VMEM_LIMIT = 62 * 2**20
MESH = pl.DeviceIdType.MESH


class Place:
    def __init__(self, n_batch):
        self.n_batch = n_batch
        self.n_out = n_batch // 2
        self.b = lax.axis_index("batch")
        self.m = lax.axis_index("mod")
        self.outer = self.b // 2
        self.inner = self.b % 2
        self.core = self.m + 1 - 2 * (self.m % 2)
        self.far = (self.m + 2) % 4
        self.farcore = (self.core + 2) % 4
        self.x_peer = self.b + 1 - 2 * self.inner
        self.line = self.n_out == 4
        self.shifts = [2, 1, 3] if self.line else list(range(1, self.n_out))
        self.is_mid = (self.outer + 1) // 2 == 1
        self.is_end = (self.outer + 1) // 2 != 1
        self.inward = 1 + 2 * (self.outer // 2)
        self.outward = 3 - 2 * (self.outer // 2)
        self.end = 3 * (self.outer // 2)
        self.relay = 2 - self.outer // 3
        self.opposite = 3 - self.outer

    def z_peer(self, s):
        return (self.outer + s) % self.n_out * 2 + self.inner

    def z_from(self, s):
        return (self.outer - s + self.n_out) % self.n_out * 2 + self.inner

    def greet(self):
        barrier = pltpu.get_barrier_semaphore()
        ids = [{"batch": self.z_peer(s), "mod": self.m} for s in self.shifts]
        ids.append({"batch": self.x_peer, "mod": self.m})
        for j in (self.core, self.far, self.farcore):
            ids.append({"batch": self.b, "mod": j})
        for device in ids:
            pl.semaphore_signal(barrier, inc=1, device_id=device, device_id_type=MESH)
        pl.semaphore_wait(barrier, len(ids))


def remote(src, dst, send, recv, **device):
    return pltpu.make_async_remote_copy(
        src_ref=src, dst_ref=dst, send_sem=send, recv_sem=recv, device_id=device, device_id_type=MESH
    )


class BatchGather:
    def __init__(self, place, tensors, sems, wides=(), wide_sems=None, early=()):
        self.p = place
        self.tensors = tensors
        self.z_send, self.z_recv, self.x_send, self.x_recv, self.own = sems
        self.started = 0
        self.early = early
        self.events = [(t, s) for t in range(len(tensors)) for s in [0] + place.shifts if s or t not in early]
        self.at = 0
        self.wides = wides
        self.wide_sems = wide_sems
        self.steps = [step for c in range(len(wides)) for step in ((self.wide_z, c), (self.wide_relay, c))]

    @staticmethod
    def semaphores(n_out, count):
        dma = pltpu.SemaphoreType.DMA
        return [dma((count, n_out)) for _ in range(4)] + [dma((count,))]

    def z_copy(self, t, s):
        src, block = self.tensors[t]
        return remote(src, block(self.p.b), self.z_send.at[t, s], self.z_recv.at[t, s],
                      batch=self.p.z_peer(s), mod=self.p.m)

    def z_relay(self, t):
        where = self.tensors[t][1]((self.p.outer + 2) % 4 * 2 + self.p.inner)
        return remote(where, where, self.z_send.at[t, 0], self.z_recv.at[t, self.p.inward],
                      batch=self.p.end * 2 + self.p.inner, mod=self.p.m)

    def own_copy(self, t):
        src, block = self.tensors[t]
        return pltpu.make_async_copy(src, block(self.p.b), self.own.at[t])

    def x_copy(self, t, s):
        src, block = self.tensors[t]
        where = block(self.p.z_from(s))
        return remote(src if s == 0 else where, where, self.x_send.at[t, s], self.x_recv.at[t, s],
                      batch=self.p.x_peer, mod=self.p.m)

    def straight(self, copy, act):
        p = self.p
        if not p.line:
            for s in p.shifts:
                act(copy(s))
            return
        act(copy(2))
        act(copy(p.inward))

        @pl.when(p.is_mid)
        def _():
            act(copy(p.outward))

    def start(self, count=1):
        for t in range(self.started, min(self.started + count, len(self.tensors))):
            self.straight(lambda s: self.z_copy(t, s), lambda c: c.start())
            self.own_copy(t).start()
            self.started = t + 1

    def pump(self, upto):
        p = self.p
        while self.at < len(self.events) and self.events[self.at][0] <= upto:
            t, s = self.events[self.at]
            if s:
                self.z_copy(t, s).wait_recv()
                if p.line and s == 2:

                    @pl.when(p.is_mid)
                    def _():
                        self.z_relay(t).start()

                if s == p.shifts[-1]:
                    self.start()
            self.x_copy(t, s).start()
            self.at += 1
            if s == p.shifts[-1] and self.steps:
                step, c = self.steps.pop(0)
                step(c)

    def arrived(self, t, ahead=1):
        self.pump(t + ahead)
        self.own_copy(t).wait()
        for s in [0] + self.p.shifts:
            self.x_copy(t, s).wait_recv()

    def wide_own(self, c):
        shard, block, _ = self.wides[c]
        return pltpu.make_async_copy(shard, block(self.p.b), self.wide_sems[2].at[c])

    def wide_x(self, c):
        shard, block, _ = self.wides[c]
        return remote(shard, block(self.p.b), self.wide_sems[0].at[c, 0], self.wide_sems[1].at[c, 0],
                      batch=self.p.x_peer, mod=self.p.m)

    def wide_copy(self, c, s):
        pair = self.wides[c][2](self.p.outer)
        return remote(pair, pair, self.wide_sems[0].at[c, s], self.wide_sems[1].at[c, s],
                      batch=self.p.z_peer(s), mod=self.p.m)

    def wide_on(self, c):
        pair = self.wides[c][2]((self.p.outer + 2) % 4)
        return remote(pair, pair, self.wide_sems[0].at[c, self.p.n_out], self.wide_sems[1].at[c, self.p.inward],
                      batch=self.p.end * 2 + self.p.inner, mod=self.p.m)

    def early_start(self):
        for t in self.early:
            self.x_copy(t, 0).start()

    def wide_start(self):
        for c in range(len(self.wides)):
            self.wide_own(c).start()
            self.wide_x(c).start()

    def wide_z(self, c):
        self.wide_own(c).wait()
        self.wide_x(c).wait_recv()
        self.straight(lambda s: self.wide_copy(c, s), lambda d: d.start())

    def wide_relay(self, c):
        if self.p.line:
            self.wide_copy(c, 2).wait_recv()

            @pl.when(self.p.is_mid)
            def _():
                self.wide_on(c).start()

    def sent(self):
        p = self.p
        for step, c in self.steps:
            step(c)
        for t in range(len(self.tensors)):
            self.straight(lambda s: self.z_copy(t, s), lambda c: c.wait_send())
            for s in [0] + p.shifts:
                self.x_copy(t, s).wait_send()
        for c in range(len(self.wides)):
            self.wide_x(c).wait_send()
            self.straight(lambda s: self.wide_copy(c, s), lambda d: d.wait_send())
            for s in p.shifts[1:] if p.line else p.shifts:
                self.wide_copy(c, s).wait_recv()
        if p.line:

            @pl.when(p.is_mid)
            def _():
                for t in range(len(self.tensors)):
                    self.z_relay(t).wait_send()
                for c in range(len(self.wides)):
                    self.wide_on(c).wait_send()


class ModGather:
    def __init__(self, place, block, send, recv):
        self.p = place
        self.block = block
        mine = block(place.m)
        far = block(place.far)
        self.near = remote(mine, mine, send.at[0], recv.at[0], batch=place.b, mod=place.core)
        self.across = remote(mine, mine, send.at[1], recv.at[1], batch=place.b, mod=place.far)
        self.on = remote(far, far, send.at[2], recv.at[2], batch=place.b, mod=place.core)

    def start(self):
        self.across.start()
        self.near.start()

    def forward(self):
        self.across.wait_recv()
        self.on.start()

    def finish(self):
        self.near.wait_recv()
        self.on.wait_recv()
        self.near.wait_send()
        self.across.wait_send()
        self.on.wait_send()


def first_kernel(n_batch, text, patches, gain_tile, patch_tile, w_qkv, w_so, w_co, w_down, cot, valid,
                 text_all, patch_all, gain_all, patch_rows, qkv_all, dy_all, so_t, co_t, down_t,
                 dy, gain_mod, gain_sum, z_send, z_recv, x_send, x_recv, own, mod_send, mod_recv, misc):
    p = Place(n_batch)
    rows = w_qkv.shape[1]
    tensors = [
        (w_qkv.at[0], lambda q: qkv_all.at[0, pl.ds(q * rows, rows)]),
        (w_qkv.at[1], lambda q: qkv_all.at[1, pl.ds(q * rows, rows)]),
        (gain_sum, lambda q: gain_all.at[q]),
        (w_qkv.at[2], lambda q: qkv_all.at[2, pl.ds(q * rows, rows)]),
    ]
    g = BatchGather(p, tensors, (z_send, z_recv, x_send, x_recv, own), early=(0, 1, 3))
    copies = [
        pltpu.make_async_copy(text, text_all.at[p.m], misc.at[0]),
        pltpu.make_async_copy(patches, patch_all.at[p.m], misc.at[1]),
        pltpu.make_async_copy(gain_tile, gain_mod.at[p.m], misc.at[2]),
        pltpu.make_async_copy(patch_tile.at[p.m], patch_rows.at[p.m], misc.at[3]),
        pltpu.make_async_copy(dy, dy_all.at[p.m], misc.at[4]),
    ]

    def mask_rows(r):
        dy[r, :] = (cot[r, :].astype(F32) * valid[r, pl.ds(0, 1)]).astype(BF)

    each_rows(dy.shape[0], mask_rows)
    for c in copies:
        c.start()
    p.greet()
    gains = [
        remote(gain_tile, gain_mod.at[p.m], mod_send.at[2, k], mod_recv.at[2, k], batch=p.b, mod=j)
        for k, j in enumerate((p.core, p.far, p.farcore))
    ]
    for c in gains:
        c.start()
    g.start()
    g.early_start()
    for c in copies:
        c.wait()
    text_g = ModGather(p, lambda j: text_all.at[j], mod_send.at[0], mod_recv.at[0])
    patch_g = ModGather(p, lambda j: patch_all.at[j], mod_send.at[1], mod_recv.at[1])
    dy_g = ModGather(p, lambda j: dy_all.at[j], mod_send.at[4], mod_recv.at[4])
    text_g.start()
    rows_c = [
        remote(patch_tile.at[j], patch_rows.at[p.m], mod_send.at[3, k], mod_recv.at[3, k], batch=p.b, mod=j)
        for k, j in enumerate((p.core, p.far, p.farcore))
    ]
    for c in rows_c:
        c.start()
    patch_g.start()
    for c in gains:
        c.wait_recv()
    gain_sum[...] = gain_mod[0] + gain_mod[1] + gain_mod[2] + gain_mod[3]
    so_t[...] = w_so[...].T
    co_t[...] = w_co[...].T
    down_t[...] = w_down[...].T
    dy_g.start()
    g.pump(3)
    text_g.forward()
    patch_g.forward()
    dy_g.forward()
    for t in range(4):
        g.arrived(t)
    text_g.finish()
    patch_g.finish()
    dy_g.finish()
    for c in gains:
        c.wait_send()
    for c in rows_c:
        c.wait_recv()
        c.wait_send()
    g.sent()


def first_call(n_batch, text, patches, gain_tile, patch_tile, w_qkv, w_so, w_co, w_down, cot, valid):
    n_out = n_batch // 2
    dma = pltpu.SemaphoreType.DMA
    j, rows, columns = w_qkv.shape
    return pl.pallas_call(
        functools.partial(first_kernel, n_batch),
        out_shape=[
            jax.ShapeDtypeStruct((4,) + text.shape, BF),
            jax.ShapeDtypeStruct((4,) + patches.shape, BF),
            jax.ShapeDtypeStruct((n_batch,) + gain_tile.shape, BF),
            jax.ShapeDtypeStruct(patch_tile.shape, BF),
            jax.ShapeDtypeStruct((j, rows * n_batch, columns), BF),
            jax.ShapeDtypeStruct((4,) + cot.shape, BF),
        ]
        + [jax.ShapeDtypeStruct(w.shape[::-1], BF) for w in (w_so, w_co, w_down)],
        in_specs=[pl.BlockSpec(memory_space=pltpu.VMEM)] * 10,
        out_specs=[pl.BlockSpec(memory_space=pl.ANY)] * 6 + [pl.BlockSpec(memory_space=pltpu.VMEM)] * 3,
        scratch_shapes=[
            pltpu.VMEM(cot.shape, BF),
            pltpu.VMEM((4,) + gain_tile.shape, BF),
            pltpu.VMEM(gain_tile.shape, BF),
        ]
        + BatchGather.semaphores(n_out, 4)
        + [dma((5, 3)), dma((5, 3)), dma((5,))],
        compiler_params=pltpu.CompilerParams(collective_id=0, has_side_effects=True),
        cost_estimate=pl.CostEstimate(flops=10**6, bytes_accessed=300 * 10**6, transcendentals=0),
    )(text, patches, gain_tile, patch_tile, w_qkv, w_so, w_co, w_down, cot, valid)


def mm(a, b):
    return lax.dot_general(a, b, (((1,), (0,)), ((), ())), preferred_element_type=F32)


def mm_nt(a, b):
    return lax.dot_general(a, b, (((1,), (1,)), ((), ())), preferred_element_type=F32)


def mm_tn(a, b):
    return lax.dot_general(a, b, (((0,), (0,)), ((), ())), preferred_element_type=F32)


class Local:
    def __init__(self, sems):
        self.sems = sems
        self.used = 0

    def go(self, src, dst):
        copy = pltpu.make_async_copy(src, dst, self.sems.at[self.used])
        self.used += 1
        copy.start()
        return copy


STEP = 32


def each_rows(rows, body, step=STEP):
    def one(r, carry):
        body(pl.ds(pl.multiple_of(r * step, step), step))
        return carry

    lax.fori_loop(0, rows // step, one, 0)


def each(count, body, first=0):
    def one(k, carry):
        body(k)
        return carry

    lax.fori_loop(first, count, one, 0)


def cols(n, width):
    return pl.ds(pl.multiple_of(n * width, width), width)


def rms_of(values, gain):
    return values * lax.rsqrt(jnp.mean(values * values, axis=-1, keepdims=True) + 1e-06) * gain


def attend(q_ref, k_ref, v_ref, out_ref, lse_ref, j, allowed, heads):
    for h in range(heads):
        at = pl.ds(h * HD, HD)
        s = mm_nt(q_ref[j, :, at], k_ref[j, :, at]) * HD ** (-0.5)
        s = jnp.where(allowed, s, -1e30)
        top = jnp.max(s, axis=-1, keepdims=True)
        e = jnp.exp(s - top)
        total = jnp.sum(e, axis=-1, keepdims=True)
        probs = (e / total).astype(BF)
        out_ref[j, :, at] = mm(probs, v_ref[j, :, at]).astype(BF)
        lse_ref[j, :, pl.ds(h, 1)] = top + jnp.log(total)


def causal_ok(key_row, rows):
    shape = (rows, key_row.shape[1])
    return (lax.broadcasted_iota(jnp.int32, shape, 1) <= lax.broadcasted_iota(jnp.int32, shape, 0)) & (
        jnp.broadcast_to(key_row, shape) > 0.5
    )


class BranchSum:
    def __init__(self, place, bufs, send, recv, step=512):
        self.p = place
        self.step = step
        self.fs, self.ns, self.cf, self.yr, self.cn = bufs
        self.to_core = remote(self.fs, self.cf, send.at[0], recv.at[0], batch=place.b, mod=place.core)
        self.to_far = remote(self.fs, self.yr, send.at[1], recv.at[1], batch=place.b, mod=place.far)
        self.to_near = remote(self.ns, self.cn, send.at[2], recv.at[2], batch=place.b, mod=place.core)

    def send(self, part):
        self.send_core(part)
        self.send_far(part)

    def send_core(self, part):
        p, step = self.p, self.step
        n = self.fs.shape[1] // step

        def first(k):
            self.fs[:, cols(k, step)] = part(p.farcore, k).astype(BF)

        def second(k):
            self.ns[:, cols(k, step)] = part(p.core, k).astype(BF)

        each(n, first)
        self.to_core.start()
        each(n, second)
        self.to_near.start()

    def send_far(self, part):
        p, step = self.p, self.step
        n = self.fs.shape[1] // step

        def third(k):
            at = cols(k, step)
            self.fs[:, at] = (part(p.far, k) + self.cf[:, at].astype(F32)).astype(BF)

        self.to_core.wait()
        each(n, third)
        self.to_far.start()

    def receive(self):
        self.to_near.wait_recv()
        self.to_far.wait_recv()

    def others(self, rows, at=slice(None)):
        return self.cn[rows, at].astype(F32) + self.yr[rows, at].astype(F32)

    def sent(self):
        self.to_near.wait_send()
        self.to_far.wait_send()


def halves(shard, whole, rows):
    half = shard.shape[1] // 2

    def piece(k):
        at = pl.ds(k * half, half)
        return (shard.at[:, at], lambda q: whole.at[pl.ds(q * rows, rows), at])

    return [piece(0), piece(1)]


STRIP = 256


def strip(shard, whole, rows, k):
    at = pl.ds(k * STRIP, STRIP)
    return (
        shard.at[:, at],
        lambda q: whole.at[pl.ds(q * rows, rows), at],
        lambda o: whole.at[pl.ds(o * 2 * rows, 2 * rows), at],
    )


def forward_kernel(n_batch, *refs):
    (text_all, patch_all, gains, patch_own, key_ok, cross_ok, qkv_w,
     w_so, w_ckv, w_cq, w_co, w_gu, w_down) = refs[:13]
    (so_all, patch_w, ckv_all, cq_all, co_all, gu_all, down_all, act1_o, act2_o, act3_o, qkv_o, cqkv_o,
     ctx_o, cctx_o, lse_o, clse_o, pp_o, x1_o, x2_o, gate_o, up_o, h_o) = refs[13:35]
    (act, x, wq, wo, wp, pat, pp, qkv, ctx, lse, fs, ns, cf, yr, cn, wg, gate, gate_b, up, hid,
     z_send, z_recv, x_send, x_recv, own, mod_send, mod_recv, sum_send, sum_recv, loc, wide_send, wide_recv, wide_own) = refs[35:]
    p = Place(n_batch)
    local = Local(loc)
    rows, width = x.shape
    heads = wq.shape[2] // HD
    cq_r, pr = w_cq.shape[0], patch_own.shape[0]
    g = BatchGather(
        p,
        [
            (w_so, lambda q: so_all.at[pl.ds(q * cq_r, cq_r)]),
            (patch_own, lambda q: patch_w.at[pl.ds(q * pr, pr)]),
            (w_ckv.at[0], lambda q: ckv_all.at[0, pl.ds(q * cq_r, cq_r)]),
            (w_ckv.at[1], lambda q: ckv_all.at[1, pl.ds(q * cq_r, cq_r)]),
            (w_cq, lambda q: cq_all.at[pl.ds(q * cq_r, cq_r)]),
            (w_co, lambda q: co_all.at[pl.ds(q * cq_r, cq_r)]),
        ]
        + halves(w_gu.at[0], gu_all.at[0], cq_r)
        + halves(w_gu.at[1], gu_all.at[1], cq_r),
        (z_send, z_recv, x_send, x_recv, own),
        [strip(w_down, down_all, cq_r, k) for k in range(w_down.shape[1] // STRIP)],
        (wide_send, wide_recv, wide_own),
    )
    SO, PATCH, CK, CV, CQ, CO, GATE, GATE2, UP, UP2 = range(10)
    load_act = local.go(text_all, act)
    load_q = local.go(qkv_w, wq)
    load_pat = local.go(patch_all, pat)
    p.greet()
    g.start()
    g.wide_start()
    bufs = (fs, ns, cf, yr, cn)
    one = BranchSum(p, bufs, sum_send.at[0], sum_recv.at[0])
    two = BranchSum(p, bufs, sum_send.at[1], sum_recv.at[1])
    act_block = lambda j: act.at[j]
    col_w = wq.shape[2]
    pp_g = ModGather(p, lambda j: pp.at[:, :, pl.ds(pl.multiple_of(j * col_w, col_w), col_w)], mod_send.at[0], mod_recv.at[0])
    a2_g = ModGather(p, act_block, mod_send.at[1], mod_recv.at[1])
    a3_g = ModGather(p, act_block, mod_send.at[2], mod_recv.at[2])

    load_act.wait()
    x[...] = act[p.m].astype(F32)

    def norm_one(j):
        def body(r):
            act[j, r, :] = rms_of(act[j, r, :].astype(F32), gains[pl.ds(0, 1), :]).astype(BF)

        each_rows(rows, body)

    each(4, norm_one)
    save_act = local.go(act, act1_o)
    load_q.wait()

    def project(j):
        for w in range(3):
            qkv[w, j] = mm(act[j], wq[w]).astype(BF)

    each(4, project)
    save_qkv = local.go(qkv, qkv_o)
    g.pump(SO)
    attend_one = lambda j: attend(qkv.at[0], qkv.at[1], qkv.at[2], ctx, lse, j, causal_ok(key_ok[j, pl.ds(0, 1), :], rows), heads)
    each(4, attend_one)
    save_ctx = local.go(ctx, ctx_o)
    save_lse = local.go(lse, lse_o)
    g.arrived(SO)
    load_o = local.go(so_all, wo)
    save_act.wait()
    save_qkv.wait()
    load_o.wait()
    part = lambda j, k: mm_nt(ctx[j], wo[cols(k, 512), :])
    one.send(part)

    def add_own(k):
        at = cols(k, 512)
        x[:, at] += part(p.m, k)

    each(width // 512, add_own)
    g.arrived(PATCH)
    if pr != cq_r:
        wp[...] = jnp.zeros(wp.shape, BF)
    for c in [local.go(patch_w.at[pl.ds(q * pr, pr)], wp.at[pl.ds(q * cq_r, pr)]) for q in range(n_batch)]:
        c.wait()
    load_pat.wait()
    own_cols = pl.ds(pl.multiple_of(p.m * col_w, col_w), col_w)

    def project_patch(j):
        pp[j, :, own_cols] = mm(pat[j], wp[...]).astype(BF)

    each(4, project_patch)
    pp_g.start()
    one.receive()

    def finish_one(r):
        x[r, :] += one.others(r)
        act[p.m, r, :] = rms_of(x[r, :], gains[pl.ds(1, 1), :]).astype(BF)

    each_rows(rows, finish_one)
    a2_g.start()
    save_x = local.go(x, x1_o)
    one.sent()
    g.pump(CV)
    pp_g.forward()
    g.pump(CQ)
    a2_g.forward()
    g.arrived(CK)
    load_ck = local.go(ckv_all.at[0], wq.at[1])
    pp_g.finish()
    save_pp = local.go(pp, pp_o)
    load_ck.wait()

    def project_pp(w):
        def body(j):
            qkv[w, j] = mm(pp[j], wq[w]).astype(BF)

        return body

    each(4, project_pp(1))
    g.arrived(CV)
    load_cv = local.go(ckv_all.at[1], wq.at[2])
    load_cv.wait()
    each(4, project_pp(2))
    g.arrived(CQ)
    load_cq = local.go(cq_all, wq.at[0])
    a2_g.finish()
    save_act = local.go(act, act2_o)
    load_cq.wait()

    def project_cq(j):
        qkv[0, j] = mm(act[j], wq[0]).astype(BF)

    each(4, project_cq)
    save_ctx.wait()
    save_lse.wait()
    save_qkv = local.go(qkv, cqkv_o)

    def attend_two(j):
        ok = jnp.broadcast_to(cross_ok[j, pl.ds(0, 1), :], (rows, cross_ok.shape[2])) > 0.5
        attend(qkv.at[0], qkv.at[1], qkv.at[2], ctx, lse, j, ok, heads)

    each(4, attend_two)
    save_ctx = local.go(ctx, cctx_o)
    save_lse = local.go(lse, clse_o)
    g.arrived(CO)
    load_o = local.go(co_all, wo)
    save_act.wait()
    save_x.wait()
    load_o.wait()
    two.send(part)
    each(width // 512, add_own)
    g.pump(GATE2)
    two.receive()

    def finish_two(r):
        x[r, :] += two.others(r)
        act[p.m, r, :] = rms_of(x[r, :], gains[pl.ds(2, 1), :]).astype(BF)

    each_rows(rows, finish_two)
    a3_g.start()
    save_x = local.go(x, x2_o)
    two.sent()
    g.pump(UP)
    a3_g.forward()
    a3_g.finish()
    save_act = local.go(act, act3_o)

    half = wg.shape[1] // 2
    low, high = pl.ds(0, half), pl.ds(half, half)

    def gate_half(at):
        def body(j):
            value = mm(act[j], wg[:, at])
            gate[j, :, at] = value
            gate_b[j, :, at] = value.astype(BF)

        each(4, body)

    def up_half(at):
        def body(j):
            u = mm(act[j], wg[:, at])
            up[j, :, at] = u.astype(BF)
            hid[j, :, at] = (jax.nn.gelu(gate[j, :, at], approximate=True) * u).astype(BF)

        each(4, body)

    for t, k, at, compute in (
        (GATE, 0, low, gate_half), (GATE2, 0, high, gate_half), (UP, 1, low, up_half), (UP2, 1, high, up_half)
    ):
        g.arrived(t)
        load_g = local.go(gu_all.at[k, :, at], wg.at[:, at])
        load_g.wait()
        compute(at)
    save_gate = local.go(gate_b, gate_o)
    save_up = local.go(up, up_o)
    save_h = local.go(hid, h_o)
    g.sent()
    for c in (save_act, save_x, save_gate, save_up, save_h, save_ctx, save_lse, save_qkv, save_pp):
        c.wait()


def forward_call(n_batch, text_all, patch_all, gains, patch_own, key_ok, cross_ok, qkv_w,
                 w_so, w_ckv, w_cq, w_co, w_gu, w_down):
    n_out = n_batch // 2
    dma = pltpu.SemaphoreType.DMA
    items, rows, width = text_all.shape
    c, f = qkv_w.shape[2], w_gu.shape[2]
    patch_width = patch_all.shape[2]
    keys = patch_all.shape[1]
    sds = jax.ShapeDtypeStruct
    any_ = pl.BlockSpec(memory_space=pl.ANY)
    vmem = pl.BlockSpec(memory_space=pltpu.VMEM)
    big = (items, rows, width)
    return pl.pallas_call(
        functools.partial(forward_kernel, n_batch),
        out_shape=[
            sds((width, c), BF), sds((n_batch * patch_own.shape[0], c), BF), sds((2, width, c), BF), sds((width, c), BF),
            sds((width, c), BF), sds((2, width, f), BF), sds((width, f), BF),
            sds(big, BF), sds(big, BF), sds(big, BF),
            sds((3, items, rows, c), BF), sds((3, items, rows, c), BF),
            sds((items, rows, c), BF), sds((items, rows, c), BF),
            sds((items, rows, 128), F32), sds((items, rows, 128), F32),
            sds((items, keys, width), BF), sds((rows, width), F32), sds((rows, width), F32),
            sds((items, rows, f), BF), sds((items, rows, f), BF), sds((items, rows, f), BF),
        ],
        in_specs=[any_, any_, vmem, vmem, vmem, vmem, any_] + [vmem] * 6,
        out_specs=[any_] * 22,
        scratch_shapes=[
            pltpu.VMEM(big, BF), pltpu.VMEM((rows, width), F32), pltpu.VMEM((3, width, c), BF),
            pltpu.VMEM((width, c), BF), pltpu.VMEM((patch_width, c), BF), pltpu.VMEM((items, keys, patch_width), BF),
            pltpu.VMEM((items, keys, width), BF), pltpu.VMEM((3, items, rows, c), BF), pltpu.VMEM((items, rows, c), BF),
            pltpu.VMEM((items, rows, 128), F32),
        ]
        + [pltpu.VMEM((rows, width), BF)] * 5
        + [pltpu.VMEM((width, f), BF), pltpu.VMEM((items, rows, f), F32), pltpu.VMEM((items, rows, f), BF), pltpu.VMEM((items, rows, f), BF), pltpu.VMEM((items, rows, f), BF)]
        + BatchGather.semaphores(n_out, 10)
        + [dma((3, 3)), dma((3, 3)), dma((2, 3)), dma((2, 3)), dma((32 + n_batch,)),
           dma((f // STRIP, n_out + 1)), dma((f // STRIP, n_out)), dma((f // STRIP,))],
        compiler_params=pltpu.CompilerParams(collective_id=1, has_side_effects=True, vmem_limit_bytes=VMEM_LIMIT),
        cost_estimate=pl.CostEstimate(flops=35 * 10**9, bytes_accessed=600 * 10**6, transcendentals=0),
    )(text_all, patch_all, gains, patch_own, key_ok, cross_ok, qkv_w, w_so, w_ckv, w_cq, w_co, w_gu, w_down)


class Line:
    def z_copy(self, t, s):
        p = self.p
        return remote(self.block(t, (p.outer + s) % p.n_out), self.slot(t, s), self.z_send.at[t, s],
                      self.z_recv.at[t, s], batch=p.z_peer(s), mod=p.m)

    def to_relay(self, t):
        p = self.p
        return remote(self.block(t, p.opposite), self.slot(t, p.n_out), self.z_send.at[t, 0], self.z_recv.at[t, 0],
                      batch=p.relay * 2 + p.inner, mod=p.m)

    def to_end(self, t):
        p = self.p
        return remote(self.block(t, p.end), self.slot(t, p.outward), self.z_send.at[t, 0],
                      self.z_recv.at[t, p.outward], batch=p.end * 2 + p.inner, mod=p.m)

    def z_start(self, t):
        p = self.p
        if not self.line:
            for s in p.shifts:
                self.z_copy(t, s).start()
            return
        self.z_copy(t, 2).start()
        self.z_copy(t, p.inward).start()

        @pl.when(p.is_end)
        def _():
            self.to_relay(t).start()

    def z_relay(self, t):
        p = self.p
        if not self.line:
            return

        @pl.when(p.is_mid)
        def _():
            self.to_relay(t).wait_recv()
            a, b = self.views(t)
            self.fetch((self.block(t, p.end), a), (self.slot(t, p.n_out), b))
            self.add(a, b)
            self.fetch((a, self.block(t, p.end)))
            self.to_end(t).start()

    def fetch(self, *pairs):
        copies = [pltpu.make_async_copy(a, b, self.loc.at[k]) for k, (a, b) in enumerate(pairs)]
        for copy in copies:
            copy.start()
        for copy in copies:
            copy.wait()

    def add(self, a, *others):
        lead, rows, width = a.shape
        step = 16
        while rows % (2 * step) == 0 and step * width < 16384:
            step *= 2

        def body(o):
            def one(r):
                total = a[o, r, :].astype(F32)
                for b in others:
                    total = total + b[o, r, :].astype(F32)
                a[o, r, :] = total.astype(BF)

            each_rows(rows, one, step)

        each(lead, body)

    def z_arrived(self, t):
        p = self.p
        if not self.line:
            for s in p.shifts:
                self.z_copy(t, s).wait_recv()
            return
        self.z_copy(t, 2).wait_recv()
        self.z_copy(t, self.first_slot()).wait_recv()

        @pl.when(p.is_mid)
        def _():
            self.z_copy(t, 3).wait_recv()

    def first_slot(self):
        return 3 - 2 * ((self.p.outer + 2) // 3)

    def z_sent(self, t):
        p = self.p
        if not self.line:
            for s in p.shifts:
                self.z_copy(t, s).wait_send()
            return
        self.z_copy(t, 2).wait_send()
        self.z_copy(t, p.inward).wait_send()
        self.to_relay(t).wait_send()


class GradSum(Line):
    def __init__(self, place, pieces, mine, got, sems, loc):
        self.p = place
        self.pieces = pieces
        self.mine, self.got = mine, got
        self.x_send, self.x_recv, self.z_send, self.z_recv = sems
        self.loc = loc
        self.line = place.line
        self.ready = self.started = self.done = 0
        self.window = 2

    @staticmethod
    def semaphores(n_out, count):
        dma = pltpu.SemaphoreType.DMA
        return [dma((count,)), dma((count,)), dma((count, n_out)), dma((count, n_out))]

    def block(self, t, o):
        return self.pieces[t][1].at[pl.ds(o, 1)]

    def slot(self, t, s):
        return self.pieces[t][2].at[pl.ds(s, 1)]

    def views(self, t):
        _, rows, width = self.pieces[t][1].shape
        return [v.at[pl.ds(0, 1), pl.ds(0, rows), pl.ds(0, width)] for v in (self.mine, self.got)]

    def x_copy(self, t):
        whole, from_x, _ = self.pieces[t]
        return remote(whole.at[:, 1 - self.p.inner], from_x, self.x_send.at[t], self.x_recv.at[t],
                      batch=self.p.x_peer, mod=self.p.m)

    def kick(self):
        while self.started < self.ready and self.started - self.done < self.window:
            self.x_copy(self.started).start()
            self.started += 1

    def advance(self):
        self.ready += 1
        self.kick()

    def pump(self, count=1):
        for _ in range(min(count, self.ready - self.done)):
            t = self.done
            whole, from_x, from_z = self.pieces[t]
            n_out, rows, width = from_x.shape
            self.x_copy(t).wait_recv()
            self.done += 1
            self.kick()
            mine = self.mine.at[:, pl.ds(0, rows), pl.ds(0, width)]
            got = self.got.at[:, pl.ds(0, rows), pl.ds(0, width)]
            self.fetch((whole.at[:, self.p.inner], mine), (from_x, got))
            self.add(mine, got)
            self.fetch((mine, from_x), (mine.at[self.p.outer], from_z.at[0]))
            self.z_start(t)
            if t:
                self.z_relay(t - 1)

    def finish(self):
        last = len(self.pieces) - 1
        self.pump(len(self.pieces))
        self.z_relay(last)
        for t in range(len(self.pieces)):
            self.x_copy(t).wait_send()
            self.z_arrived(t)
            self.z_sent(t)


def attend_back(q_ref, k_ref, v_ref, do_ref, lse_ref, dq_ref, dk_ref, dv_ref, j, allowed, heads):
    scale = HD ** (-0.5)
    for h in range(heads):
        at = pl.ds(h * HD, HD)
        q, k, v, do = q_ref[j, :, at], k_ref[j, :, at], v_ref[j, :, at], do_ref[j, :, at]
        s = jnp.where(allowed, mm_nt(q, k) * scale, -1e30)
        probs = jnp.exp(s - lse_ref[j, :, pl.ds(h, 1)])
        dp = mm_nt(do, v)
        ds = (probs * (dp - jnp.sum(probs * dp, axis=-1, keepdims=True))).astype(BF)
        dv_ref[j, :, at] = mm_tn(probs.astype(BF), do).astype(BF)
        dq_ref[j, :, at] = (mm(ds, k) * scale).astype(BF)
        dk_ref[j, :, at] = (mm_tn(ds, q) * scale).astype(BF)


def gelu_parts(g):
    c = 0.7978845608028654
    t = jnp.tanh(c * (g + 0.044715 * g * g * g))
    half = 0.5 * (1.0 + t)
    return g * half, half + 0.5 * g * (1.0 - t * t) * c * (1.0 + 3 * 0.044715 * g * g)


def backward_kernel(n_batch, *refs):
    (dy_all, text, pat_all, gains, key_ok, cross_ok, qkv_w, so_all, ckv_all, cq_all, co_all, gu_all, down_all,
     act1, act2, act3, qkv_i, cqkv_i, ctx_i, cctx_i, lse_i, clse_i, pp_i, x1_i, x2_i, gate_i, up_i, h_i) = refs[:28]
    (result, d_text, gain_out, whole_f, from_x_f, from_z_f, whole_c, from_x_c, from_z_c,
     whole_p, from_x_p, from_z_p) = refs[28:40]
    (dy, act_a, act_b, gate, up, hid, w0, w1, qkv, dqkv, ctx, dctx, dpp, lse, g, da, v, fs, ns, cf, yr, cn,
     cf2, yr2, cn2, st, mine, got, dg, dgm, dgx, dgz,
     gx_send, gx_recv, gz_send, gz_recv, mod_send, mod_recv, sum_send, sum_recv, gain_send, gain_recv,
     gx, loc, loc2) = refs[40:]
    p = Place(n_batch)
    local = Local(loc)
    items, rows, width = dy.shape
    c, f = qkv_w.shape[2], gu_all.shape[2]
    half = f // 2
    n_out, blk = p.n_out, width // n_batch
    heads = c // HD
    pieces = [
        (whole_f.at[k], from_x_f.at[k], from_z_f.at[k // 2, :, :, pl.ds(k % 2 * half, half)]) for k in range(6)
    ]
    pieces += [(whole_c.at[k], from_x_c.at[k], from_z_c.at[k]) for k in range(8)]
    pieces.append((whole_p, from_x_p, from_z_p))
    gs = GradSum(p, pieces, mine, got, (gx_send, gx_recv, gz_send, gz_recv), loc2)
    left = pl.ds(0, c)
    right = pl.ds(c, c)

    load_dy = local.go(dy_all, dy)
    load_h = local.go(h_i, hid)
    load_w0 = local.go(down_all, w0)
    load_v = local.go(x2_i, v)
    load_gate = local.go(gate_i, gate)
    load_up = local.go(up_i, up)
    load_w1 = local.go(gu_all.at[0], w1)
    load_a = local.go(act3, act_a)
    load_b = local.go(act2, act_b)
    p.greet()
    set_a = (fs, ns, cf, yr, cn)
    set_b = (fs, ns, cf2, yr2, cn2)
    sums = [
        BranchSum(p, bufs, sum_send.at[k], sum_recv.at[k])
        for k, bufs in enumerate((set_b, set_a, set_a, set_b, set_a))
    ]
    gathers = [ModGather(p, lambda j: dy.at[j], mod_send.at[k], mod_recv.at[k]) for k in range(2)]
    dg[...] = jnp.zeros(dg.shape, F32)

    def piece(acts, grads, first, count):
        t = gs.ready
        whole = pieces[t][0]
        used = whole.shape[2]
        chunk = max(256, 2 * blk)
        per = chunk // (2 * blk)

        def body(n):
            a = acts[:, :, cols(n, chunk)].reshape(items * rows, chunk)
            b = grads[:, :, pl.ds(first, count)].reshape(items * rows, count)
            st[pl.ds(n * per, per), :, :, pl.ds(0, count)] = mm_tn(a, b).astype(BF).reshape(per, 2, blk, count)

        each(width // chunk, body)
        copy = pltpu.make_async_copy(st.at[:, :, pl.ds(0, used), pl.ds(0, count)], whole, loc2.at[2])
        copy.start()
        copy.wait()
        gs.advance()

    def norm_back(k, total, v_rows):
        def body(r):
            grad = da[r, :] + total.others(r)
            val = v_rows(r)
            factor = lax.rsqrt(jnp.mean(val * val, axis=-1, keepdims=True) + 1e-06)
            dg[pl.ds(k, 1), :] += jnp.sum(grad * val * factor, axis=0, keepdims=True)
            scaled = gains[pl.ds(k, 1), :] * grad
            back = factor * scaled - val * (factor * factor * factor * jnp.mean(scaled * val, axis=-1, keepdims=True))
            g[r, :] += back
            if k:
                dy[p.m, r, :] = g[r, :].astype(BF)

        each_rows(rows, body)

    load_dy.wait()
    load_h.wait()
    g[...] = dy[p.m].astype(F32)
    piece(dy, hid, 0, half)
    piece(dy, hid, half, half)
    load_w0.wait()
    load_gate.wait()
    load_up.wait()

    def mix_back(j):
        dh = mm(dy[j], w0[...])
        value, slope = gelu_parts(gate[j].astype(F32))
        gate[j] = (dh * up[j].astype(F32) * slope).astype(BF)
        up[j] = (dh * value).astype(BF)

    each(items, mix_back)
    load_w0 = local.go(gu_all.at[1], w0)
    load_w1.wait()
    load_w0.wait()
    act_part = lambda j, k: mm_nt(gate[j], w1[cols(k, 512), :]) + mm_nt(up[j], w0[cols(k, 512), :])
    sums[1].send(act_part)
    gs.pump()

    def own_part(part):
        def body(k):
            da[:, cols(k, 512)] = part(p.m, k)

        each(width // 512, body)

    own_part(act_part)
    load_w0 = [local.go(co_all, w0.at[:, left]), local.go(cq_all, w0.at[:, right])]
    load_w1 = [local.go(ckv_all.at[0], w1.at[:, left]), local.go(ckv_all.at[1], w1.at[:, right])]
    load_s = [local.go(cqkv_i, qkv), local.go(cctx_i, ctx), local.go(clse_i, lse)]
    load_a.wait()
    piece(act_a, gate, 0, half)
    piece(act_a, gate, half, half)
    piece(act_a, up, 0, half)
    gs.pump()
    load_v.wait()
    sums[1].receive()
    norm_back(2, sums[1], lambda r: v[r, :])
    gathers[0].start()
    sums[1].sent()
    load_v = local.go(x1_i, v)
    piece(act_a, up, half, half)
    load_a = local.go(pp_i, act_a)
    gs.pump()
    gathers[0].forward()
    gathers[0].finish()

    for copy in load_w0 + load_w1 + load_s:
        copy.wait()

    def ctx_back(j):
        dctx[j] = mm(dy[j], w0[:, left]).astype(BF)

    each(items, ctx_back)
    piece(dy, ctx, 0, c)

    def cross_back(j):
        ok = jnp.broadcast_to(cross_ok[j, pl.ds(0, 1), :], (rows, cross_ok.shape[2])) > 0.5
        attend_back(qkv.at[0], qkv.at[1], qkv.at[2], dctx, lse, dqkv.at[0], dqkv.at[1], dqkv.at[2], j, ok, heads)

    each(items, cross_back)
    query_part = lambda j, k: mm_nt(dqkv[0, j], w0[cols(k, 512), right])
    sums[2].send(query_part)
    gs.pump()
    own_part(query_part)
    load_w0 = [local.go(so_all, w0.at[:, left]), local.go(qkv_w.at[0], w0.at[:, right])]
    load_s = [local.go(qkv_i, qkv), local.go(ctx_i, ctx), local.go(lse_i, lse)]
    load_b.wait()
    piece(act_b, dqkv.at[0], 0, c)
    load_b = local.go(act1, act_b)
    load_a.wait()
    piece(act_a, dqkv.at[1], 0, c)
    piece(act_a, dqkv.at[2], 0, c)
    load_a = local.go(pat_all, act_a)
    load_v.wait()
    sums[2].receive()
    norm_back(1, sums[2], lambda r: v[r, :])
    gathers[1].start()
    sums[2].sent()
    load_v = local.go(x2_i, v)
    gs.pump()
    proj_part = lambda j, k: mm_nt(dqkv[1, k], w1[cols(j, c), left]) + mm_nt(dqkv[2, k], w1[cols(j, c), right])
    sums[3].send_core(proj_part)

    def proj_own(k):
        dpp[k] = proj_part(p.m, k).astype(BF)

    each(items, proj_own)
    gathers[1].forward()
    gathers[1].finish()
    sums[3].send_far(proj_part)
    load_w1 = [local.go(qkv_w.at[1], w1.at[:, left]), local.go(qkv_w.at[2], w1.at[:, right])]

    for copy in load_w0 + load_s:
        copy.wait()
    each(items, ctx_back)
    piece(dy, ctx, 0, c)
    gs.pump()

    def self_back(j):
        ok = causal_ok(key_ok[j, pl.ds(0, 1), :], rows)
        attend_back(qkv.at[0], qkv.at[1], qkv.at[2], dctx, lse, dqkv.at[0], dqkv.at[1], dqkv.at[2], j, ok, heads)

    each(items, self_back)
    load_b.wait()
    for k in range(3):
        piece(act_b, dqkv.at[k], 0, c)
    gs.pump()
    sums[3].receive()

    def proj_done(k):
        every = pl.ds(0, rows)
        dpp[k] = (dpp[k].astype(F32) + sums[3].others(every, cols(k, c))).astype(BF)

    each(items, proj_done)
    sums[3].sent()
    for copy in load_w1:
        copy.wait()
    self_part = lambda j, k: (
        mm_nt(dqkv[0, j], w0[cols(k, 512), right])
        + mm_nt(dqkv[1, j], w1[cols(k, 512), left])
        + mm_nt(dqkv[2, j], w1[cols(k, 512), right])
    )
    sums[4].send(self_part)
    own_part(self_part)
    load_w0 = local.go(down_all, w0)
    gs.pump()
    load_a.wait()
    piece(act_a, dpp, 0, c)
    gs.pump()
    sums[4].receive()
    norm_back(0, sums[4], lambda r: text[r, :].astype(F32))
    save_text = local.go(g, d_text)
    sums[4].sent()

    mod_g = [
        remote(dg, dgm.at[k], gain_send.at[k], gain_recv.at[k], batch=p.b, mod=j)
        for k, j in enumerate((p.core, p.far, p.farcore))
    ]
    for copy in mod_g:
        copy.start()
    load_w0.wait()
    out_part = lambda j, k: mm_nt(hid[j], w0[cols(k, 512), :])
    sums[0].send(out_part)
    gs.pump()
    load_v.wait()

    def result_own(k):
        at = cols(k, 512)
        da[:, at] = v[:, at] + out_part(p.m, k)

    each(width // 512, result_own)
    for copy in mod_g:
        copy.wait()
    dg[...] += dgm[0] + dgm[1] + dgm[2]
    across = remote(dg, dgx, gx.at[0], gx.at[1], batch=p.x_peer, mod=p.m)
    across.start()
    gs.pump()
    sums[0].receive()

    def result_done(r):
        da[r, :] += sums[0].others(r)

    each_rows(rows, result_done)
    save_result = local.go(da, result)
    sums[0].sent()
    across.wait()
    dg[...] += dgx[...]
    along = [
        remote(dg, dgz.at[s], gain_send.at[3 + s], gain_recv.at[3 + s], batch=p.z_peer(s), mod=p.m)
        for s in p.shifts
    ]
    for copy in along:
        copy.start()
    gs.pump()
    for copy in along:
        copy.wait()
    total = dg[...]
    for s in p.shifts:
        total = total + dgz[s]
    gain_out[...] = total
    gs.finish()
    save_result.wait()
    save_text.wait()


def backward_call(n_batch, inputs, patch_rows):
    n_out = n_batch // 2
    dma = pltpu.SemaphoreType.DMA
    sds = jax.ShapeDtypeStruct
    items, rows, width = inputs[0].shape
    c, f = inputs[6].shape[2], inputs[11].shape[2]
    blk = width // n_batch
    any_ = pl.BlockSpec(memory_space=pl.ANY)
    vmem = pl.BlockSpec(memory_space=pltpu.VMEM)
    big = (items, rows, width)
    heads_shape = (items, rows, c)
    V = lambda shape, dtype=BF: pltpu.VMEM(shape, dtype)

    def bufs(count, r, w):
        lead = (count,) if count else ()
        return [sds(lead + (n_out, 2, r, w), BF), sds(lead + (n_out, r, w), BF), sds(lead + (n_out + 1, r, w), BF)]

    return pl.pallas_call(
        functools.partial(backward_kernel, n_batch),
        out_shape=[sds((rows, width), F32), sds((rows, width), F32), sds((8, width), F32)]
        + bufs(6, blk, f // 2)[:2] + [sds((3, n_out + 1, blk, f), BF)] + bufs(8, blk, c) + bufs(0, patch_rows, c),
        in_specs=[any_, vmem, any_, vmem, vmem, vmem] + [any_] * 22,
        out_specs=[any_, any_, vmem] + [any_] * 9,
        scratch_shapes=[V(big)] * 3
        + [V((items, rows, f))] * 3
        + [V((width, f))] * 2
        + [V((3,) + heads_shape)] * 2
        + [V(heads_shape)] * 3
        + [V((items, rows, 128), F32)]
        + [V((rows, width), F32)] * 3
        + [V((rows, width))] * 8
        + [V((n_out, 2, blk, f // 2)), V((n_out, blk, f // 2)), V((n_out, blk, f // 2))]
        + [V((8, width), F32), V((3, 8, width), F32), V((8, width), F32), V((n_out, 8, width), F32)]
        + GradSum.semaphores(n_out, 15)
        + [dma((2, 3)), dma((2, 3)), dma((5, 3)), dma((5, 3)), dma((3 + n_out,)), dma((3 + n_out,)), dma((2,)),
           dma((48,)), dma((4,))],
        compiler_params=pltpu.CompilerParams(collective_id=2, has_side_effects=True, vmem_limit_bytes=VMEM_LIMIT),
        cost_estimate=pl.CostEstimate(flops=75 * 10**9, bytes_accessed=800 * 10**6, transcendentals=0),
    )(*inputs)


def local(n_batch, n_mod, text, patches, text_lengths, patch_mask, cotangent, gains,
          w_qkv, w_so, w_cq, w_ckv, w_co, w_patch, w_gu, w_down):
    own_items, text_rows, width = text.shape
    mod = lax.axis_index("mod")
    nb = n_batch
    blk = width // nb
    positions = jnp.arange(text_rows)

    gw = blk // n_mod
    gain_tile = lax.dynamic_update_slice(jnp.zeros((16, blk), BF), gains, (0, mod * gw))
    col_w = width // n_mod
    pr = w_patch.shape[0]
    pr_pad = -(-pr // 16) * 16
    patch_tile = jnp.pad(w_patch, ((0, pr_pad - pr), (0, 0))).reshape(pr_pad, n_mod, col_w)
    patch_tile = jnp.transpose(patch_tile, (1, 0, 2))
    block, block_pad = n_mod * pr, -(-n_mod * pr // 16) * 16
    patch_in = jnp.pad(patches[0].reshape(-1, nb, block), ((0, 0), (0, 0), (0, blk - block))).reshape(-1, width)
    own_length = lax.dynamic_slice_in_dim(text_lengths, mod * own_items, own_items)
    valid = jnp.broadcast_to((positions[:, None] < own_length).astype(F32), (text_rows, 128))
    text_all, patch_all, gain_raw, patch_rows, self_qkv, dy_all, so_t, co_t, down_t = first_call(
        n_batch, text[0], patch_in, gain_tile, patch_tile, w_qkv, w_so, w_co, w_down, cotangent[0], valid
    )
    gain_all = jnp.transpose(gain_raw[:, :8], (1, 0, 2)).reshape(8, width).astype(F32)
    patch_own = patch_rows[:, :pr].reshape(block, col_w)
    patch_own = jnp.pad(patch_own, ((0, block_pad - block), (0, 0)))
    row_ok = (positions[None, :] < text_lengths[:, None]).astype(F32)
    key_ok = jnp.broadcast_to(row_ok[:, None, :], (n_mod, 8, text_rows))
    cross_ok = jnp.broadcast_to((patch_mask > 0).astype(F32)[:, None, :], (n_mod, 8, patch_mask.shape[1]))
    (so_all, _, ckv_all, cq_all, co_all, gu_all, down_all, act1, act2, act3, qkv, cqkv,
     ctx, cctx, lse, clse, pp, x1, x2, gate, up, hid) = forward_call(
        n_batch, text_all, patch_all, gain_all, patch_own, key_ok, cross_ok, self_qkv,
        so_t, w_ckv, w_cq, co_t, w_gu, down_t)
    outs = backward_call(
        n_batch,
        (dy_all, text[0], patch_all, gain_all, key_ok, cross_ok, self_qkv, so_all, ckv_all, cq_all, co_all, gu_all,
         down_all, act1, act2, act3, qkv, cqkv, ctx, cctx, lse, clse, pp, x1, x2, gate, up, hid),
        block_pad,
    )
    result, d_text, gain_sum = outs[:3]
    sum_f, sum_c, sum_p = outs[5], outs[8], outs[11]
    at = lax.axis_index("batch") * blk + mod * gw
    d_gains = lax.dynamic_slice(gain_sum, (0, at), (3, gw))

    n_out = nb // 2
    outer = lax.axis_index("batch") // 2
    slots = jnp.arange(n_out)
    missing = (((outer == 0) & (slots == 1)) | ((outer == 3) & (slots == 3))) & (n_out == 4)

    def total(parts, axis=0):
        parts = lax.slice_in_dim(parts, 0, n_out, axis=axis)
        gone = missing.reshape((1,) * axis + (n_out,) + (1,) * (parts.ndim - axis - 1))
        return jnp.sum(jnp.where(gone, 0.0, parts.astype(F32)), axis=axis)

    grad_patch = total(sum_p)[:block].reshape(n_mod, pr, col_w)
    grad_patch = lax.all_to_all(grad_patch, "mod", 0, 0, tiled=True)
    grad_patch = jnp.transpose(grad_patch, (1, 0, 2)).reshape(pr, width)
    return (
        result[None],
        d_text[None],
        d_gains,
        total(sum_c[5:8], 1),
        total(sum_c[4]).T,
        total(sum_c[1]),
        total(sum_c[2:4], 1),
        total(sum_c[0]).T,
        grad_patch,
        total(sum_f[1:], 1),
        total(sum_f[0]).T,
    )


def solution(mesh):
    placed = (
        P(("batch", "mod"), None, None),
        P(("batch", "mod"), None, None),
        P("batch"),
        P("batch", None),
        P(("batch", "mod"), None, None),
        P(None, ("batch", "mod")),
        P(None, "batch", "mod"),
        P("mod", "batch"),
        P("batch", "mod"),
        P(None, "batch", "mod"),
        P("mod", "batch"),
        P(("batch", "mod"), None),
        P(None, "batch", "mod"),
        P("mod", "batch"),
    )

    def run(*args):
        return local(mesh.shape["batch"], mesh.shape["mod"], *args)

    return jax.shard_map(
        run,
        mesh=mesh,
        in_specs=placed,
        out_specs=(
            P(("batch", "mod"), None, None),
            P(("batch", "mod"), None, None),
            P(None, ("batch", "mod")),
            P(None, "batch", "mod"),
            P("mod", "batch"),
            P("batch", "mod"),
            P(None, "batch", "mod"),
            P("mod", "batch"),
            P(("batch", "mod"), None),
            P(None, "batch", "mod"),
            P("mod", "batch"),
        ),
        check_vma=False,
    )
```

```python
import functools

import jax
import jax.numpy as jnp
from jax import lax
from jax.experimental import pallas as pl
from jax.experimental.pallas import tpu as pltpu
from jax.sharding import PartitionSpec as P

HD = 128
F32 = jnp.float32
BF = jnp.bfloat16


VMEM_LIMIT = 62 * 2**20
MESH = pl.DeviceIdType.MESH


class Place:
    def __init__(self, n_batch):
        self.n_batch = n_batch
        self.n_out = n_batch // 2
        self.b = lax.axis_index("batch")
        self.m = lax.axis_index("mod")
        self.outer = self.b // 2
        self.inner = self.b % 2
        self.core = self.m + 1 - 2 * (self.m % 2)
        self.far = (self.m + 2) % 4
        self.farcore = (self.core + 2) % 4
        self.x_peer = self.b + 1 - 2 * self.inner
        self.line = self.n_out == 4
        self.shifts = [2, 1, 3] if self.line else list(range(1, self.n_out))
        self.is_mid = (self.outer + 1) // 2 == 1
        self.is_end = (self.outer + 1) // 2 != 1
        self.inward = 1 + 2 * (self.outer // 2)
        self.outward = 3 - 2 * (self.outer // 2)
        self.end = 3 * (self.outer // 2)
        self.relay = 2 - self.outer // 3
        self.opposite = 3 - self.outer

    def z_peer(self, s):
        return (self.outer + s) % self.n_out * 2 + self.inner

    def z_from(self, s):
        return (self.outer - s + self.n_out) % self.n_out * 2 + self.inner

    def greet(self):
        barrier = pltpu.get_barrier_semaphore()
        ids = [{"batch": self.z_peer(s), "mod": self.m} for s in self.shifts]
        ids.append({"batch": self.x_peer, "mod": self.m})
        for j in (self.core, self.far, self.farcore):
            ids.append({"batch": self.b, "mod": j})
        for device in ids:
            pl.semaphore_signal(barrier, inc=1, device_id=device, device_id_type=MESH)
        pl.semaphore_wait(barrier, len(ids))


def remote(src, dst, send, recv, **device):
    return pltpu.make_async_remote_copy(
        src_ref=src, dst_ref=dst, send_sem=send, recv_sem=recv, device_id=device, device_id_type=MESH
    )


class BatchGather:
    def __init__(self, place, tensors, sems, wides=(), wide_sems=None, early=()):
        self.p = place
        self.tensors = tensors
        self.z_send, self.z_recv, self.x_send, self.x_recv, self.own = sems
        self.started = 0
        self.early = early
        self.events = [(t, s) for t in range(len(tensors)) for s in [0] + place.shifts if s or t not in early]
        self.at = 0
        self.wides = wides
        self.wide_sems = wide_sems
        self.steps = [step for c in range(len(wides)) for step in ((self.wide_z, c), (self.wide_relay, c))]

    @staticmethod
    def semaphores(n_out, count):
        dma = pltpu.SemaphoreType.DMA
        return [dma((count, n_out)) for _ in range(4)] + [dma((count,))]

    def z_copy(self, t, s):
        src, block = self.tensors[t]
        return remote(src, block(self.p.b), self.z_send.at[t, s], self.z_recv.at[t, s],
                      batch=self.p.z_peer(s), mod=self.p.m)

    def z_relay(self, t):
        where = self.tensors[t][1]((self.p.outer + 2) % 4 * 2 + self.p.inner)
        return remote(where, where, self.z_send.at[t, 0], self.z_recv.at[t, self.p.inward],
                      batch=self.p.end * 2 + self.p.inner, mod=self.p.m)

    def own_copy(self, t):
        src, block = self.tensors[t]
        return pltpu.make_async_copy(src, block(self.p.b), self.own.at[t])

    def x_copy(self, t, s):
        src, block = self.tensors[t]
        where = block(self.p.z_from(s))
        return remote(src if s == 0 else where, where, self.x_send.at[t, s], self.x_recv.at[t, s],
                      batch=self.p.x_peer, mod=self.p.m)

    def straight(self, copy, act):
        p = self.p
        if not p.line:
            for s in p.shifts:
                act(copy(s))
            return
        act(copy(2))
        act(copy(p.inward))

        @pl.when(p.is_mid)
        def _():
            act(copy(p.outward))

    def start(self, count=1):
        for t in range(self.started, min(self.started + count, len(self.tensors))):
            self.straight(lambda s: self.z_copy(t, s), lambda c: c.start())
            self.own_copy(t).start()
            self.started = t + 1

    def pump(self, upto):
        p = self.p
        while self.at < len(self.events) and self.events[self.at][0] <= upto:
            t, s = self.events[self.at]
            if s:
                self.z_copy(t, s).wait_recv()
                if p.line and s == 2:

                    @pl.when(p.is_mid)
                    def _():
                        self.z_relay(t).start()

                if s == p.shifts[-1]:
                    self.start()
            self.x_copy(t, s).start()
            self.at += 1
            if s == p.shifts[-1] and self.steps:
                step, c = self.steps.pop(0)
                step(c)

    def arrived(self, t, ahead=1):
        self.pump(t + ahead)
        self.own_copy(t).wait()
        for s in [0] + self.p.shifts:
            self.x_copy(t, s).wait_recv()

    def wide_own(self, c):
        shard, block, _ = self.wides[c]
        return pltpu.make_async_copy(shard, block(self.p.b), self.wide_sems[2].at[c])

    def wide_x(self, c):
        shard, block, _ = self.wides[c]
        return remote(shard, block(self.p.b), self.wide_sems[0].at[c, 0], self.wide_sems[1].at[c, 0],
                      batch=self.p.x_peer, mod=self.p.m)

    def wide_copy(self, c, s):
        pair = self.wides[c][2](self.p.outer)
        return remote(pair, pair, self.wide_sems[0].at[c, s], self.wide_sems[1].at[c, s],
                      batch=self.p.z_peer(s), mod=self.p.m)

    def wide_on(self, c):
        pair = self.wides[c][2]((self.p.outer + 2) % 4)
        return remote(pair, pair, self.wide_sems[0].at[c, self.p.n_out], self.wide_sems[1].at[c, self.p.inward],
                      batch=self.p.end * 2 + self.p.inner, mod=self.p.m)

    def early_start(self):
        for t in self.early:
            self.x_copy(t, 0).start()

    def wide_start(self):
        for c in range(len(self.wides)):
            self.wide_own(c).start()
            self.wide_x(c).start()

    def wide_z(self, c):
        self.wide_own(c).wait()
        self.wide_x(c).wait_recv()
        self.straight(lambda s: self.wide_copy(c, s), lambda d: d.start())

    def wide_relay(self, c):
        if self.p.line:
            self.wide_copy(c, 2).wait_recv()

            @pl.when(self.p.is_mid)
            def _():
                self.wide_on(c).start()

    def sent(self):
        p = self.p
        for step, c in self.steps:
            step(c)
        for t in range(len(self.tensors)):
            self.straight(lambda s: self.z_copy(t, s), lambda c: c.wait_send())
            for s in [0] + p.shifts:
                self.x_copy(t, s).wait_send()
        for c in range(len(self.wides)):
            self.wide_x(c).wait_send()
            self.straight(lambda s: self.wide_copy(c, s), lambda d: d.wait_send())
            for s in p.shifts[1:] if p.line else p.shifts:
                self.wide_copy(c, s).wait_recv()
        if p.line:

            @pl.when(p.is_mid)
            def _():
                for t in range(len(self.tensors)):
                    self.z_relay(t).wait_send()
                for c in range(len(self.wides)):
                    self.wide_on(c).wait_send()


class ModGather:
    def __init__(self, place, block, send, recv):
        self.p = place
        self.block = block
        mine = block(place.m)
        far = block(place.far)
        self.near = remote(mine, mine, send.at[0], recv.at[0], batch=place.b, mod=place.core)
        self.across = remote(mine, mine, send.at[1], recv.at[1], batch=place.b, mod=place.far)
        self.on = remote(far, far, send.at[2], recv.at[2], batch=place.b, mod=place.core)

    def start(self):
        self.across.start()
        self.near.start()

    def forward(self):
        self.across.wait_recv()
        self.on.start()

    def finish(self):
        self.near.wait_recv()
        self.on.wait_recv()
        self.near.wait_send()
        self.across.wait_send()
        self.on.wait_send()


def first_kernel(n_batch, text, patches, gain_tile, patch_tile, w_qkv, w_so, w_co, w_down, cot, valid,
                 text_all, patch_all, gain_all, patch_rows, qkv_all, dy_all, so_t, co_t, down_t,
                 dy, gain_mod, gain_sum, z_send, z_recv, x_send, x_recv, own, mod_send, mod_recv, misc):
    p = Place(n_batch)
    rows = w_qkv.shape[1]
    tensors = [
        (w_qkv.at[0], lambda q: qkv_all.at[0, pl.ds(q * rows, rows)]),
        (w_qkv.at[1], lambda q: qkv_all.at[1, pl.ds(q * rows, rows)]),
        (gain_sum, lambda q: gain_all.at[q]),
        (w_qkv.at[2], lambda q: qkv_all.at[2, pl.ds(q * rows, rows)]),
    ]
    g = BatchGather(p, tensors, (z_send, z_recv, x_send, x_recv, own), early=(0, 1, 3))
    copies = [
        pltpu.make_async_copy(text, text_all.at[p.m], misc.at[0]),
        pltpu.make_async_copy(patches, patch_all.at[p.m], misc.at[1]),
        pltpu.make_async_copy(gain_tile, gain_mod.at[p.m], misc.at[2]),
        pltpu.make_async_copy(patch_tile.at[p.m], patch_rows.at[p.m], misc.at[3]),
        pltpu.make_async_copy(dy, dy_all.at[p.m], misc.at[4]),
    ]

    def mask_rows(r):
        dy[r, :] = (cot[r, :].astype(F32) * valid[r, pl.ds(0, 1)]).astype(BF)

    each_rows(dy.shape[0], mask_rows)
    for c in copies:
        c.start()
    p.greet()
    gains = [
        remote(gain_tile, gain_mod.at[p.m], mod_send.at[2, k], mod_recv.at[2, k], batch=p.b, mod=j)
        for k, j in enumerate((p.core, p.far, p.farcore))
    ]
    for c in gains:
        c.start()
    g.start()
    g.early_start()
    for c in copies:
        c.wait()
    text_g = ModGather(p, lambda j: text_all.at[j], mod_send.at[0], mod_recv.at[0])
    patch_g = ModGather(p, lambda j: patch_all.at[j], mod_send.at[1], mod_recv.at[1])
    dy_g = ModGather(p, lambda j: dy_all.at[j], mod_send.at[4], mod_recv.at[4])
    text_g.start()
    rows_c = [
        remote(patch_tile.at[j], patch_rows.at[p.m], mod_send.at[3, k], mod_recv.at[3, k], batch=p.b, mod=j)
        for k, j in enumerate((p.core, p.far, p.farcore))
    ]
    for c in rows_c:
        c.start()
    patch_g.start()
    for c in gains:
        c.wait_recv()
    gain_sum[...] = gain_mod[0] + gain_mod[1] + gain_mod[2] + gain_mod[3]
    so_t[...] = w_so[...].T
    co_t[...] = w_co[...].T
    down_t[...] = w_down[...].T
    dy_g.start()
    g.pump(3)
    text_g.forward()
    patch_g.forward()
    dy_g.forward()
    for t in range(4):
        g.arrived(t)
    text_g.finish()
    patch_g.finish()
    dy_g.finish()
    for c in gains:
        c.wait_send()
    for c in rows_c:
        c.wait_recv()
        c.wait_send()
    g.sent()


def first_call(n_batch, text, patches, gain_tile, patch_tile, w_qkv, w_so, w_co, w_down, cot, valid):
    n_out = n_batch // 2
    dma = pltpu.SemaphoreType.DMA
    j, rows, columns = w_qkv.shape
    return pl.pallas_call(
        functools.partial(first_kernel, n_batch),
        out_shape=[
            jax.ShapeDtypeStruct((4,) + text.shape, BF),
            jax.ShapeDtypeStruct((4,) + patches.shape, BF),
            jax.ShapeDtypeStruct((n_batch,) + gain_tile.shape, BF),
            jax.ShapeDtypeStruct(patch_tile.shape, BF),
            jax.ShapeDtypeStruct((j, rows * n_batch, columns), BF),
            jax.ShapeDtypeStruct((4,) + cot.shape, BF),
        ]
        + [jax.ShapeDtypeStruct(w.shape[::-1], BF) for w in (w_so, w_co, w_down)],
        in_specs=[pl.BlockSpec(memory_space=pltpu.VMEM)] * 10,
        out_specs=[pl.BlockSpec(memory_space=pl.ANY)] * 6 + [pl.BlockSpec(memory_space=pltpu.VMEM)] * 3,
        scratch_shapes=[
            pltpu.VMEM(cot.shape, BF),
            pltpu.VMEM((4,) + gain_tile.shape, BF),
            pltpu.VMEM(gain_tile.shape, BF),
        ]
        + BatchGather.semaphores(n_out, 4)
        + [dma((5, 3)), dma((5, 3)), dma((5,))],
        compiler_params=pltpu.CompilerParams(collective_id=0, has_side_effects=True),
        cost_estimate=pl.CostEstimate(flops=10**6, bytes_accessed=300 * 10**6, transcendentals=0),
    )(text, patches, gain_tile, patch_tile, w_qkv, w_so, w_co, w_down, cot, valid)


def mm(a, b):
    return lax.dot_general(a, b, (((1,), (0,)), ((), ())), preferred_element_type=F32)


def mm_nt(a, b):
    return lax.dot_general(a, b, (((1,), (1,)), ((), ())), preferred_element_type=F32)


def mm_tn(a, b):
    return lax.dot_general(a, b, (((0,), (0,)), ((), ())), preferred_element_type=F32)


class Local:
    def __init__(self, sems):
        self.sems = sems
        self.used = 0

    def go(self, src, dst):
        copy = pltpu.make_async_copy(src, dst, self.sems.at[self.used])
        self.used += 1
        copy.start()
        return copy


STEP = 32


def each_rows(rows, body, step=STEP):
    def one(r, carry):
        body(pl.ds(pl.multiple_of(r * step, step), step))
        return carry

    lax.fori_loop(0, rows // step, one, 0)


def each(count, body, first=0):
    def one(k, carry):
        body(k)
        return carry

    lax.fori_loop(first, count, one, 0)


def cols(n, width):
    return pl.ds(pl.multiple_of(n * width, width), width)


def rms_of(values, gain):
    return values * lax.rsqrt(jnp.mean(values * values, axis=-1, keepdims=True) + 1e-06) * gain


def attend(q_ref, k_ref, v_ref, out_ref, lse_ref, j, allowed, heads):
    for h in range(heads):
        at = pl.ds(h * HD, HD)
        s = mm_nt(q_ref[j, :, at], k_ref[j, :, at]) * HD ** (-0.5)
        s = jnp.where(allowed, s, -1e30)
        top = jnp.max(s, axis=-1, keepdims=True)
        e = jnp.exp(s - top)
        total = jnp.sum(e, axis=-1, keepdims=True)
        probs = (e / total).astype(BF)
        out_ref[j, :, at] = mm(probs, v_ref[j, :, at]).astype(BF)
        lse_ref[j, :, pl.ds(h, 1)] = top + jnp.log(total)


def causal_ok(key_row, rows):
    shape = (rows, key_row.shape[1])
    return (lax.broadcasted_iota(jnp.int32, shape, 1) <= lax.broadcasted_iota(jnp.int32, shape, 0)) & (
        jnp.broadcast_to(key_row, shape) > 0.5
    )


class BranchSum:
    def __init__(self, place, bufs, send, recv, step=512):
        self.p = place
        self.step = step
        self.fs, self.ns, self.cf, self.yr, self.cn = bufs
        self.to_core = remote(self.fs, self.cf, send.at[0], recv.at[0], batch=place.b, mod=place.core)
        self.to_far = remote(self.fs, self.yr, send.at[1], recv.at[1], batch=place.b, mod=place.far)
        self.to_near = remote(self.ns, self.cn, send.at[2], recv.at[2], batch=place.b, mod=place.core)

    def send(self, part):
        self.send_core(part)
        self.send_far(part)

    def send_core(self, part):
        p, step = self.p, self.step
        n = self.fs.shape[1] // step

        def first(k):
            self.fs[:, cols(k, step)] = part(p.farcore, k).astype(BF)

        def second(k):
            self.ns[:, cols(k, step)] = part(p.core, k).astype(BF)

        each(n, first)
        self.to_core.start()
        each(n, second)
        self.to_near.start()

    def send_far(self, part):
        p, step = self.p, self.step
        n = self.fs.shape[1] // step

        def third(k):
            at = cols(k, step)
            self.fs[:, at] = (part(p.far, k) + self.cf[:, at].astype(F32)).astype(BF)

        self.to_core.wait()
        each(n, third)
        self.to_far.start()

    def receive(self):
        self.to_near.wait_recv()
        self.to_far.wait_recv()

    def others(self, rows, at=slice(None)):
        return self.cn[rows, at].astype(F32) + self.yr[rows, at].astype(F32)

    def sent(self):
        self.to_near.wait_send()
        self.to_far.wait_send()


def halves(shard, whole, rows):
    half = shard.shape[1] // 2

    def piece(k):
        at = pl.ds(k * half, half)
        return (shard.at[:, at], lambda q: whole.at[pl.ds(q * rows, rows), at])

    return [piece(0), piece(1)]


STRIP = 256


def strip(shard, whole, rows, k):
    at = pl.ds(k * STRIP, STRIP)
    return (
        shard.at[:, at],
        lambda q: whole.at[pl.ds(q * rows, rows), at],
        lambda o: whole.at[pl.ds(o * 2 * rows, 2 * rows), at],
    )


def forward_kernel(n_batch, *refs):
    (text_all, patch_all, gains, patch_own, key_ok, cross_ok, qkv_w,
     w_so, w_ckv, w_cq, w_co, w_gu, w_down) = refs[:13]
    (so_all, patch_w, ckv_all, cq_all, co_all, gu_all, down_all, act1_o, act2_o, act3_o, qkv_o, cqkv_o,
     ctx_o, cctx_o, lse_o, clse_o, pp_o, x1_o, x2_o, gate_o, up_o, h_o) = refs[13:35]
    (act, x, wq, wo, wp, pat, pp, qkv, ctx, lse, fs, ns, cf, yr, cn, wg, gate, gate_b, up, hid,
     z_send, z_recv, x_send, x_recv, own, mod_send, mod_recv, sum_send, sum_recv, loc, wide_send, wide_recv, wide_own) = refs[35:]
    p = Place(n_batch)
    local = Local(loc)
    rows, width = x.shape
    heads = wq.shape[2] // HD
    cq_r, pr = w_cq.shape[0], patch_own.shape[0]
    g = BatchGather(
        p,
        [
            (w_so, lambda q: so_all.at[pl.ds(q * cq_r, cq_r)]),
            (patch_own, lambda q: patch_w.at[pl.ds(q * pr, pr)]),
            (w_ckv.at[0], lambda q: ckv_all.at[0, pl.ds(q * cq_r, cq_r)]),
            (w_ckv.at[1], lambda q: ckv_all.at[1, pl.ds(q * cq_r, cq_r)]),
            (w_cq, lambda q: cq_all.at[pl.ds(q * cq_r, cq_r)]),
            (w_co, lambda q: co_all.at[pl.ds(q * cq_r, cq_r)]),
        ]
        + halves(w_gu.at[0], gu_all.at[0], cq_r)
        + halves(w_gu.at[1], gu_all.at[1], cq_r),
        (z_send, z_recv, x_send, x_recv, own),
        [strip(w_down, down_all, cq_r, k) for k in range(w_down.shape[1] // STRIP)],
        (wide_send, wide_recv, wide_own),
    )
    SO, PATCH, CK, CV, CQ, CO, GATE, GATE2, UP, UP2 = range(10)
    load_act = local.go(text_all, act)
    load_q = local.go(qkv_w, wq)
    load_pat = local.go(patch_all, pat)
    p.greet()
    g.start()
    g.wide_start()
    bufs = (fs, ns, cf, yr, cn)
    one = BranchSum(p, bufs, sum_send.at[0], sum_recv.at[0])
    two = BranchSum(p, bufs, sum_send.at[1], sum_recv.at[1])
    act_block = lambda j: act.at[j]
    col_w = wq.shape[2]
    pp_g = ModGather(p, lambda j: pp.at[:, :, pl.ds(pl.multiple_of(j * col_w, col_w), col_w)], mod_send.at[0], mod_recv.at[0])
    a2_g = ModGather(p, act_block, mod_send.at[1], mod_recv.at[1])
    a3_g = ModGather(p, act_block, mod_send.at[2], mod_recv.at[2])

    load_act.wait()
    x[...] = act[p.m].astype(F32)

    def norm_one(j):
        def body(r):
            act[j, r, :] = rms_of(act[j, r, :].astype(F32), gains[pl.ds(0, 1), :]).astype(BF)

        each_rows(rows, body)

    each(4, norm_one)
    save_act = local.go(act, act1_o)
    load_q.wait()

    def project(j):
        for w in range(3):
            qkv[w, j] = mm(act[j], wq[w]).astype(BF)

    each(4, project)
    save_qkv = local.go(qkv, qkv_o)
    g.pump(SO)
    attend_one = lambda j: attend(qkv.at[0], qkv.at[1], qkv.at[2], ctx, lse, j, causal_ok(key_ok[j, pl.ds(0, 1), :], rows), heads)
    each(4, attend_one)
    save_ctx = local.go(ctx, ctx_o)
    save_lse = local.go(lse, lse_o)
    g.arrived(SO)
    load_o = local.go(so_all, wo)
    save_act.wait()
    save_qkv.wait()
    load_o.wait()
    part = lambda j, k: mm_nt(ctx[j], wo[cols(k, 512), :])
    one.send(part)

    def add_own(k):
        at = cols(k, 512)
        x[:, at] += part(p.m, k)

    each(width // 512, add_own)
    g.arrived(PATCH)
    if pr != cq_r:
        wp[...] = jnp.zeros(wp.shape, BF)
    for c in [local.go(patch_w.at[pl.ds(q * pr, pr)], wp.at[pl.ds(q * cq_r, pr)]) for q in range(n_batch)]:
        c.wait()
    load_pat.wait()
    own_cols = pl.ds(pl.multiple_of(p.m * col_w, col_w), col_w)

    def project_patch(j):
        pp[j, :, own_cols] = mm(pat[j], wp[...]).astype(BF)

    each(4, project_patch)
    pp_g.start()
    one.receive()

    def finish_one(r):
        x[r, :] += one.others(r)
        act[p.m, r, :] = rms_of(x[r, :], gains[pl.ds(1, 1), :]).astype(BF)

    each_rows(rows, finish_one)
    a2_g.start()
    save_x = local.go(x, x1_o)
    one.sent()
    g.pump(CV)
    pp_g.forward()
    g.pump(CQ)
    a2_g.forward()
    g.arrived(CK)
    load_ck = local.go(ckv_all.at[0], wq.at[1])
    pp_g.finish()
    save_pp = local.go(pp, pp_o)
    load_ck.wait()

    def project_pp(w):
        def body(j):
            qkv[w, j] = mm(pp[j], wq[w]).astype(BF)

        return body

    each(4, project_pp(1))
    g.arrived(CV)
    load_cv = local.go(ckv_all.at[1], wq.at[2])
    load_cv.wait()
    each(4, project_pp(2))
    g.arrived(CQ)
    load_cq = local.go(cq_all, wq.at[0])
    a2_g.finish()
    save_act = local.go(act, act2_o)
    load_cq.wait()

    def project_cq(j):
        qkv[0, j] = mm(act[j], wq[0]).astype(BF)

    each(4, project_cq)
    save_ctx.wait()
    save_lse.wait()
    save_qkv = local.go(qkv, cqkv_o)

    def attend_two(j):
        ok = jnp.broadcast_to(cross_ok[j, pl.ds(0, 1), :], (rows, cross_ok.shape[2])) > 0.5
        attend(qkv.at[0], qkv.at[1], qkv.at[2], ctx, lse, j, ok, heads)

    each(4, attend_two)
    save_ctx = local.go(ctx, cctx_o)
    save_lse = local.go(lse, clse_o)
    g.arrived(CO)
    load_o = local.go(co_all, wo)
    save_act.wait()
    save_x.wait()
    load_o.wait()
    two.send(part)
    each(width // 512, add_own)
    g.pump(GATE2)
    two.receive()

    def finish_two(r):
        x[r, :] += two.others(r)
        act[p.m, r, :] = rms_of(x[r, :], gains[pl.ds(2, 1), :]).astype(BF)

    each_rows(rows, finish_two)
    a3_g.start()
    save_x = local.go(x, x2_o)
    two.sent()
    g.pump(UP)
    a3_g.forward()
    a3_g.finish()
    save_act = local.go(act, act3_o)

    half = wg.shape[1] // 2
    low, high = pl.ds(0, half), pl.ds(half, half)

    def gate_half(at):
        def body(j):
            value = mm(act[j], wg[:, at])
            gate[j, :, at] = value
            gate_b[j, :, at] = value.astype(BF)

        each(4, body)

    def up_half(at):
        def body(j):
            u = mm(act[j], wg[:, at])
            up[j, :, at] = u.astype(BF)
            hid[j, :, at] = (jax.nn.gelu(gate[j, :, at], approximate=True) * u).astype(BF)

        each(4, body)

    for t, k, at, compute in (
        (GATE, 0, low, gate_half), (GATE2, 0, high, gate_half), (UP, 1, low, up_half), (UP2, 1, high, up_half)
    ):
        g.arrived(t)
        load_g = local.go(gu_all.at[k, :, at], wg.at[:, at])
        load_g.wait()
        compute(at)
    save_gate = local.go(gate_b, gate_o)
    save_up = local.go(up, up_o)
    save_h = local.go(hid, h_o)
    g.sent()
    for c in (save_act, save_x, save_gate, save_up, save_h, save_ctx, save_lse, save_qkv, save_pp):
        c.wait()


def forward_call(n_batch, text_all, patch_all, gains, patch_own, key_ok, cross_ok, qkv_w,
                 w_so, w_ckv, w_cq, w_co, w_gu, w_down):
    n_out = n_batch // 2
    dma = pltpu.SemaphoreType.DMA
    items, rows, width = text_all.shape
    c, f = qkv_w.shape[2], w_gu.shape[2]
    patch_width = patch_all.shape[2]
    keys = patch_all.shape[1]
    sds = jax.ShapeDtypeStruct
    any_ = pl.BlockSpec(memory_space=pl.ANY)
    vmem = pl.BlockSpec(memory_space=pltpu.VMEM)
    big = (items, rows, width)
    return pl.pallas_call(
        functools.partial(forward_kernel, n_batch),
        out_shape=[
            sds((width, c), BF), sds((n_batch * patch_own.shape[0], c), BF), sds((2, width, c), BF), sds((width, c), BF),
            sds((width, c), BF), sds((2, width, f), BF), sds((width, f), BF),
            sds(big, BF), sds(big, BF), sds(big, BF),
            sds((3, items, rows, c), BF), sds((3, items, rows, c), BF),
            sds((items, rows, c), BF), sds((items, rows, c), BF),
            sds((items, rows, 128), F32), sds((items, rows, 128), F32),
            sds((items, keys, width), BF), sds((rows, width), F32), sds((rows, width), F32),
            sds((items, rows, f), BF), sds((items, rows, f), BF), sds((items, rows, f), BF),
        ],
        in_specs=[any_, any_, vmem, vmem, vmem, vmem, any_] + [vmem] * 6,
        out_specs=[any_] * 22,
        scratch_shapes=[
            pltpu.VMEM(big, BF), pltpu.VMEM((rows, width), F32), pltpu.VMEM((3, width, c), BF),
            pltpu.VMEM((width, c), BF), pltpu.VMEM((patch_width, c), BF), pltpu.VMEM((items, keys, patch_width), BF),
            pltpu.VMEM((items, keys, width), BF), pltpu.VMEM((3, items, rows, c), BF), pltpu.VMEM((items, rows, c), BF),
            pltpu.VMEM((items, rows, 128), F32),
        ]
        + [pltpu.VMEM((rows, width), BF)] * 5
        + [pltpu.VMEM((width, f), BF), pltpu.VMEM((items, rows, f), F32), pltpu.VMEM((items, rows, f), BF), pltpu.VMEM((items, rows, f), BF), pltpu.VMEM((items, rows, f), BF)]
        + BatchGather.semaphores(n_out, 10)
        + [dma((3, 3)), dma((3, 3)), dma((2, 3)), dma((2, 3)), dma((32 + n_batch,)),
           dma((f // STRIP, n_out + 1)), dma((f // STRIP, n_out)), dma((f // STRIP,))],
        compiler_params=pltpu.CompilerParams(collective_id=1, has_side_effects=True, vmem_limit_bytes=VMEM_LIMIT),
        cost_estimate=pl.CostEstimate(flops=35 * 10**9, bytes_accessed=600 * 10**6, transcendentals=0),
    )(text_all, patch_all, gains, patch_own, key_ok, cross_ok, qkv_w, w_so, w_ckv, w_cq, w_co, w_gu, w_down)


class Line:
    def z_copy(self, t, s):
        p = self.p
        return remote(self.block(t, (p.outer + s) % p.n_out), self.slot(t, s), self.z_send.at[t, s],
                      self.z_recv.at[t, s], batch=p.z_peer(s), mod=p.m)

    def to_relay(self, t):
        p = self.p
        return remote(self.block(t, p.opposite), self.slot(t, p.n_out), self.z_send.at[t, 0], self.z_recv.at[t, 0],
                      batch=p.relay * 2 + p.inner, mod=p.m)

    def to_end(self, t):
        p = self.p
        return remote(self.block(t, p.end), self.slot(t, p.outward), self.z_send.at[t, 0],
                      self.z_recv.at[t, p.outward], batch=p.end * 2 + p.inner, mod=p.m)

    def z_start(self, t):
        p = self.p
        if not self.line:
            for s in p.shifts:
                self.z_copy(t, s).start()
            return
        self.z_copy(t, 2).start()
        self.z_copy(t, p.inward).start()

        @pl.when(p.is_end)
        def _():
            self.to_relay(t).start()

    def z_relay(self, t):
        p = self.p
        if not self.line:
            return

        @pl.when(p.is_mid)
        def _():
            self.to_relay(t).wait_recv()
            a, b = self.views(t)
            self.fetch((self.block(t, p.end), a), (self.slot(t, p.n_out), b))
            self.add(a, b)
            self.fetch((a, self.block(t, p.end)))
            self.to_end(t).start()

    def fetch(self, *pairs):
        copies = [pltpu.make_async_copy(a, b, self.loc.at[k]) for k, (a, b) in enumerate(pairs)]
        for copy in copies:
            copy.start()
        for copy in copies:
            copy.wait()

    def add(self, a, *others):
        lead, rows, width = a.shape
        step = 16
        while rows % (2 * step) == 0 and step * width < 16384:
            step *= 2

        def body(o):
            def one(r):
                total = a[o, r, :].astype(F32)
                for b in others:
                    total = total + b[o, r, :].astype(F32)
                a[o, r, :] = total.astype(BF)

            each_rows(rows, one, step)

        each(lead, body)

    def z_arrived(self, t):
        p = self.p
        if not self.line:
            for s in p.shifts:
                self.z_copy(t, s).wait_recv()
            return
        self.z_copy(t, 2).wait_recv()
        self.z_copy(t, self.first_slot()).wait_recv()

        @pl.when(p.is_mid)
        def _():
            self.z_copy(t, 3).wait_recv()

    def first_slot(self):
        return 3 - 2 * ((self.p.outer + 2) // 3)

    def z_sent(self, t):
        p = self.p
        if not self.line:
            for s in p.shifts:
                self.z_copy(t, s).wait_send()
            return
        self.z_copy(t, 2).wait_send()
        self.z_copy(t, p.inward).wait_send()
        self.to_relay(t).wait_send()


class GradSum(Line):
    def __init__(self, place, pieces, mine, got, sems, loc):
        self.p = place
        self.pieces = pieces
        self.mine, self.got = mine, got
        self.x_send, self.x_recv, self.z_send, self.z_recv = sems
        self.loc = loc
        self.line = place.line
        self.ready = self.started = self.done = 0
        self.window = 2

    @staticmethod
    def semaphores(n_out, count):
        dma = pltpu.SemaphoreType.DMA
        return [dma((count,)), dma((count,)), dma((count, n_out)), dma((count, n_out))]

    def block(self, t, o):
        return self.pieces[t][1].at[pl.ds(o, 1)]

    def slot(self, t, s):
        return self.pieces[t][2].at[pl.ds(s, 1)]

    def views(self, t):
        _, rows, width = self.pieces[t][1].shape
        return [v.at[pl.ds(0, 1), pl.ds(0, rows), pl.ds(0, width)] for v in (self.mine, self.got)]

    def x_copy(self, t):
        whole, from_x, _ = self.pieces[t]
        return remote(whole.at[:, 1 - self.p.inner], from_x, self.x_send.at[t], self.x_recv.at[t],
                      batch=self.p.x_peer, mod=self.p.m)

    def kick(self):
        while self.started < self.ready and self.started - self.done < self.window:
            self.x_copy(self.started).start()
            self.started += 1

    def advance(self):
        self.ready += 1
        self.kick()

    def pump(self, count=1):
        for _ in range(min(count, self.ready - self.done)):
            t = self.done
            whole, from_x, from_z = self.pieces[t]
            n_out, rows, width = from_x.shape
            self.x_copy(t).wait_recv()
            self.done += 1
            self.kick()
            mine = self.mine.at[:, pl.ds(0, rows), pl.ds(0, width)]
            got = self.got.at[:, pl.ds(0, rows), pl.ds(0, width)]
            self.fetch((whole.at[:, self.p.inner], mine), (from_x, got))
            self.add(mine, got)
            self.fetch((mine, from_x), (mine.at[self.p.outer], from_z.at[0]))
            self.z_start(t)
            if t:
                self.z_relay(t - 1)

    def finish(self):
        last = len(self.pieces) - 1
        self.pump(len(self.pieces))
        self.z_relay(last)
        for t in range(len(self.pieces)):
            self.x_copy(t).wait_send()
            self.z_arrived(t)
            self.z_sent(t)


def attend_back(q_ref, k_ref, v_ref, do_ref, lse_ref, dq_ref, dk_ref, dv_ref, j, allowed, heads):
    scale = HD ** (-0.5)
    for h in range(heads):
        at = pl.ds(h * HD, HD)
        q, k, v, do = q_ref[j, :, at], k_ref[j, :, at], v_ref[j, :, at], do_ref[j, :, at]
        s = jnp.where(allowed, mm_nt(q, k) * scale, -1e30)
        probs = jnp.exp(s - lse_ref[j, :, pl.ds(h, 1)])
        dp = mm_nt(do, v)
        ds = (probs * (dp - jnp.sum(probs * dp, axis=-1, keepdims=True))).astype(BF)
        dv_ref[j, :, at] = mm_tn(probs.astype(BF), do).astype(BF)
        dq_ref[j, :, at] = (mm(ds, k) * scale).astype(BF)
        dk_ref[j, :, at] = (mm_tn(ds, q) * scale).astype(BF)


def gelu_parts(g):
    c = 0.7978845608028654
    t = jnp.tanh(c * (g + 0.044715 * g * g * g))
    half = 0.5 * (1.0 + t)
    return g * half, half + 0.5 * g * (1.0 - t * t) * c * (1.0 + 3 * 0.044715 * g * g)


def backward_kernel(n_batch, *refs):
    (dy_all, text, pat_all, gains, key_ok, cross_ok, qkv_w, so_all, ckv_all, cq_all, co_all, gu_all, down_all,
     act1, act2, act3, qkv_i, cqkv_i, ctx_i, cctx_i, lse_i, clse_i, pp_i, x1_i, x2_i, gate_i, up_i, h_i) = refs[:28]
    (result, d_text, gain_out, whole_f, from_x_f, from_z_f, whole_c, from_x_c, from_z_c,
     whole_p, from_x_p, from_z_p) = refs[28:40]
    (dy, act_a, act_b, gate, up, hid, w0, w1, qkv, dqkv, ctx, dctx, dpp, lse, g, da, v, fs, ns, cf, yr, cn,
     cf2, yr2, cn2, st, mine, got, dg, dgm, dgx, dgz,
     gx_send, gx_recv, gz_send, gz_recv, mod_send, mod_recv, sum_send, sum_recv, gain_send, gain_recv,
     gx, loc, loc2) = refs[40:]
    p = Place(n_batch)
    local = Local(loc)
    items, rows, width = dy.shape
    c, f = qkv_w.shape[2], gu_all.shape[2]
    half = f // 2
    n_out, blk = p.n_out, width // n_batch
    heads = c // HD
    pieces = [
        (whole_f.at[k], from_x_f.at[k], from_z_f.at[k // 2, :, :, pl.ds(k % 2 * half, half)]) for k in range(6)
    ]
    pieces += [(whole_c.at[k], from_x_c.at[k], from_z_c.at[k]) for k in range(8)]
    pieces.append((whole_p, from_x_p, from_z_p))
    gs = GradSum(p, pieces, mine, got, (gx_send, gx_recv, gz_send, gz_recv), loc2)
    left = pl.ds(0, c)
    right = pl.ds(c, c)

    load_dy = local.go(dy_all, dy)
    load_h = local.go(h_i, hid)
    p.greet()
    set_a = (fs, ns, cf, yr, cn)
    set_b = (fs, ns, cf2, yr2, cn2)
    sums = [
        BranchSum(p, bufs, sum_send.at[k], sum_recv.at[k])
        for k, bufs in enumerate((set_b, set_a, set_a, set_b, set_a))
    ]
    gathers = [ModGather(p, lambda j: dy.at[j], mod_send.at[k], mod_recv.at[k]) for k in range(2)]
    dg[...] = jnp.zeros(dg.shape, F32)

    def piece(acts, grads, first, count):
        t = gs.ready
        whole = pieces[t][0]
        used = whole.shape[2]
        chunk = max(256, 2 * blk)
        per = chunk // (2 * blk)

        def body(n):
            a = acts[:, :, cols(n, chunk)].reshape(items * rows, chunk)
            b = grads[:, :, pl.ds(first, count)].reshape(items * rows, count)
            st[pl.ds(n * per, per), :, :, pl.ds(0, count)] = mm_tn(a, b).astype(BF).reshape(per, 2, blk, count)

        each(width // chunk, body)
        copy = pltpu.make_async_copy(st.at[:, :, pl.ds(0, used), pl.ds(0, count)], whole, loc2.at[2])
        copy.start()
        copy.wait()
        gs.advance()

    def norm_back(k, total, v_rows):
        def body(r):
            grad = da[r, :] + total.others(r)
            val = v_rows(r)
            factor = lax.rsqrt(jnp.mean(val * val, axis=-1, keepdims=True) + 1e-06)
            dg[pl.ds(k, 1), :] += jnp.sum(grad * val * factor, axis=0, keepdims=True)
            scaled = gains[pl.ds(k, 1), :] * grad
            back = factor * scaled - val * (factor * factor * factor * jnp.mean(scaled * val, axis=-1, keepdims=True))
            g[r, :] += back
            if k:
                dy[p.m, r, :] = g[r, :].astype(BF)

        each_rows(rows, body)

    load_dy.wait()
    load_h.wait()
    load_w0 = local.go(down_all, w0)
    load_v = local.go(x2_i, v)
    load_gate = local.go(gate_i, gate)
    load_up = local.go(up_i, up)
    load_w1 = local.go(gu_all.at[0], w1)
    load_a = local.go(act3, act_a)
    load_b = local.go(act2, act_b)
    piece(dy, hid, 0, half)
    g[...] = dy[p.m].astype(F32)
    piece(dy, hid, half, half)
    load_w0.wait()
    load_gate.wait()
    load_up.wait()

    def mix_back(j):
        dh = mm(dy[j], w0[...])
        value, slope = gelu_parts(gate[j].astype(F32))
        gate[j] = (dh * up[j].astype(F32) * slope).astype(BF)
        up[j] = (dh * value).astype(BF)

    each(items, mix_back)
    load_w0 = local.go(gu_all.at[1], w0)
    load_w1.wait()
    load_w0.wait()
    act_part = lambda j, k: mm_nt(gate[j], w1[cols(k, 512), :]) + mm_nt(up[j], w0[cols(k, 512), :])
    sums[1].send(act_part)
    gs.pump()

    def own_part(part):
        def body(k):
            da[:, cols(k, 512)] = part(p.m, k)

        each(width // 512, body)

    own_part(act_part)
    load_w0 = [local.go(co_all, w0.at[:, left]), local.go(cq_all, w0.at[:, right])]
    load_w1 = [local.go(ckv_all.at[0], w1.at[:, left]), local.go(ckv_all.at[1], w1.at[:, right])]
    load_s = [local.go(cqkv_i, qkv), local.go(cctx_i, ctx), local.go(clse_i, lse)]
    load_a.wait()
    piece(act_a, gate, 0, half)
    piece(act_a, gate, half, half)
    piece(act_a, up, 0, half)
    gs.pump()
    load_v.wait()
    sums[1].receive()
    norm_back(2, sums[1], lambda r: v[r, :])
    gathers[0].start()
    sums[1].sent()
    load_v = local.go(x1_i, v)
    piece(act_a, up, half, half)
    load_a = local.go(pp_i, act_a)
    gs.pump()
    gathers[0].forward()
    gathers[0].finish()

    for copy in load_w0 + load_w1 + load_s:
        copy.wait()

    def ctx_back(j):
        dctx[j] = mm(dy[j], w0[:, left]).astype(BF)

    each(items, ctx_back)
    piece(dy, ctx, 0, c)

    def cross_back(j):
        ok = jnp.broadcast_to(cross_ok[j, pl.ds(0, 1), :], (rows, cross_ok.shape[2])) > 0.5
        attend_back(qkv.at[0], qkv.at[1], qkv.at[2], dctx, lse, dqkv.at[0], dqkv.at[1], dqkv.at[2], j, ok, heads)

    each(items, cross_back)
    query_part = lambda j, k: mm_nt(dqkv[0, j], w0[cols(k, 512), right])
    sums[2].send(query_part)
    gs.pump()
    own_part(query_part)
    load_w0 = [local.go(so_all, w0.at[:, left]), local.go(qkv_w.at[0], w0.at[:, right])]
    load_s = [local.go(qkv_i, qkv), local.go(ctx_i, ctx), local.go(lse_i, lse)]
    load_b.wait()
    piece(act_b, dqkv.at[0], 0, c)
    load_b = local.go(act1, act_b)
    load_a.wait()
    piece(act_a, dqkv.at[1], 0, c)
    piece(act_a, dqkv.at[2], 0, c)
    load_a = local.go(pat_all, act_a)
    load_v.wait()
    sums[2].receive()
    norm_back(1, sums[2], lambda r: v[r, :])
    gathers[1].start()
    sums[2].sent()
    load_v = local.go(x2_i, v)
    gs.pump()
    proj_part = lambda j, k: mm_nt(dqkv[1, k], w1[cols(j, c), left]) + mm_nt(dqkv[2, k], w1[cols(j, c), right])
    sums[3].send_core(proj_part)

    def proj_own(k):
        dpp[k] = proj_part(p.m, k).astype(BF)

    each(items, proj_own)
    gathers[1].forward()
    gathers[1].finish()
    sums[3].send_far(proj_part)
    load_w1 = [local.go(qkv_w.at[1], w1.at[:, left]), local.go(qkv_w.at[2], w1.at[:, right])]

    for copy in load_w0 + load_s:
        copy.wait()
    each(items, ctx_back)
    piece(dy, ctx, 0, c)
    gs.pump()

    def self_back(j):
        ok = causal_ok(key_ok[j, pl.ds(0, 1), :], rows)
        attend_back(qkv.at[0], qkv.at[1], qkv.at[2], dctx, lse, dqkv.at[0], dqkv.at[1], dqkv.at[2], j, ok, heads)

    each(items, self_back)
    load_b.wait()
    for k in range(3):
        piece(act_b, dqkv.at[k], 0, c)
    gs.pump()
    sums[3].receive()

    def proj_done(k):
        every = pl.ds(0, rows)
        dpp[k] = (dpp[k].astype(F32) + sums[3].others(every, cols(k, c))).astype(BF)

    each(items, proj_done)
    sums[3].sent()
    for copy in load_w1:
        copy.wait()
    self_part = lambda j, k: (
        mm_nt(dqkv[0, j], w0[cols(k, 512), right])
        + mm_nt(dqkv[1, j], w1[cols(k, 512), left])
        + mm_nt(dqkv[2, j], w1[cols(k, 512), right])
    )
    sums[4].send(self_part)
    own_part(self_part)
    load_w0 = local.go(down_all, w0)
    gs.pump()
    load_a.wait()
    piece(act_a, dpp, 0, c)
    gs.pump()
    sums[4].receive()
    norm_back(0, sums[4], lambda r: text[r, :].astype(F32))
    save_text = local.go(g, d_text)
    sums[4].sent()

    mod_g = [
        remote(dg, dgm.at[k], gain_send.at[k], gain_recv.at[k], batch=p.b, mod=j)
        for k, j in enumerate((p.core, p.far, p.farcore))
    ]
    for copy in mod_g:
        copy.start()
    load_w0.wait()
    out_part = lambda j, k: mm_nt(hid[j], w0[cols(k, 512), :])
    sums[0].send(out_part)
    gs.pump()
    load_v.wait()

    def result_own(k):
        at = cols(k, 512)
        da[:, at] = v[:, at] + out_part(p.m, k)

    each(width // 512, result_own)
    for copy in mod_g:
        copy.wait()
    dg[...] += dgm[0] + dgm[1] + dgm[2]
    across = remote(dg, dgx, gx.at[0], gx.at[1], batch=p.x_peer, mod=p.m)
    across.start()
    gs.pump()
    sums[0].receive()

    def result_done(r):
        da[r, :] += sums[0].others(r)

    each_rows(rows, result_done)
    save_result = local.go(da, result)
    sums[0].sent()
    across.wait()
    dg[...] += dgx[...]
    along = [
        remote(dg, dgz.at[s], gain_send.at[3 + s], gain_recv.at[3 + s], batch=p.z_peer(s), mod=p.m)
        for s in p.shifts
    ]
    for copy in along:
        copy.start()
    gs.pump()
    for copy in along:
        copy.wait()
    total = dg[...]
    for s in p.shifts:
        total = total + dgz[s]
    gain_out[...] = total
    gs.finish()
    save_result.wait()
    save_text.wait()


def backward_call(n_batch, inputs, patch_rows):
    n_out = n_batch // 2
    dma = pltpu.SemaphoreType.DMA
    sds = jax.ShapeDtypeStruct
    items, rows, width = inputs[0].shape
    c, f = inputs[6].shape[2], inputs[11].shape[2]
    blk = width // n_batch
    any_ = pl.BlockSpec(memory_space=pl.ANY)
    vmem = pl.BlockSpec(memory_space=pltpu.VMEM)
    big = (items, rows, width)
    heads_shape = (items, rows, c)
    V = lambda shape, dtype=BF: pltpu.VMEM(shape, dtype)

    def bufs(count, r, w):
        lead = (count,) if count else ()
        return [sds(lead + (n_out, 2, r, w), BF), sds(lead + (n_out, r, w), BF), sds(lead + (n_out + 1, r, w), BF)]

    return pl.pallas_call(
        functools.partial(backward_kernel, n_batch),
        out_shape=[sds((rows, width), F32), sds((rows, width), F32), sds((8, width), F32)]
        + bufs(6, blk, f // 2)[:2] + [sds((3, n_out + 1, blk, f), BF)] + bufs(8, blk, c) + bufs(0, patch_rows, c),
        in_specs=[any_, vmem, any_, vmem, vmem, vmem] + [any_] * 22,
        out_specs=[any_, any_, vmem] + [any_] * 9,
        scratch_shapes=[V(big)] * 3
        + [V((items, rows, f))] * 3
        + [V((width, f))] * 2
        + [V((3,) + heads_shape)] * 2
        + [V(heads_shape)] * 3
        + [V((items, rows, 128), F32)]
        + [V((rows, width), F32)] * 3
        + [V((rows, width))] * 8
        + [V((n_out, 2, blk, f // 2)), V((n_out, blk, f // 2)), V((n_out, blk, f // 2))]
        + [V((8, width), F32), V((3, 8, width), F32), V((8, width), F32), V((n_out, 8, width), F32)]
        + GradSum.semaphores(n_out, 15)
        + [dma((2, 3)), dma((2, 3)), dma((5, 3)), dma((5, 3)), dma((3 + n_out,)), dma((3 + n_out,)), dma((2,)),
           dma((48,)), dma((4,))],
        compiler_params=pltpu.CompilerParams(collective_id=2, has_side_effects=True, vmem_limit_bytes=VMEM_LIMIT),
        cost_estimate=pl.CostEstimate(flops=75 * 10**9, bytes_accessed=800 * 10**6, transcendentals=0),
    )(*inputs)


def local(n_batch, n_mod, text, patches, text_lengths, patch_mask, cotangent, gains,
          w_qkv, w_so, w_cq, w_ckv, w_co, w_patch, w_gu, w_down):
    own_items, text_rows, width = text.shape
    mod = lax.axis_index("mod")
    nb = n_batch
    blk = width // nb
    positions = jnp.arange(text_rows)

    gw = blk // n_mod
    gain_tile = lax.dynamic_update_slice(jnp.zeros((16, blk), BF), gains, (0, mod * gw))
    col_w = width // n_mod
    pr = w_patch.shape[0]
    pr_pad = -(-pr // 16) * 16
    patch_tile = jnp.pad(w_patch, ((0, pr_pad - pr), (0, 0))).reshape(pr_pad, n_mod, col_w)
    patch_tile = jnp.transpose(patch_tile, (1, 0, 2))
    block, block_pad = n_mod * pr, -(-n_mod * pr // 16) * 16
    patch_in = jnp.pad(patches[0].reshape(-1, nb, block), ((0, 0), (0, 0), (0, blk - block))).reshape(-1, width)
    own_length = lax.dynamic_slice_in_dim(text_lengths, mod * own_items, own_items)
    valid = jnp.broadcast_to((positions[:, None] < own_length).astype(F32), (text_rows, 128))
    text_all, patch_all, gain_raw, patch_rows, self_qkv, dy_all, so_t, co_t, down_t = first_call(
        n_batch, text[0], patch_in, gain_tile, patch_tile, w_qkv, w_so, w_co, w_down, cotangent[0], valid
    )
    gain_all = jnp.transpose(gain_raw[:, :8], (1, 0, 2)).reshape(8, width).astype(F32)
    patch_own = patch_rows[:, :pr].reshape(block, col_w)
    patch_own = jnp.pad(patch_own, ((0, block_pad - block), (0, 0)))
    row_ok = (positions[None, :] < text_lengths[:, None]).astype(F32)
    key_ok = jnp.broadcast_to(row_ok[:, None, :], (n_mod, 8, text_rows))
    cross_ok = jnp.broadcast_to((patch_mask > 0).astype(F32)[:, None, :], (n_mod, 8, patch_mask.shape[1]))
    (so_all, _, ckv_all, cq_all, co_all, gu_all, down_all, act1, act2, act3, qkv, cqkv,
     ctx, cctx, lse, clse, pp, x1, x2, gate, up, hid) = forward_call(
        n_batch, text_all, patch_all, gain_all, patch_own, key_ok, cross_ok, self_qkv,
        so_t, w_ckv, w_cq, co_t, w_gu, down_t)
    outs = backward_call(
        n_batch,
        (dy_all, text[0], patch_all, gain_all, key_ok, cross_ok, self_qkv, so_all, ckv_all, cq_all, co_all, gu_all,
         down_all, act1, act2, act3, qkv, cqkv, ctx, cctx, lse, clse, pp, x1, x2, gate, up, hid),
        block_pad,
    )
    result, d_text, gain_sum = outs[:3]
    sum_f, sum_c, sum_p = outs[5], outs[8], outs[11]
    at = lax.axis_index("batch") * blk + mod * gw
    d_gains = lax.dynamic_slice(gain_sum, (0, at), (3, gw))

    n_out = nb // 2
    outer = lax.axis_index("batch") // 2
    slots = jnp.arange(n_out)
    missing = (((outer == 0) & (slots == 1)) | ((outer == 3) & (slots == 3))) & (n_out == 4)

    def total(parts, axis=0):
        parts = lax.slice_in_dim(parts, 0, n_out, axis=axis)
        gone = missing.reshape((1,) * axis + (n_out,) + (1,) * (parts.ndim - axis - 1))
        return jnp.sum(jnp.where(gone, 0.0, parts.astype(F32)), axis=axis)

    grad_patch = total(sum_p)[:block].reshape(n_mod, pr, col_w)
    grad_patch = lax.all_to_all(grad_patch, "mod", 0, 0, tiled=True)
    grad_patch = jnp.transpose(grad_patch, (1, 0, 2)).reshape(pr, width)
    return (
        result[None],
        d_text[None],
        d_gains,
        total(sum_c[5:8], 1),
        total(sum_c[4]).T,
        total(sum_c[1]),
        total(sum_c[2:4], 1),
        total(sum_c[0]).T,
        grad_patch,
        total(sum_f[1:], 1),
        total(sum_f[0]).T,
    )


def solution(mesh):
    placed = (
        P(("batch", "mod"), None, None),
        P(("batch", "mod"), None, None),
        P("batch"),
        P("batch", None),
        P(("batch", "mod"), None, None),
        P(None, ("batch", "mod")),
        P(None, "batch", "mod"),
        P("mod", "batch"),
        P("batch", "mod"),
        P(None, "batch", "mod"),
        P("mod", "batch"),
        P(("batch", "mod"), None),
        P(None, "batch", "mod"),
        P("mod", "batch"),
    )

    def run(*args):
        return local(mesh.shape["batch"], mesh.shape["mod"], *args)

    return jax.shard_map(
        run,
        mesh=mesh,
        in_specs=placed,
        out_specs=(
            P(("batch", "mod"), None, None),
            P(("batch", "mod"), None, None),
            P(None, ("batch", "mod")),
            P(None, "batch", "mod"),
            P("mod", "batch"),
            P("batch", "mod"),
            P(None, "batch", "mod"),
            P("mod", "batch"),
            P(("batch", "mod"), None),
            P(None, "batch", "mod"),
            P("mod", "batch"),
        ),
        check_vma=False,
    )
```
